32 devices in a mesh: seq: 2 (over x), ctx: 8 (over z, y), wsh: 2 (over core).
Axes of the slice: x: 2, y: 2, z: 4, core: 2. Of those that a mesh axis runs over, the one named last changes fastest.
Arguments:
- tokens: bfloat16 [4, 1024, 768], P(('seq', 'wsh'), 'ctx'), may hold values from -6 to 6
- w_qkv: bfloat16 [768, 2304], P('wsh'), may hold values from -0.21875 to 0.21875
- w_out: bfloat16 [768, 768], P('wsh'), may hold values from -4 to 4
- w_in: bfloat16 [768, 2304], P('wsh'), may hold values from -0.21875 to 0.21875
- w_mlp: bfloat16 [1152, 768], P('wsh'), may hold values from -0.1875 to 0.1875
- gain_attn: bfloat16 [768], P('wsh'), may hold values from 0.099609375 to 1.8984375
- gain_mlp: bfloat16 [768], P('wsh'), may hold values from 0.099609375 to 1.8984375
- cotangent: bfloat16 [4, 1024, 768], P(('seq', 'wsh'), 'ctx'), may hold values from -6 to 6
Outputs:
- layer_out: bfloat16 [4, 1024, 768], P(('seq', 'wsh'), 'ctx')
- tokens_grad: bfloat16 [4, 1024, 768], P(('seq', 'wsh'), 'ctx')
- w_qkv_grad: float32 [768, 2304], P('wsh')
- w_out_grad: float32 [768, 768], P('wsh')
- w_in_grad: float32 [768, 2304], P('wsh')
- w_mlp_grad: float32 [1152, 768], P('wsh')
- gain_attn_grad: float32 [768], P('wsh')
- gain_mlp_grad: float32 [768], P('wsh')
The draws below stay inside these ranges and needn't reach their ends.
All inputs are finite; a program needn't handle non-finite values.
Results may differ from the reference program's by a relative error of at most 0.018.
Values may be sent and summed in bfloat16 or wider, within the bound.
No kernel may reach another device: no remote copies, remote signals or barrier semaphores. Data moves between devices by JAX's collectives and lax.ppermute only.
A program may use at most 128 MiB of HBM per device.

```python
import math
import jax
import jax.numpy as jnp
from jax import lax

D = 768
HEADS = 12
FF = 1152
LENGTH = 1024
SEQS = 4


def strengthened(values, own_key, source, target, blocks, factor):
    owner, partner = [(jnp.arange(values.shape[position]) // (values.shape[position] // blocks)).reshape([-1 if axis == position else 1 for axis in range(values.ndim)]) for position in (source, target)]
    chosen = jax.random.permutation(own_key, blocks)[partner]
    strong = (owner == chosen) | (owner == (partner + blocks // 2) % blocks)
    return jnp.where(strong, factor * values, values)


def level_of(rng, extent, split, least, high):
    def one(dim, parts):
        heights = jax.random.uniform(jax.random.fold_in(jax.random.fold_in(rng, 6), dim), (parts,), jnp.float32, least / len(split), high / len(split))
        return jnp.repeat(jnp.exp(heights), extent[dim] // parts).reshape((-1,) + (1,) * (len(extent) - dim - 1))

    gain = one(*split[0])
    for cut in split[1:]:
        gain = gain * one(*cut)
    return gain


def normal_values(own_key, dims, deviation, bound, split=(), held_as=jnp.bfloat16):
    values = deviation * jax.random.normal(own_key, dims, jnp.float32)
    if split:
        values = values * level_of(own_key, dims, split, -0.22, 0.18)
    return jnp.clip(values, -bound, bound).astype(held_as)


def bell_draw_with(rng, extent, spread, reach, split, heavy, kind=jnp.bfloat16):
    entries = spread * jax.random.normal(rng, extent, jnp.float32)
    if split:
        entries = entries * level_of(rng, extent, split, -0.22, 0.18)
    return jnp.clip(strengthened(entries, jax.random.fold_in(rng, 3), *heavy), -reach, reach).astype(kind)


def setup_inputs(seed: int = 0) -> dict:
    streams_of = jax.random.split(jax.random.key(seed), 9)
    return {
        "tokens": normal_values(streams_of[0], (SEQS, LENGTH, D), 1.0, 6.0, ((0, 4), (1, 8))),
        "w_qkv": normal_values(streams_of[1], (D, 3 * D), D ** -0.5, 0.21875, ((0, 2),)),
        "w_out": normal_values(streams_of[2], (D, D), (max(1, 3 * D // LENGTH)) ** -0.5, 4.0, ((0, 2),)),
        "w_in": normal_values(streams_of[3], (D, 2 * FF), D ** -0.5, 0.21875, ((0, 2),)),
        "w_mlp": normal_values(streams_of[4], (FF, D), FF ** -0.5, 0.1875, ((0, 2),)),
        "gain_attn": jnp.clip(1.0 + 0.18 * jax.random.normal(streams_of[5], (D,), jnp.float32), 0.099609375, 1.8984375).astype(jnp.bfloat16),
        "gain_mlp": jnp.clip(1.0 + 0.18 * jax.random.normal(streams_of[6], (D,), jnp.float32), 0.099609375, 1.8984375).astype(jnp.bfloat16),
        "cotangent": bell_draw_with(streams_of[7], (SEQS, LENGTH, D), 1.0, 6.0, ((0, 4), (1, 8)), (1, 2, 8, 2.0)),
    }


@jax.custom_vjp
def low(v):
    return lax.optimization_barrier(v.astype(jnp.bfloat16)).astype(jnp.float32)

@jax.custom_vjp
def low_back(v):
    return v

def low_keep(v):
    return (low(v), None)

def low_pass(kept, grad):
    return (grad,)

def back_keep(v):
    return (v, None)

def back_low(kept, grad):
    return (low(grad),)
low.defvjp(low_keep, low_pass)
low_back.defvjp(back_keep, back_low)
EPSILON = 1e-05
THETA = 160000.0
HIGH = lax.Precision.HIGHEST

def matmul_high(left_rows, right_rows):
    return jnp.dot(left_rows, right_rows, precision=HIGH, preferred_element_type=jnp.float32)

def normalize(inputs):
    average = lax.optimization_barrier(jnp.mean(inputs, axis=-1, keepdims=True))
    centred = inputs - average
    variance = lax.optimization_barrier(jnp.mean(centred * centred, axis=-1, keepdims=True))
    return centred * lax.rsqrt(variance + EPSILON)

def rotary_tables(positions, head_dim):
    half_dim = head_dim // 2
    inverse = jnp.power(jnp.float32(THETA), -(jnp.arange(half_dim, dtype=jnp.float32) * (2.0 / head_dim)))
    angles = positions[:, None] * inverse[None, :]
    return (jnp.cos(angles), jnp.sin(angles))

def rotate(vectors, cos_table, sin_table):
    half_dim = vectors.shape[-1] // 2
    first_half = vectors[..., :half_dim]
    second_half = vectors[..., half_dim:]
    cos_rows = cos_table[:, None, :]
    sin_rows = sin_table[:, None, :]
    return jnp.concatenate([first_half * cos_rows - second_half * sin_rows, second_half * cos_rows + first_half * sin_rows], axis=-1)

def attend(queries, key_rows, values):
    row_count, head_count, head_dim = queries.shape
    block_rows = math.gcd(row_count, 512)
    score_scale = head_dim ** (-0.5)

    def one_block(query_block):
        scores = low_back(jnp.einsum('qhd,khd->hqk', query_block, key_rows, precision=HIGH) * score_scale)
        row_peak = lax.optimization_barrier(jnp.max(scores, axis=-1, keepdims=True))
        weights = jnp.exp(scores - row_peak)
        row_total = lax.optimization_barrier(jnp.sum(weights, axis=-1))
        mixed_rows = jnp.einsum('hqk,khd->qhd', low(weights), values, precision=HIGH)
        return mixed_rows / jnp.transpose(row_total)[:, :, None]
    blocks = lax.map(jax.checkpoint(one_block), queries.reshape(row_count // block_rows, block_rows, head_count, head_dim))
    return blocks.reshape(row_count, head_count * head_dim)

def block_forward(inputs, w_qkv, w_out, w_in, w_mlp, gain_attn, gain_mlp):
    row_count, model_width = inputs.shape
    head_dim = model_width // HEADS
    normed = low(normalize(inputs) * gain_attn)
    projected = low_back(matmul_high(normed, w_qkv))
    cos_table, sin_table = rotary_tables(jnp.arange(row_count, dtype=jnp.float32), head_dim)
    queries = low(rotate(projected[:, :model_width].reshape(row_count, HEADS, head_dim), cos_table, sin_table))
    key_rows = low(rotate(projected[:, model_width:2 * model_width].reshape(row_count, HEADS, head_dim), cos_table, sin_table))
    values = low(projected[:, 2 * model_width:].reshape(row_count, HEADS, head_dim))
    attended = low(low_back(attend(queries, key_rows, values)))
    middle = inputs + low_back(matmul_high(attended, w_out))
    second = low(normalize(middle) * gain_mlp)
    gate_up = low_back(matmul_high(second, w_in))
    hidden = low(low_back(jax.nn.gelu(gate_up[:, :FF], approximate=False) * gate_up[:, FF:]))
    return middle + matmul_high(hidden, w_mlp)

def reference(tokens, w_qkv, w_out, w_in, w_mlp, gain_attn, gain_mlp, cotangent):

    def forward(inputs, qkv_f, out_f, in_f, mlp_f, attn_f, norm_f):

        def one_seq(sequence):
            return block_forward(sequence, qkv_f, out_f, in_f, mlp_f, attn_f, norm_f)
        return lax.map(jax.checkpoint(one_seq), inputs)
    params = (tokens.astype(jnp.float32), w_qkv.astype(jnp.float32), w_out.astype(jnp.float32), w_in.astype(jnp.float32), w_mlp.astype(jnp.float32), gain_attn.astype(jnp.float32), gain_mlp.astype(jnp.float32))
    outputs, pullback = jax.vjp(forward, params[0], params[1], params[2], params[3], params[4], params[5], params[6])
    gradients = pullback(cotangent.astype(jnp.float32))
    return (outputs.astype(jnp.bfloat16), gradients[0].astype(jnp.bfloat16), gradients[1], gradients[2], gradients[3], gradients[4], gradients[5], gradients[6])
```

```python
from functools import partial

import jax
import jax.numpy as jnp
from jax import lax
from jax.experimental import pallas as pl
from jax.experimental.pallas import tpu as pltpu
from jax.sharding import PartitionSpec as P

HEADS = 12
FF = 1152
EPSILON = 1e-05
THETA = 160000.0
LANES = 128
PIECE = 2 * HEADS
NORMED_AT = 640
ATTENDED_AT = 1024
HALVES_WIDTH = 1408
MIB = 1 << 20
BF16 = jnp.bfloat16
F32 = jnp.float32


def bits_of(axis):
    return [(axis, k) for k in range((lax.axis_size(axis) - 1).bit_length())]


def my_bit(axis, k):
    return (lax.axis_index(axis) >> k) & 1


def flip(block, first, second):
    n_seq, n_ctx = lax.axis_size("seq"), lax.axis_size("ctx")
    route = []
    for s in range(n_seq):
        for t in range(n_ctx):
            for core, (axis, k) in enumerate((first, second)):
                s2, t2 = (s ^ (1 << k), t) if axis == "seq" else (s, t ^ (1 << k))
                route.append(((s * n_ctx + t) * 2 + core, (s2 * n_ctx + t2) * 2 + core))
    return lax.ppermute(block, ("seq", "ctx", "wsh"), route)


def swap_cores(block):
    return lax.ppermute(block, "wsh", [(0, 1), (1, 0)])


def gather_orders():
    bits = bits_of("ctx")
    return bits[::-1], bits[:1] + bits[:0:-1]


def gather_context(block):
    stages = list(zip(*gather_orders()))
    for first, second in stages[:-1]:
        block = jnp.concatenate([block, flip(block, first, second)], axis=0)
    return block, flip(block, *stages[-1])


def gathered_blocks():
    tables = []
    for order in gather_orders():
        slots = [0]
        for _, k in order:
            slots = slots + [slot | (1 << k) for slot in slots]
        tables.append(slots)
    mine = jnp.where(lax.axis_index("wsh") == 0, jnp.array(tables[0]), jnp.array(tables[1]))
    return mine ^ lax.axis_index("ctx")


def sum_orders():
    seq, ctx = bits_of("seq"), bits_of("ctx")
    return list(zip(seq + ctx[1:2] + ctx[:1] + ctx[2:], ctx[:2] + seq + ctx[2:]))


def stage_bit(first, second):
    return jnp.where(lax.axis_index("wsh") == 0, my_bit(*first), my_bit(*second))


def scatter_sum(rows):
    parts = [rows]
    for first, second in sum_orders():
        bit = stage_bit(first, second)
        half = parts[0].shape[0] // 2

        def side(which):
            cut = [lax.dynamic_slice_in_dim(part, which * half, half, 0) for part in parts]
            if len(cut) == 1:
                return cut[0]
            return (cut[0].astype(F32) + cut[1].astype(F32)).astype(BF16)

        away = side(1 - bit)
        parts = [side(bit), flip(away, first, second)]
    return (parts[0].astype(F32) + parts[1].astype(F32)).astype(BF16)


def gather_rows(rows):
    stages = sum_orders()[::-1]
    for first, second in stages[:-1]:
        bit = stage_bit(first, second)
        other = flip(rows, first, second)
        low = jnp.where(bit == 0, rows, other)
        high = jnp.where(bit == 0, other, rows)
        rows = jnp.concatenate([low, high], axis=0)
    return rows, flip(rows, *stages[-1]), stage_bit(*stages[-1])


def both_halves(block):
    other = swap_cores(block)
    core = lax.axis_index("wsh")
    return jnp.concatenate(
        [jnp.where(core == 0, block, other), jnp.where(core == 0, other, block)], axis=0
    )


def dot_nn(a, b):
    return lax.dot_general(a, b, (((1,), (0,)), ((), ())), preferred_element_type=F32)


def dot_nt(a, b):
    return lax.dot_general(a, b, (((1,), (1,)), ((), ())), preferred_element_type=F32)


def dot_tn(a, b):
    return lax.dot_general(a, b, (((0,), (0,)), ((), ())), preferred_element_type=F32)


def cost(flops, moved):
    return pl.CostEstimate(flops=int(flops), bytes_accessed=int(moved), transcendentals=0)


PARAMS = pltpu.CompilerParams(vmem_limit_bytes=40 * MIB)


def normalize(inputs):
    average = jnp.mean(inputs, axis=-1, keepdims=True)
    centred = inputs - average
    variance = jnp.mean(centred * centred, axis=-1, keepdims=True)
    rstd = lax.rsqrt(variance + EPSILON)
    return centred * rstd, rstd


def norm_back(grad_rows, normed, rstd, gain):
    scaled = grad_rows * gain
    inner = jnp.mean(scaled * normed, axis=-1, keepdims=True)
    return rstd * (scaled - jnp.mean(scaled, axis=-1, keepdims=True) - normed * inner)


def lane_of(shape):
    return lax.broadcasted_iota(jnp.int32, shape, len(shape) - 1)


def halves_swapped(vectors):
    first = (lane_of(vectors.shape) & 63) < 32
    return jnp.where(first, pltpu.roll(vectors, LANES - 32, 1), pltpu.roll(vectors, 32, 1))


def project_kernel(tokens, weights, gain, cos, sin, out):
    normed, _ = normalize(tokens[...].astype(F32))
    low = (normed * gain[...].astype(F32)).astype(BF16)
    width = tokens.shape[1]
    cos_rows, sin_rows = cos[...], sin[...]
    for part in range(3):
        columns = dot_nn(low, weights[:, part * width : (part + 1) * width])
        for j in range(width // LANES):
            piece = columns[:, j * LANES : (j + 1) * LANES]
            if part < 2:
                piece = piece * cos_rows + halves_swapped(piece) * sin_rows
            if part == 0:
                piece = piece * 0.125
            at = part * width + j * LANES
            out[:, at : at + LANES] = piece.astype(BF16)


def project(tokens, weights, gain, cos, sin):
    rows, width = tokens.shape
    step = min(rows, 256)
    return pl.pallas_call(
        project_kernel,
        grid=(rows // step,),
        in_specs=[
            pl.BlockSpec((step, width), lambda i: (i, 0)),
            pl.BlockSpec((width, 3 * width), lambda i: (0, 0)),
            pl.BlockSpec((1, width), lambda i: (0, 0)),
            pl.BlockSpec((step, LANES), lambda i: (i, 0)),
            pl.BlockSpec((step, LANES), lambda i: (i, 0)),
        ],
        out_specs=pl.BlockSpec((step, 3 * width), lambda i: (i, 0)),
        out_shape=jax.ShapeDtypeStruct((rows, 3 * width), BF16),
        compiler_params=PARAMS,
        cost_estimate=cost(6 * rows * width * width, 8 * rows * width),
        name="project",
    )(tokens, weights, gain, cos, sin)


def two_heads(block):
    first = lane_of(block.shape) < 64
    zero = jnp.zeros_like(block)
    return jnp.concatenate([jnp.where(first, block, zero), jnp.where(first, zero, block)], axis=0)


def one_pair(stacked):
    rows = stacked.shape[0] // 2
    return jnp.where(lane_of((rows, LANES)) < 64, stacked[:rows], stacked[rows:])


def column_pair(columns, at):
    lanes = lane_of(columns.shape)
    picked = [
        jnp.sum(jnp.where(lanes == at + k, columns, 0.0), axis=1, keepdims=True) for k in (0, 1)
    ]
    return jnp.concatenate(picked, axis=0)


def put_pair(ref, pair, values):
    rows = ref.shape[0]

    @pl.when(pair == 0)
    def _():
        ref[...] = jnp.zeros_like(ref)

    lanes = lane_of((rows, LANES))
    kept = jnp.where(lanes == 2 * pair, values[:rows], ref[...])
    ref[...] = jnp.where(lanes == 2 * pair + 1, values[rows:], kept)


def chunks_of(count):
    step = min(count, 1024)
    return [slice(at, at + step) for at in range(0, count, step)]


def attend_over(stacked, keys, values, peak, total, mixed):
    for at in chunks_of(keys.shape[0]):
        logits = dot_nt(stacked, keys[at, :])
        top = jnp.max(logits, axis=1, keepdims=True)
        if peak is None:
            weights = jnp.exp(logits - top)
            total = jnp.sum(weights, axis=1, keepdims=True)
            mixed = dot_nn(weights.astype(BF16), values[at, :])
        else:
            top = jnp.maximum(peak, top)
            weights = jnp.exp(logits - top)
            factor = jnp.exp(peak - top)
            total = total * factor + jnp.sum(weights, axis=1, keepdims=True)
            mixed = mixed * factor + dot_nn(weights.astype(BF16), values[at, :])
        peak = top
    return peak, total, mixed


def attend_first_kernel(queries, keys, values, out_mixed, out_peak, out_total):
    pair = pl.program_id(0)
    stacked = two_heads(queries[...])
    peak, total, mixed = attend_over(stacked, keys, values, None, None, None)
    out_mixed[...] = one_pair(mixed)
    put_pair(out_peak, pair, peak)
    put_pair(out_total, pair, total)


def attend_last_kernel(
    queries, keys, values, in_mixed, in_peak, in_total, attended, log_total
):
    pair = pl.program_id(0)
    stacked = two_heads(queries[...])
    peak = column_pair(in_peak[...], 2 * pair)
    total = column_pair(in_total[...], 2 * pair)
    mixed = jnp.concatenate([in_mixed[...]] * 2, axis=0)
    peak, total, mixed = attend_over(stacked, keys, values, peak, total, mixed)
    attended[...] = one_pair(mixed / total)
    put_pair(log_total, pair, peak + jnp.log(total))


def attend(halves, rows):
    count, width = halves[0].shape[0], halves[0].shape[1] // 3
    pairs = width // LANES
    queries = pl.BlockSpec((rows, LANES), lambda j: (0, j))
    shared = pl.BlockSpec((rows, LANES), lambda j: (0, 0))
    keys = pl.BlockSpec((count, LANES), lambda j: (0, pairs + j))
    values = pl.BlockSpec((count, LANES), lambda j: (0, 2 * pairs + j))
    wide = jax.ShapeDtypeStruct((rows, width), F32)
    thin = jax.ShapeDtypeStruct((rows, LANES), F32)
    work = cost(8 * rows * count * width, 6 * count * width)
    mixed, peak, total = pl.pallas_call(
        attend_first_kernel,
        grid=(pairs,),
        in_specs=[queries, keys, values],
        out_specs=[queries, shared, shared],
        out_shape=[wide, thin, thin],
        compiler_params=PARAMS,
        cost_estimate=work,
        name="attend_first",
    )(halves[0], halves[0], halves[0])
    return pl.pallas_call(
        attend_last_kernel,
        grid=(pairs,),
        in_specs=[queries, keys, values, queries, shared, shared],
        out_specs=[queries, shared],
        out_shape=[wide, thin],
        compiler_params=PARAMS,
        cost_estimate=work,
        name="attend_last",
    )(halves[0], halves[1], halves[1], mixed, peak, total)


def middle_kernel(
    core, tokens, attended, log_total, cotangent, w_out, w_in, w_mlp, gain,
    layer_out, own_halves, other_halves, whole,
    grad_middle, sent, logs_deltas, gain_grad,
):
    rows, width = tokens.shape
    first = core[0] == 0

    def put_halves(at, block):
        half = block.shape[1] // 2
        left, right = block[:, :half], block[:, half:]
        own_halves[:, at : at + half] = jnp.where(first, left, right)
        other_halves[:, at : at + half] = jnp.where(first, right, left)

    mixed = attended[...]
    mixed_low = mixed.astype(BF16)
    put_halves(ATTENDED_AT, mixed_low)
    middle = tokens[...].astype(F32) + dot_nn(mixed_low, w_out[...])
    normed, rstd = normalize(middle)
    gain_row = gain[...].astype(F32)
    second = (normed * gain_row).astype(BF16)
    put_halves(NORMED_AT, second)
    gate = dot_nn(second, w_in[:, :FF])
    up = dot_nn(second, w_in[:, FF:])
    cdf = 0.5 * (1.0 + lax.erf(gate * (0.5**0.5)))
    activated = gate * cdf
    hidden = (activated * up).astype(BF16)
    put_halves(0, hidden)
    layer_out[...] = (middle + dot_nn(hidden, w_mlp[...])).astype(BF16)
    upstream = cotangent[...]
    grad_hidden = dot_nt(upstream, w_mlp[...]).astype(BF16).astype(F32)
    density = jnp.exp(-0.5 * gate * gate) * 0.3989422804014327
    grad_gate = (grad_hidden * up * (cdf + gate * density)).astype(BF16)
    grad_up = (grad_hidden * activated).astype(BF16)
    whole[:, :FF] = grad_gate
    whole[:, FF : 2 * FF] = grad_up
    grad_second = dot_nt(grad_gate, w_in[:, :FF]) + dot_nt(grad_up, w_in[:, FF:])
    gain_grad[...] = jnp.sum(grad_second * normed, axis=0, keepdims=True)
    grad_mid = upstream.astype(F32) + norm_back(grad_second, normed, rstd, gain_row)
    grad_middle[...] = grad_mid
    branch = grad_mid.astype(BF16)
    whole[:, 2 * FF :] = branch
    grad_attended = dot_nt(branch, w_out[...]).astype(BF16)
    sent[:, :width] = grad_attended
    products = grad_attended.astype(F32) * mixed
    head = lax.broadcasted_iota(jnp.int32, (width, LANES), 0) // 64
    to_lane = (lane_of((width, LANES)) == head + HEADS).astype(F32)
    both = log_total[...] + lax.dot_general(
        products,
        to_lane,
        (((1,), (0,)), ((), ())),
        precision=lax.Precision.HIGHEST,
        preferred_element_type=F32,
    )
    logs_deltas[...] = both
    high = both.astype(BF16).astype(F32)
    rest = both - high
    mid = rest.astype(BF16).astype(F32)
    last = rest - mid
    packed = high + pltpu.roll(mid, PIECE, 1) + pltpu.roll(last, 2 * PIECE, 1)
    sent[:, width:] = packed.astype(BF16)


VMEM_SPEC = pl.BlockSpec(memory_space=pltpu.VMEM)


def middle_part(core, tokens, attended, log_total, cotangent, w_out, w_in, w_mlp, gain):
    rows, width = tokens.shape
    shapes = [
        ((rows, width), BF16),
        ((rows, HALVES_WIDTH), BF16),
        ((rows, HALVES_WIDTH), BF16),
        ((rows, 2 * FF + width), BF16),
        ((rows, width), F32),
        ((rows, width + LANES), BF16),
        ((rows, LANES), F32),
        ((1, width), F32),
    ]
    return pl.pallas_call(
        middle_kernel,
        in_specs=[pl.BlockSpec(memory_space=pltpu.SMEM)] + [VMEM_SPEC] * 8,
        out_shape=[jax.ShapeDtypeStruct(*shape) for shape in shapes],
        compiler_params=PARAMS,
        cost_estimate=cost(4 * rows * width * (2 * width + 6 * FF), 24 * MIB),
        name="middle",
    )(core, tokens, attended, log_total, cotangent, w_out, w_in, w_mlp, gain)


def rows_kernel(width, items, gained, *refs):
    out = refs[-1]
    at = 0
    for k, (left_lanes, right_lanes) in enumerate(items):
        left_own, left_other, right_own, right_other = refs[4 * k : 4 * k + 4]
        left = jnp.concatenate([left_own[:, left_lanes], left_other[:, left_lanes]], axis=0)
        made = left.shape[1]
        turned = left.T
        for start in range(right_lanes.start, right_lanes.stop, width):
            lanes = slice(start, start + width)
            right = jnp.concatenate([right_own[:, lanes], right_other[:, lanes]], axis=0)
            out[at : at + made, :] = dot_nn(turned, right).astype(BF16)
            at += made
    if at < out.shape[0]:
        out[at:, :] = jnp.zeros((out.shape[0] - at, width), BF16)
    if gained:
        own, other = refs[4 * len(items) : 4 * len(items) + 2]
        half = own.shape[1]
        tile = (16, half)
        top = lax.broadcasted_iota(jnp.int32, tile, 0) == 0
        row = jnp.broadcast_to(own[...] + other[...], tile)
        out[at : at + 16, :half] = jnp.where(top, row, 0.0).astype(BF16)


def grad_rows(width, pieces, items, gain=None):
    lanes, arrays, used = [], [], 0
    for left_own, left_other, left_lanes, right_own, right_other, right_lanes in items:
        arrays += [left_own, left_other, right_own, right_other]
        lanes.append((left_lanes, right_lanes))
        blocks = (right_lanes.stop - right_lanes.start) // width
        used += (left_lanes.stop - left_lanes.start) * blocks
    flops = 4 * items[0][0].shape[0] * used * width
    if gain is not None:
        arrays += gain
        used += 1
    unit = 8 * pieces
    total = (used + unit - 1) // unit * unit
    return pl.pallas_call(
        partial(rows_kernel, width, lanes, gain is not None),
        in_specs=[VMEM_SPEC] * len(arrays),
        out_shape=jax.ShapeDtypeStruct((total, width), BF16),
        compiler_params=PARAMS,
        cost_estimate=cost(flops, 4 * total * width),
        name="grad_rows",
    )(*arrays)


def unpack_kernel(places, gained, bit, own, other, *outs):
    half = own.shape[0]

    def put(low, high):
        at = 0
        for out, blocks in places:
            ref = outs[out]
            made = ref.shape[0]
            for k in range(blocks):
                columns = slice(k * low.shape[1], (k + 1) * low.shape[1])
                cut = min(max(half - at, 0), made)
                if cut > 0:
                    ref[:cut, columns] = low[at : at + cut, :].astype(F32)
                if cut < made:
                    start = at + cut - half
                    ref[cut:, columns] = high[start : start + made - cut, :].astype(F32)
                at += made
        if gained:
            ref = outs[-1]
            source, row = (low, at) if at < half else (high, at - half)
            ref[...] = source[row : row + 16, : ref.shape[1]].astype(F32)[:1]

    @pl.when(bit[0] == 0)
    def _():
        put(own, other)

    @pl.when(bit[0] != 0)
    def _():
        put(other, own)


def unpack(rows, shapes, gained=False):
    own, other, bit = gather_rows(scatter_sum(rows))
    width = own.shape[1]
    places = [(k, shape[1] // width) for k, shape in enumerate(shapes)]
    if gained:
        shapes = shapes + [(1, width // 2)]
    return pl.pallas_call(
        partial(unpack_kernel, places, gained),
        in_specs=[pl.BlockSpec(memory_space=pltpu.SMEM), VMEM_SPEC, VMEM_SPEC],
        out_shape=[jax.ShapeDtypeStruct(shape, F32) for shape in shapes],
        compiler_params=PARAMS,
        cost_estimate=cost(0, 12 * own.size),
        name="unpack",
    )(bit.reshape(1), own, other)


def unrotated(block, cos, sin):
    return block * cos - halves_swapped(block) * sin


def query_grad_kernel(
    queries, keys_a, values_a, keys_b, values_b, grads, logs_deltas, cos, sin, out
):
    pair = pl.program_id(0)
    rows = queries.shape[0]
    stacked = two_heads(queries[...])
    grads_two = two_heads(grads[...])
    logs = column_pair(logs_deltas[...], 2 * pair)
    deltas = column_pair(logs_deltas[...], HEADS + 2 * pair)
    total = jnp.zeros((2 * rows, LANES), F32)
    for keys, values in ((keys_a, values_a), (keys_b, values_b)):
        for at in chunks_of(keys.shape[0]):
            key_rows = keys[at, :]
            probs = jnp.exp(dot_nt(stacked, key_rows) - logs)
            grad_probs = dot_nt(grads_two, values[at, :])
            grad_scores = (probs * (grad_probs - deltas)).astype(BF16)
            total = total + dot_nn(grad_scores, key_rows)
    grad = one_pair(total) * 0.125
    out[...] = unrotated(grad, cos[...], sin[...]).astype(BF16)


def query_grads(halves, sent, logs_deltas, cos, sin, rows):
    count, width = halves[0].shape[0], halves[0].shape[1] // 3
    pairs = width // LANES
    queries = pl.BlockSpec((rows, LANES), lambda j: (0, j))
    shared = pl.BlockSpec((rows, LANES), lambda j: (0, 0))
    keys = pl.BlockSpec((count, LANES), lambda j: (0, pairs + j))
    values = pl.BlockSpec((count, LANES), lambda j: (0, 2 * pairs + j))
    return pl.pallas_call(
        query_grad_kernel,
        grid=(pairs,),
        in_specs=[queries, keys, values, keys, values, queries, shared, shared, shared],
        out_specs=queries,
        out_shape=jax.ShapeDtypeStruct((rows, width), BF16),
        compiler_params=PARAMS,
        cost_estimate=cost(24 * rows * count * width, 12 * count * width),
        name="query_grads",
    )(
        halves[0], halves[0], halves[0], halves[1], halves[1],
        sent, logs_deltas, cos, sin,
    )


def key_grads_over(pair, keys, values, queries, grads, packed, total_keys, total_values):
    rows = keys.shape[0]
    keys_two = two_heads(keys[...])
    values_two = two_heads(values[...])
    pick_shape = (8, LANES)
    row = lax.broadcasted_iota(jnp.int32, pick_shape, 0)
    lane = lane_of(pick_shape)
    wanted = 2 * pair + (row & 1) + jnp.where(row >= 2, HEADS, 0)
    held = (lane == wanted) | (lane == wanted + PIECE) | (lane == wanted + 2 * PIECE)
    pick = jnp.where(held, 1.0, 0.0).astype(BF16)
    for at in chunks_of(queries.shape[0]):
        query_rows, grad_rows_ = queries[at, :], grads[at, :]
        picked = dot_nt(pick, packed[at, :])
        shape = (rows, query_rows.shape[0])
        logs, deltas = (
            jnp.concatenate(
                [jnp.broadcast_to(picked[k : k + 1], shape) for k in (base, base + 1)], axis=0
            )
            for base in (0, 2)
        )
        probs = jnp.exp(dot_nt(keys_two, query_rows) - logs)
        grad_probs = dot_nt(values_two, grad_rows_)
        grad_scores = (probs * (grad_probs - deltas)).astype(BF16)
        add_values = dot_nn(probs.astype(BF16), grad_rows_)
        add_keys = dot_nn(grad_scores, query_rows)
        total_values = add_values if total_values is None else total_values + add_values
        total_keys = add_keys if total_keys is None else total_keys + add_keys
    return total_keys, total_values


def key_first_kernel(keys, values, queries, grads, packed, out_keys, out_values):
    pair = pl.program_id(0)
    grad_k, grad_v = key_grads_over(pair, keys, values, queries, grads, packed, None, None)
    out_keys[...] = one_pair(grad_k)
    out_values[...] = one_pair(grad_v)


def key_last_kernel(
    keys, values, queries, grads, packed, first_keys, first_values, cos, sin, out_keys, out_values
):
    pair = pl.program_id(0)
    grad_k, grad_v = key_grads_over(pair, keys, values, queries, grads, packed, None, None)
    grad_k = one_pair(grad_k) + first_keys[...]
    out_keys[...] = unrotated(grad_k, cos[...], sin[...]).astype(BF16)
    out_values[...] = (one_pair(grad_v) + first_values[...]).astype(BF16)


def key_grads(halves, sent_halves, cos, sin, rows):
    count, width = halves[0].shape[0], halves[0].shape[1] // 3
    pairs = width // LANES
    keys = pl.BlockSpec((rows, LANES), lambda j: (0, pairs + j))
    values = pl.BlockSpec((rows, LANES), lambda j: (0, 2 * pairs + j))
    queries = pl.BlockSpec((count, LANES), lambda j: (0, j))
    packed = pl.BlockSpec((count, LANES), lambda j: (0, pairs))
    own = pl.BlockSpec((rows, LANES), lambda j: (0, j))
    shared = pl.BlockSpec((rows, LANES), lambda j: (0, 0))
    work = cost(16 * rows * count * width, 6 * count * width)
    first = pl.pallas_call(
        key_first_kernel,
        grid=(pairs,),
        in_specs=[keys, values, queries, queries, packed],
        out_specs=[own, own],
        out_shape=[jax.ShapeDtypeStruct((rows, width), F32)] * 2,
        compiler_params=PARAMS,
        cost_estimate=work,
        name="key_grads_first",
    )(halves[0], halves[0], halves[0], sent_halves[0], sent_halves[0])
    return pl.pallas_call(
        key_last_kernel,
        grid=(pairs,),
        in_specs=[keys, values, queries, queries, packed, own, own, shared, shared],
        out_specs=[own, own],
        out_shape=[jax.ShapeDtypeStruct((rows, width), BF16)] * 2,
        compiler_params=PARAMS,
        cost_estimate=work,
        name="key_grads_last",
    )(
        halves[0], halves[0], halves[1], sent_halves[1], sent_halves[1],
        first[0], first[1], cos, sin,
    )


def last_kernel(tokens, grad_middle, grad_q, grad_k, grad_v, weights, gain, out, gain_grad):
    width = tokens.shape[1]
    normed, rstd = normalize(tokens[...].astype(F32))
    grad_first = dot_nt(grad_q[...], weights[:, :width])
    grad_first = grad_first + dot_nt(grad_k[...], weights[:, width : 2 * width])
    grad_first = grad_first + dot_nt(grad_v[...], weights[:, 2 * width :])
    gain_grad[...] = jnp.sum(grad_first * normed, axis=0, keepdims=True)
    back = norm_back(grad_first, normed, rstd, gain[...].astype(F32))
    out[...] = (grad_middle[...] + back).astype(BF16)


def last_part(tokens, grad_middle, grad_q, grad_k, grad_v, weights, gain):
    rows, width = tokens.shape
    return pl.pallas_call(
        last_kernel,
        in_specs=[VMEM_SPEC] * 7,
        out_shape=[
            jax.ShapeDtypeStruct((rows, width), BF16),
            jax.ShapeDtypeStruct((1, width), F32),
        ],
        compiler_params=PARAMS,
        cost_estimate=cost(6 * rows * width * width, 8 * MIB),
        name="last",
    )(tokens, grad_middle, grad_q, grad_k, grad_v, weights, gain)


def rotary_tables(positions, head_dim):
    half = head_dim // 2
    inverse = jnp.power(F32(THETA), -(jnp.arange(half, dtype=F32) * (2.0 / head_dim)))
    angles = positions[:, None] * inverse[None, :]
    cos, sin = jnp.cos(angles), jnp.sin(angles)
    return (
        jnp.concatenate([cos, cos, cos, cos], axis=1),
        jnp.concatenate([-sin, sin, -sin, sin], axis=1),
    )


def local(tokens, w_qkv, w_out, w_in, w_mlp, gain_attn, gain_mlp, cotangent):
    seqs_here, rows, width = tokens.shape
    half, half_ff = width // 2, FF // 2
    core = lax.axis_index("wsh")
    own = tokens.reshape(rows, width)
    upstream = cotangent.reshape(rows, width)
    pieces = lax.axis_size("seq") * lax.axis_size("ctx")

    gathered = gather_context(own)
    full_qkv = both_halves(w_qkv)
    gains = jnp.stack([gain_attn, gain_mlp])
    gains_other = swap_cores(gains)
    gains_all = jnp.concatenate(
        [jnp.where(core == 0, gains, gains_other), jnp.where(core == 0, gains_other, gains)], axis=1
    )
    attn_gain, mlp_gain = gains_all[:1], gains_all[1:]
    full_out = both_halves(w_out)
    full_in = both_halves(w_in)
    full_mlp = both_halves(w_mlp)
    upstream_other = swap_cores(upstream)
    first_in = (normalize(own.astype(F32))[0] * attn_gain.astype(F32)).astype(BF16)
    first_own = lax.dynamic_slice_in_dim(first_in, core * half, half, 1)
    first_other = swap_cores(lax.dynamic_slice_in_dim(first_in, (1 - core) * half, half, 1))

    blocks = gathered_blocks()
    positions = (blocks[:, None] * rows + jnp.arange(rows, dtype=jnp.int32)[None, :]).reshape(-1)
    cos, sin = rotary_tables(positions.astype(F32), 64)
    own_cos, own_sin = cos[:rows], sin[:rows]
    count = gathered[0].shape[0]
    halves = [
        project(
            part, full_qkv, attn_gain,
            cos[k * count : (k + 1) * count], sin[k * count : (k + 1) * count],
        )
        for k, part in enumerate(gathered)
    ]

    attended, log_total = attend(halves, rows)
    (
        layer_out, own_halves, other_halves, whole,
        grad_middle, sent, logs_deltas, gain_mlp_part,
    ) = middle_part(
        core.reshape(1), own, attended, log_total, upstream,
        full_out, full_in, full_mlp, mlp_gain,
    )

    def gain_pair(part):
        mine = lax.dynamic_slice_in_dim(part, core * half, half, 1)
        theirs = lax.dynamic_slice_in_dim(part, (1 - core) * half, half, 1)
        return [mine, swap_cores(theirs)]

    sent_halves = gather_context(sent)
    other_halves = swap_cores(other_halves)
    whole_other = swap_cores(whole)

    mlp_rows = grad_rows(
        width,
        pieces,
        [(own_halves, other_halves, slice(0, half_ff), upstream, upstream_other, slice(0, width))],
        gain_pair(gain_mlp_part),
    )
    in_rows = grad_rows(
        width,
        pieces,
        [
            (
                own_halves, other_halves, slice(NORMED_AT, NORMED_AT + half),
                whole, whole_other, slice(0, 2 * FF),
            )
        ],
    )
    grad_q = query_grads(halves, sent, logs_deltas, own_cos, own_sin, rows)
    out_rows = grad_rows(
        width,
        pieces,
        [
            (
                own_halves, other_halves, slice(ATTENDED_AT, ATTENDED_AT + half),
                whole, whole_other, slice(2 * FF, 2 * FF + width),
            ),
            (
                first_own, first_other, slice(0, half),
                grad_q, swap_cores(grad_q), slice(0, width),
            ),
        ],
    )
    grad_k, grad_v = key_grads(halves, sent_halves, own_cos, own_sin, rows)
    tokens_grad, gain_attn_part = last_part(
        own, grad_middle, grad_q, grad_k, grad_v, full_qkv, attn_gain
    )
    key_rows = grad_rows(
        width,
        pieces,
        [
            (first_own, first_other, slice(0, half), grad_k, swap_cores(grad_k), slice(0, width)),
            (first_own, first_other, slice(0, half), grad_v, swap_cores(grad_v), slice(0, width)),
        ],
        gain_pair(gain_attn_part),
    )

    mlp_grad, gain_mlp_grad = unpack(mlp_rows, [(half_ff, width)], True)
    (in_grad,) = unpack(in_rows, [(half, 2 * FF)])
    out_grad, q_grad = unpack(out_rows, [(half, width), (half, width)])
    kv_grad, gain_attn_grad = unpack(key_rows, [(half, 2 * width)], True)
    return (
        layer_out.reshape(seqs_here, rows, width),
        tokens_grad.reshape(seqs_here, rows, width),
        jnp.concatenate([q_grad, kv_grad], axis=1),
        out_grad,
        in_grad,
        mlp_grad,
        gain_attn_grad.reshape(half),
        gain_mlp_grad.reshape(half),
    )


def solution(mesh):
    placed = (
        P(("seq", "wsh"), "ctx", None),
        P("wsh", None),
        P("wsh", None),
        P("wsh", None),
        P("wsh", None),
        P("wsh"),
        P("wsh"),
        P(("seq", "wsh"), "ctx", None),
    )
    return jax.shard_map(
        local,
        mesh=mesh,
        in_specs=placed,
        out_specs=(
            P(("seq", "wsh"), "ctx", None),
            P(("seq", "wsh"), "ctx", None),
            P("wsh", None),
            P("wsh", None),
            P("wsh", None),
            P("wsh", None),
            P("wsh"),
            P("wsh"),
        ),
        check_vma=False,
    )
```

```python
from functools import partial

import jax
import jax.numpy as jnp
from jax import lax
from jax.experimental import pallas as pl
from jax.experimental.pallas import tpu as pltpu
from jax.sharding import PartitionSpec as P

HEADS = 12
FF = 1152
EPSILON = 1e-05
THETA = 160000.0
LANES = 128
NORMED_AT = 640
ATTENDED_AT = 1024
HALVES_WIDTH = 1408
MIB = 1 << 20
BF16 = jnp.bfloat16
F32 = jnp.float32


def bits_of(axis):
    return [(axis, k) for k in range((lax.axis_size(axis) - 1).bit_length())]


def my_bit(axis, k):
    return (lax.axis_index(axis) >> k) & 1


def flip(block, first, second):
    n_seq, n_ctx = lax.axis_size("seq"), lax.axis_size("ctx")
    route = []
    for s in range(n_seq):
        for t in range(n_ctx):
            for core, (axis, k) in enumerate((first, second)):
                s2, t2 = (s ^ (1 << k), t) if axis == "seq" else (s, t ^ (1 << k))
                route.append(((s * n_ctx + t) * 2 + core, (s2 * n_ctx + t2) * 2 + core))
    return lax.ppermute(block, ("seq", "ctx", "wsh"), route)


def swap_cores(block):
    return lax.ppermute(block, "wsh", [(0, 1), (1, 0)])


def gather_orders():
    bits = bits_of("ctx")
    return bits[::-1], bits[:1] + bits[:0:-1]


def gather_context(block, ready):
    stages = list(zip(*gather_orders()))
    for first, second in stages[:-1]:
        block = jnp.concatenate([block, flip(block, first, second)], axis=0)
    block, ready = lax.optimization_barrier((block, ready))
    return (block, flip(block, *stages[-1])), ready


def scatter_context(rows):
    parts = [rows]
    for first, second in list(zip(*gather_orders()))[::-1]:
        half = parts[0].shape[0] // 2
        away, kept = (
            sum(part[at : at + half].astype(F32) for part in parts).astype(BF16) for at in (half, 0)
        )
        parts = [kept, flip(away, first, second)]
    return parts


def gathered_blocks():
    tables = []
    for order in gather_orders():
        slots = [0]
        for _, k in order:
            slots = slots + [slot | (1 << k) for slot in slots]
        tables.append(slots)
    mine = jnp.where(lax.axis_index("wsh") == 0, jnp.array(tables[0]), jnp.array(tables[1]))
    return mine ^ lax.axis_index("ctx")


def sum_orders():
    seq, ctx = bits_of("seq"), bits_of("ctx")
    return list(zip(seq + ctx[1:2] + ctx[:1] + ctx[2:], ctx[:2] + seq + ctx[2:]))


def stage_bit(first, second):
    return jnp.where(lax.axis_index("wsh") == 0, my_bit(*first), my_bit(*second))


def scatter_sum(parts):
    for first, second in sum_orders():
        bit = stage_bit(first, second)
        half = parts[0].shape[0] // 2

        def side(which):
            cut = [lax.dynamic_slice_in_dim(part, which * half, half, 0) for part in parts]
            if len(cut) == 1:
                return cut[0]
            return (cut[0].astype(F32) + cut[1].astype(F32)).astype(BF16)

        away = side(1 - bit)
        parts = [side(bit), flip(away, first, second)]
    return (parts[0].astype(F32) + parts[1].astype(F32)).astype(BF16)


def gather_rows(rows):
    stages = sum_orders()[::-1]
    for first, second in stages[:-1]:
        bit = stage_bit(first, second)
        other = flip(rows, first, second)
        low = jnp.where(bit == 0, rows, other)
        high = jnp.where(bit == 0, other, rows)
        rows = jnp.concatenate([low, high], axis=0)
    return rows, flip(rows, *stages[-1]), stage_bit(*stages[-1])


def both_halves(block):
    other = swap_cores(block)
    core = lax.axis_index("wsh")
    return jnp.concatenate(
        [jnp.where(core == 0, block, other), jnp.where(core == 0, other, block)], axis=0
    )


def dot_nn(a, b):
    return lax.dot_general(a, b, (((1,), (0,)), ((), ())), preferred_element_type=F32)


def dot_nt(a, b):
    return lax.dot_general(a, b, (((1,), (1,)), ((), ())), preferred_element_type=F32)


def dot_tn(a, b):
    return lax.dot_general(a, b, (((0,), (0,)), ((), ())), preferred_element_type=F32)


def cost(flops, moved):
    return pl.CostEstimate(flops=int(flops), bytes_accessed=int(moved), transcendentals=0)


PARAMS = pltpu.CompilerParams(vmem_limit_bytes=40 * MIB)


def normalize(inputs):
    average = jnp.mean(inputs, axis=-1, keepdims=True)
    centred = inputs - average
    variance = jnp.mean(centred * centred, axis=-1, keepdims=True)
    rstd = lax.rsqrt(variance + EPSILON)
    return centred * rstd, rstd


def norm_back(grad_rows, normed, rstd, gain):
    scaled = grad_rows * gain
    inner = jnp.mean(scaled * normed, axis=-1, keepdims=True)
    return rstd * (scaled - jnp.mean(scaled, axis=-1, keepdims=True) - normed * inner)


def lane_of(shape):
    return lax.broadcasted_iota(jnp.int32, shape, len(shape) - 1)


def halves_swapped(vectors):
    first = (lane_of(vectors.shape) & 63) < 32
    return jnp.where(first, pltpu.roll(vectors, LANES - 32, 1), pltpu.roll(vectors, 32, 1))


def project_kernel(tokens, weights, gain, cos, sin, out, *out_queries):
    normed, _ = normalize(tokens[...].astype(F32))
    low = (normed * gain[...].astype(F32)).astype(BF16)
    width = tokens.shape[1]

    def put(ref, start, rows, columns, turned, scale):
        for j in range(width // LANES):
            piece = columns[:, j * LANES : (j + 1) * LANES]
            if turned:
                piece = piece * cos[:rows, :] + halves_swapped(piece) * sin[:rows, :]
            ref[:, start + j * LANES : start + (j + 1) * LANES] = (piece * scale).astype(BF16)

    rows = tokens.shape[0]
    put(out, 0, rows, dot_nn(low, weights[:, width : 2 * width]), True, 1.0)
    put(out, width, rows, dot_nn(low, weights[:, 2 * width :]), False, 1.0)
    for ref in out_queries:

        @pl.when(pl.program_id(0) == 0)
        def _():
            own = ref.shape[0]
            put(ref, 0, own, dot_nn(low[:own], weights[:, :width]), True, 0.125)


def project(tokens, weights, gain, cos, sin, own_rows):
    rows, width = tokens.shape
    step = min(rows, 256)
    out_specs = [pl.BlockSpec((step, 2 * width), lambda i: (i, 0))]
    out_shape = [jax.ShapeDtypeStruct((rows, 2 * width), BF16)]
    if own_rows:
        out_specs.append(pl.BlockSpec((own_rows, width), lambda i: (0, 0)))
        out_shape.append(jax.ShapeDtypeStruct((own_rows, width), BF16))
    return pl.pallas_call(
        project_kernel,
        grid=(rows // step,),
        in_specs=[
            pl.BlockSpec((step, width), lambda i: (i, 0)),
            pl.BlockSpec((width, 3 * width), lambda i: (0, 0)),
            pl.BlockSpec((1, width), lambda i: (0, 0)),
            pl.BlockSpec((step, LANES), lambda i: (i, 0)),
            pl.BlockSpec((step, LANES), lambda i: (i, 0)),
        ],
        out_specs=out_specs,
        out_shape=out_shape,
        compiler_params=PARAMS,
        cost_estimate=cost(4 * rows * width * width, 8 * rows * width),
        name="project",
    )(tokens, weights, gain, cos, sin)


def two_heads(block):
    first = lane_of(block.shape) < 64
    zero = jnp.zeros_like(block)
    return jnp.concatenate([jnp.where(first, block, zero), jnp.where(first, zero, block)], axis=0)


def one_pair(stacked):
    rows = stacked.shape[0] // 2
    return jnp.where(lane_of((rows, LANES)) < 64, stacked[:rows], stacked[rows:])


def column_pair(columns, at):
    lanes = lane_of(columns.shape)
    picked = [
        jnp.sum(jnp.where(lanes == at + k, columns, 0.0), axis=1, keepdims=True) for k in (0, 1)
    ]
    return jnp.concatenate(picked, axis=0)


def put_pair(ref, pair, values):
    rows = ref.shape[0]

    @pl.when(pair == 0)
    def _():
        ref[...] = jnp.zeros_like(ref)

    lanes = lane_of((rows, LANES))
    kept = jnp.where(lanes == 2 * pair, values[:rows], ref[...])
    ref[...] = jnp.where(lanes == 2 * pair + 1, values[rows:], kept)


def chunks_of(count):
    step = min(count, 1024)
    return [slice(at, at + step) for at in range(0, count, step)]


def attend_over(stacked, keys, values, peak, total, mixed):
    for at in chunks_of(keys.shape[0]):
        logits = dot_nt(stacked, keys[at, :])
        top = jnp.max(logits, axis=1, keepdims=True)
        if peak is None:
            weights = jnp.exp(logits - top)
            total = jnp.sum(weights, axis=1, keepdims=True)
            mixed = dot_nn(weights.astype(BF16), values[at, :])
        else:
            top = jnp.maximum(peak, top)
            weights = jnp.exp(logits - top)
            factor = jnp.exp(peak - top)
            total = total * factor + jnp.sum(weights, axis=1, keepdims=True)
            mixed = mixed * factor + dot_nn(weights.astype(BF16), values[at, :])
        peak = top
    return peak, total, mixed


def attend_first_kernel(queries, keys, values, out_mixed, out_peak, out_total):
    pair = pl.program_id(0)
    stacked = two_heads(queries[...])
    peak, total, mixed = attend_over(stacked, keys, values, None, None, None)
    out_mixed[...] = one_pair(mixed)
    put_pair(out_peak, pair, peak)
    put_pair(out_total, pair, total)


def attend_last_kernel(
    queries, keys, values, in_mixed, in_peak, in_total, attended, log_total
):
    pair = pl.program_id(0)
    stacked = two_heads(queries[...])
    peak = column_pair(in_peak[...], 2 * pair)
    total = column_pair(in_total[...], 2 * pair)
    mixed = jnp.concatenate([in_mixed[...]] * 2, axis=0)
    peak, total, mixed = attend_over(stacked, keys, values, peak, total, mixed)
    attended[...] = one_pair(mixed / total)
    put_pair(log_total, pair, peak + jnp.log(total))


def attend(own_queries, halves):
    count = halves[0].shape[0]
    rows, width = own_queries.shape
    pairs = width // LANES
    queries = pl.BlockSpec((rows, LANES), lambda j: (0, j))
    shared = pl.BlockSpec((rows, LANES), lambda j: (0, 0))
    keys = pl.BlockSpec((count, LANES), lambda j: (0, j))
    values = pl.BlockSpec((count, LANES), lambda j: (0, pairs + j))
    wide = jax.ShapeDtypeStruct((rows, width), F32)
    thin = jax.ShapeDtypeStruct((rows, LANES), F32)
    work = cost(8 * rows * count * width, 6 * count * width)
    mixed, peak, total = pl.pallas_call(
        attend_first_kernel,
        grid=(pairs,),
        in_specs=[queries, keys, values],
        out_specs=[queries, shared, shared],
        out_shape=[wide, thin, thin],
        compiler_params=PARAMS,
        cost_estimate=work,
        name="attend_first",
    )(own_queries, halves[0], halves[0])
    return pl.pallas_call(
        attend_last_kernel,
        grid=(pairs,),
        in_specs=[queries, keys, values, queries, shared, shared],
        out_specs=[queries, shared],
        out_shape=[wide, thin],
        compiler_params=PARAMS,
        cost_estimate=work,
        name="attend_last",
    )(own_queries, halves[1], halves[1], mixed, peak, total)


def middle_kernel(
    core, tokens, attended, log_total, cotangent, w_out, w_in, w_mlp, gain,
    layer_out, own_halves, other_halves, whole,
    grad_middle, grads, logs_deltas, gain_grad,
):
    rows, width = tokens.shape
    first = core[0] == 0

    def put_halves(at, block):
        half = block.shape[1] // 2
        left, right = block[:, :half], block[:, half:]
        own_halves[:, at : at + half] = jnp.where(first, left, right)
        other_halves[:, at : at + half] = jnp.where(first, right, left)

    mixed = attended[...]
    mixed_low = mixed.astype(BF16)
    put_halves(ATTENDED_AT, mixed_low)
    middle = tokens[...].astype(F32) + dot_nn(mixed_low, w_out[...])
    normed, rstd = normalize(middle)
    gain_row = gain[...].astype(F32)
    second = (normed * gain_row).astype(BF16)
    put_halves(NORMED_AT, second)
    gate = dot_nn(second, w_in[:, :FF])
    up = dot_nn(second, w_in[:, FF:])
    cdf = 0.5 * (1.0 + lax.erf(gate * (0.5**0.5)))
    activated = gate * cdf
    hidden = (activated * up).astype(BF16)
    put_halves(0, hidden)
    layer_out[...] = (middle + dot_nn(hidden, w_mlp[...])).astype(BF16)
    upstream = cotangent[...]
    grad_hidden = dot_nt(upstream, w_mlp[...]).astype(BF16).astype(F32)
    density = jnp.exp(-0.5 * gate * gate) * 0.3989422804014327
    grad_gate = (grad_hidden * up * (cdf + gate * density)).astype(BF16)
    grad_up = (grad_hidden * activated).astype(BF16)
    whole[:, :FF] = grad_gate
    whole[:, FF : 2 * FF] = grad_up
    grad_second = dot_nt(grad_gate, w_in[:, :FF]) + dot_nt(grad_up, w_in[:, FF:])
    gain_grad[...] = jnp.sum(grad_second * normed, axis=0, keepdims=True)
    grad_mid = upstream.astype(F32) + norm_back(grad_second, normed, rstd, gain_row)
    grad_middle[...] = grad_mid
    branch = grad_mid.astype(BF16)
    whole[:, 2 * FF :] = branch
    grad_attended = dot_nt(branch, w_out[...]).astype(BF16)
    grads[...] = grad_attended
    products = grad_attended.astype(F32) * mixed
    head = lax.broadcasted_iota(jnp.int32, (width, LANES), 0) // 64
    to_lane = (lane_of((width, LANES)) == head + HEADS).astype(F32)
    both = log_total[...] + lax.dot_general(
        products,
        to_lane,
        (((1,), (0,)), ((), ())),
        precision=lax.Precision.HIGHEST,
        preferred_element_type=F32,
    )
    logs_deltas[...] = both.T


SMEM_SPEC = pl.BlockSpec(memory_space=pltpu.SMEM)
WHOLE = pl.BlockSpec()


def middle_part(core, tokens, attended, log_total, cotangent, w_out, w_in, w_mlp, gain):
    rows, width = tokens.shape
    shapes = [
        ((rows, width), BF16),
        ((rows, HALVES_WIDTH), BF16),
        ((rows, HALVES_WIDTH), BF16),
        ((rows, 2 * FF + width), BF16),
        ((rows, width), F32),
        ((rows, width), BF16),
        ((LANES, rows), F32),
        ((1, width), F32),
    ]
    return pl.pallas_call(
        middle_kernel,
        in_specs=[SMEM_SPEC] + [WHOLE] * 8,
        out_shape=[jax.ShapeDtypeStruct(*shape) for shape in shapes],
        compiler_params=PARAMS,
        cost_estimate=cost(4 * rows * width * (2 * width + 6 * FF), 24 * MIB),
        name="middle",
    )(core, tokens, attended, log_total, cotangent, w_out, w_in, w_mlp, gain)


def rows_kernel(width, items, gained, *refs):
    out = refs[-1]
    at = 0
    for k, (left_lanes, right_lanes) in enumerate(items):
        left_own, left_other, right_own, right_other = refs[4 * k : 4 * k + 4]
        left = jnp.concatenate([left_own[:, left_lanes], left_other[:, left_lanes]], axis=0)
        made = left.shape[1]
        turned = left.T
        for start in range(right_lanes.start, right_lanes.stop, width):
            lanes = slice(start, start + width)
            right = jnp.concatenate([right_own[:, lanes], right_other[:, lanes]], axis=0)
            out[at : at + made, :] = dot_nn(turned, right).astype(BF16)
            at += made
    if at < out.shape[0]:
        out[at:, :] = jnp.zeros((out.shape[0] - at, width), BF16)
    if gained:
        own, other = refs[4 * len(items) : 4 * len(items) + 2]
        half = own.shape[1]
        tile = (16, half)
        top = lax.broadcasted_iota(jnp.int32, tile, 0) == 0
        row = jnp.broadcast_to(own[...] + other[...], tile)
        out[at : at + 16, :half] = jnp.where(top, row, 0.0).astype(BF16)


def grad_rows(width, pieces, items, gain=None):
    lanes, arrays, used = [], [], 0
    for left_own, left_other, left_lanes, right_own, right_other, right_lanes in items:
        arrays += [left_own, left_other, right_own, right_other]
        lanes.append((left_lanes, right_lanes))
        blocks = (right_lanes.stop - right_lanes.start) // width
        used += (left_lanes.stop - left_lanes.start) * blocks
    flops = 4 * items[0][0].shape[0] * used * width
    if gain is not None:
        arrays += gain
        used += 1
    unit = 8 * pieces
    total = (used + unit - 1) // unit * unit
    return pl.pallas_call(
        partial(rows_kernel, width, lanes, gain is not None),
        in_specs=[WHOLE] * len(arrays),
        out_shape=jax.ShapeDtypeStruct((total, width), BF16),
        compiler_params=PARAMS,
        cost_estimate=cost(flops, 4 * total * width),
        name="grad_rows",
    )(*arrays)


def unpack_kernel(places, gained, bit, own, other, *outs):
    half = own.shape[0]

    def put(low, high):
        at = 0
        for out, blocks in places:
            ref = outs[out]
            made = ref.shape[0]
            for k in range(blocks):
                columns = slice(k * low.shape[1], (k + 1) * low.shape[1])
                cut = min(max(half - at, 0), made)
                if cut > 0:
                    ref[:cut, columns] = low[at : at + cut, :].astype(F32)
                if cut < made:
                    start = at + cut - half
                    ref[cut:, columns] = high[start : start + made - cut, :].astype(F32)
                at += made
        if gained:
            ref = outs[-1]
            source, row = (low, at) if at < half else (high, at - half)
            ref[...] = source[row : row + 16, : ref.shape[1]].astype(F32)[:1]

    @pl.when(bit[0] == 0)
    def _():
        put(own, other)

    @pl.when(bit[0] != 0)
    def _():
        put(other, own)


def unpack(parts, shapes, gained=False):
    own, other, bit = gather_rows(scatter_sum(parts))
    width = own.shape[1]
    places = [(k, shape[1] // width) for k, shape in enumerate(shapes)]
    if gained:
        shapes = shapes + [(1, width // 2)]
    return pl.pallas_call(
        partial(unpack_kernel, places, gained),
        in_specs=[SMEM_SPEC, WHOLE, WHOLE],
        out_shape=[jax.ShapeDtypeStruct(shape, F32) for shape in shapes],
        compiler_params=PARAMS,
        cost_estimate=cost(0, 12 * own.size),
        name="unpack",
    )(bit.reshape(1), own, other)


def unrotated(block, cos, sin):
    return block * cos - halves_swapped(block) * sin


def row_pair(rows, at):
    index = lax.broadcasted_iota(jnp.int32, rows.shape, 0)
    picked = [
        jnp.sum(jnp.where(index == at + k, rows, 0.0), axis=0, keepdims=True) for k in (0, 1)
    ]
    return jnp.concatenate(picked, axis=1)


def attend_back_kernel(
    queries, keys_a, values_a, keys_b, values_b, grads, logs_deltas, cos, sin,
    out_queries, out_keys, out_values,
):
    pair = pl.program_id(0)
    rows, count = queries.shape[0], keys_a.shape[0]
    queries_two = two_heads(queries[...])
    grads_two = two_heads(grads[...])
    logs = row_pair(logs_deltas[...], 2 * pair)
    deltas = row_pair(logs_deltas[...], HEADS + 2 * pair)
    total = jnp.zeros((2 * rows, LANES), F32)
    for base, keys, values in ((0, keys_a, values_a), (count, keys_b, values_b)):
        for at in chunks_of(count):
            to = slice(base + at.start, base + at.stop)
            key_rows = keys[at, :]
            probs = jnp.exp(dot_nt(key_rows, queries_two) - logs)
            grad_probs = dot_nt(values[at, :], grads_two)
            grad_scores = (probs * (grad_probs - deltas)).astype(BF16)
            out_values[to, :] = dot_nn(probs.astype(BF16), grads_two).astype(BF16)
            grad_keys = dot_nn(grad_scores, queries_two)
            out_keys[to, :] = unrotated(grad_keys, cos[to, :], sin[to, :]).astype(BF16)
            total = total + dot_tn(grad_scores, key_rows)
    grad = one_pair(total) * 0.125
    out_queries[...] = unrotated(grad, cos[:rows, :], sin[:rows, :]).astype(BF16)


def attend_back(own_queries, halves, grads, logs_deltas, cos, sin):
    count = halves[0].shape[0]
    rows, width = own_queries.shape
    pairs = width // LANES
    queries = pl.BlockSpec((rows, LANES), lambda j: (0, j))
    shared = pl.BlockSpec((LANES, rows), lambda j: (0, 0))
    keys = pl.BlockSpec((count, LANES), lambda j: (0, j))
    values = pl.BlockSpec((count, LANES), lambda j: (0, pairs + j))
    table = pl.BlockSpec((2 * count, LANES), lambda j: (0, 0))
    made = pl.BlockSpec((2 * count, LANES), lambda j: (0, j))
    return pl.pallas_call(
        attend_back_kernel,
        grid=(pairs,),
        in_specs=[queries, keys, values, keys, values, queries, shared, table, table],
        out_specs=[queries, made, made],
        out_shape=[
            jax.ShapeDtypeStruct((rows, width), BF16),
            jax.ShapeDtypeStruct((2 * count, width), BF16),
            jax.ShapeDtypeStruct((2 * count, width), BF16),
        ],
        compiler_params=PARAMS,
        cost_estimate=cost(40 * rows * count * width, 20 * count * width),
        name="attend_back",
    )(
        own_queries, halves[0], halves[0], halves[1], halves[1],
        grads, logs_deltas, cos, sin,
    )


def back_project_kernel(
    core, tokens_a, tokens_b, grad_q, grad_k, grad_v, weights, gain,
    out_first, out_own, out_other, totals, gain_total,
):
    step = pl.program_id(0)
    width = tokens_a.shape[1]
    half = width // 2
    own_rows = grad_q.shape[0]
    tokens = jnp.where(2 * step < pl.num_programs(0), tokens_a[...], tokens_b[...])
    normed, _ = normalize(tokens.astype(F32))
    low = (normed * gain[...].astype(F32)).astype(BF16)
    grad_first = dot_nt(grad_k[...], weights[:, width : 2 * width])
    grad_first = grad_first + dot_nt(grad_v[...], weights[:, 2 * width :])
    turned = low.T

    @pl.when(step == 0)
    def _():
        query_part = dot_nt(grad_q[...], weights[:, :width])
        first = grad_first[:own_rows] + query_part
        out_first[:own_rows, :] = first.astype(BF16)
        out_first[own_rows:, :] = grad_first[own_rows:].astype(BF16)
        gain_total[...] = jnp.sum(grad_first * normed, axis=0, keepdims=True) + jnp.sum(
            query_part * normed[:own_rows], axis=0, keepdims=True
        )
        totals[:, :width] = dot_nn(turned[:, :own_rows], grad_q[...])
        totals[:, width : 2 * width] = dot_nn(turned, grad_k[...])
        totals[:, 2 * width :] = dot_nn(turned, grad_v[...])

    @pl.when(step > 0)
    def _():
        out_first[...] = grad_first.astype(BF16)
        gain_total[...] += jnp.sum(grad_first * normed, axis=0, keepdims=True)
        totals[:, width : 2 * width] += dot_nn(turned, grad_k[...])
        totals[:, 2 * width :] += dot_nn(turned, grad_v[...])

    @pl.when(step == pl.num_programs(0) - 1)
    def _():
        tile = (16, half)
        top = lax.broadcasted_iota(jnp.int32, tile, 0) == 0
        sides = gain_total[:, :half], gain_total[:, half:]
        for out, side in ((out_own, core[0]), (out_other, 1 - core[0])):
            start = pl.multiple_of(side * half, half)
            for k in range(3):
                columns = slice(k * width, (k + 1) * width)
                out[k * half : (k + 1) * half, :] = totals[pl.ds(start, half), columns].astype(BF16)
            out[3 * half :, :] = jnp.zeros((out.shape[0] - 3 * half, width), BF16)
            row = jnp.broadcast_to(jnp.where(side == 0, *sides), tile)
            out[3 * half : 3 * half + 16, :half] = jnp.where(top, row, 0.0).astype(BF16)


def back_project(core, pieces, tokens, grad_q, grad_k, grad_v, weights, gain):
    count, width = tokens[0].shape
    rows, own_rows = 2 * count, grad_q.shape[0]
    step = min(count, 2 * own_rows)
    each = count // step
    unit = 8 * pieces
    total = (3 * (width // 2) + 1 + unit - 1) // unit * unit
    block = pl.BlockSpec((step, width), lambda i: (i, 0))

    def fixed(shape):
        return pl.BlockSpec(shape, lambda i: (0, 0))

    return pl.pallas_call(
        back_project_kernel,
        grid=(rows // step,),
        in_specs=[
            SMEM_SPEC,
            pl.BlockSpec((step, width), lambda i: (jnp.minimum(i, each - 1), 0)),
            pl.BlockSpec((step, width), lambda i: (jnp.maximum(i - each, 0), 0)),
            fixed((own_rows, width)), block, block,
            fixed((width, 3 * width)), fixed((1, width)),
        ],
        out_specs=[block, fixed((total, width)), fixed((total, width))],
        out_shape=[
            jax.ShapeDtypeStruct((rows, width), BF16),
            jax.ShapeDtypeStruct((total, width), BF16),
            jax.ShapeDtypeStruct((total, width), BF16),
        ],
        scratch_shapes=[pltpu.VMEM((width, 3 * width), F32), pltpu.VMEM((1, width), F32)],
        compiler_params=PARAMS,
        cost_estimate=cost(8 * rows * width * width, 12 * rows * width),
        name="back_project",
    )(core, *tokens, grad_q, grad_k, grad_v, weights, gain)


def last_kernel(tokens, grad_middle, part_a, part_b, gain, out):
    normed, rstd = normalize(tokens[...].astype(F32))
    grad_first = part_a[...].astype(F32) + part_b[...].astype(F32)
    back = norm_back(grad_first, normed, rstd, gain[...].astype(F32))
    out[...] = (grad_middle[...] + back).astype(BF16)


def last_part(tokens, grad_middle, parts, gain):
    return pl.pallas_call(
        last_kernel,
        out_shape=jax.ShapeDtypeStruct(tokens.shape, BF16),
        compiler_params=PARAMS,
        cost_estimate=cost(20 * tokens.size, 12 * tokens.size),
        name="last",
    )(tokens, grad_middle, *parts, gain)


def rotary_tables(positions, head_dim):
    half = head_dim // 2
    inverse = jnp.power(F32(THETA), -(jnp.arange(half, dtype=F32) * (2.0 / head_dim)))
    angles = positions[:, None] * inverse[None, :]
    cos, sin = jnp.cos(angles), jnp.sin(angles)
    return (
        jnp.concatenate([cos, cos, cos, cos], axis=1),
        jnp.concatenate([-sin, sin, -sin, sin], axis=1),
    )


def local(tokens, w_qkv, w_out, w_in, w_mlp, gain_attn, gain_mlp, cotangent):
    seqs_here, rows, width = tokens.shape
    half, half_ff = width // 2, FF // 2
    core = lax.axis_index("wsh")
    own = tokens.reshape(rows, width)
    upstream = cotangent.reshape(rows, width)
    pieces = lax.axis_size("seq") * lax.axis_size("ctx")

    full_qkv = both_halves(w_qkv)
    gathered, full_qkv = gather_context(own, full_qkv)
    gains = jnp.stack([gain_attn, gain_mlp])
    gains_other = swap_cores(gains)
    gains_all = jnp.concatenate(
        [jnp.where(core == 0, gains, gains_other), jnp.where(core == 0, gains_other, gains)], axis=1
    )
    attn_gain, mlp_gain = gains_all[:1], gains_all[1:]
    full_out = both_halves(w_out)
    full_in = both_halves(w_in)
    full_mlp = both_halves(w_mlp)
    upstream_other = swap_cores(upstream)
    blocks = gathered_blocks()
    positions = (blocks[:, None] * rows + jnp.arange(rows, dtype=jnp.int32)[None, :]).reshape(-1)
    cos, sin = rotary_tables(positions.astype(F32), 64)
    count = gathered[0].shape[0]
    (first_half, queries), (last_half,) = [
        project(
            part, full_qkv, attn_gain,
            cos[k * count : (k + 1) * count], sin[k * count : (k + 1) * count],
            0 if k else rows,
        )
        for k, part in enumerate(gathered)
    ]
    halves = first_half, last_half
    attended, log_total = attend(queries, halves)
    (
        layer_out, own_halves, other_halves, whole,
        grad_middle, grads, logs_deltas, gain_mlp_part,
    ) = middle_part(
        core.reshape(1), own, attended, log_total, upstream,
        full_out, full_in, full_mlp, mlp_gain,
    )

    def gain_pair(part):
        mine = lax.dynamic_slice_in_dim(part, core * half, half, 1)
        theirs = lax.dynamic_slice_in_dim(part, (1 - core) * half, half, 1)
        return [mine, swap_cores(theirs)]

    other_halves = swap_cores(other_halves)
    whole_other = swap_cores(whole)
    mlp_rows = grad_rows(
        width,
        pieces,
        [
            (
                own_halves, other_halves, slice(0, half_ff),
                upstream, upstream_other, slice(0, width),
            ),
            (
                own_halves, other_halves, slice(ATTENDED_AT, ATTENDED_AT + half),
                whole, whole_other, slice(2 * FF, 2 * FF + width),
            ),
        ],
        gain_pair(gain_mlp_part),
    )
    in_rows = grad_rows(
        width,
        pieces,
        [
            (
                own_halves, other_halves, slice(NORMED_AT, NORMED_AT + half),
                whole, whole_other, slice(0, 2 * FF),
            )
        ],
    )

    grad_q, grad_k, grad_v = attend_back(queries, halves, grads, logs_deltas, cos, sin)
    first_rows, qkv_own, qkv_other = back_project(
        core.reshape(1), pieces, gathered, grad_q, grad_k, grad_v, full_qkv, attn_gain
    )
    tokens_grad = last_part(own, grad_middle, scatter_context(first_rows), attn_gain)

    mlp_grad, out_grad, gain_mlp_grad = unpack([mlp_rows], [(half_ff, width), (half, width)], True)
    (in_grad,) = unpack([in_rows], [(half, 2 * FF)])
    qkv_grad, gain_attn_grad = unpack([qkv_own, swap_cores(qkv_other)], [(half, 3 * width)], True)
    return (
        layer_out.reshape(seqs_here, rows, width),
        tokens_grad.reshape(seqs_here, rows, width),
        qkv_grad,
        out_grad,
        in_grad,
        mlp_grad,
        gain_attn_grad.reshape(half),
        gain_mlp_grad.reshape(half),
    )


def solution(mesh):
    placed = (
        P(("seq", "wsh"), "ctx", None),
        P("wsh", None),
        P("wsh", None),
        P("wsh", None),
        P("wsh", None),
        P("wsh"),
        P("wsh"),
        P(("seq", "wsh"), "ctx", None),
    )
    return jax.shard_map(
        local,
        mesh=mesh,
        in_specs=placed,
        out_specs=(
            P(("seq", "wsh"), "ctx", None),
            P(("seq", "wsh"), "ctx", None),
            P("wsh", None),
            P("wsh", None),
            P("wsh", None),
            P("wsh", None),
            P("wsh"),
            P("wsh"),
        ),
        check_vma=False,
    )
```

```python
from functools import partial

import jax
import jax.numpy as jnp
from jax import lax
from jax.experimental import pallas as pl
from jax.experimental.pallas import tpu as pltpu
from jax.sharding import PartitionSpec as P

HEADS = 12
FF = 1152
EPSILON = 1e-05
THETA = 160000.0
LANES = 128
NORMED_AT = 640
ATTENDED_AT = 1024
HALVES_WIDTH = 1408
MLP_ORDERS = ("yaxb", "ybxa")
IN_ORDERS = ("xyba", "axyb")
LATE_ORDERS = ("xyab", "bxya")
MIB = 1 << 20
BF16 = jnp.bfloat16
F32 = jnp.float32


def bits_of(axis):
    return [(axis, k) for k in range((lax.axis_size(axis) - 1).bit_length())]


def my_bit(axis, k):
    return (lax.axis_index(axis) >> k) & 1


def flip(block, first, second):
    n_seq, n_ctx = lax.axis_size("seq"), lax.axis_size("ctx")
    route = []
    for s in range(n_seq):
        for t in range(n_ctx):
            for core, (axis, k) in enumerate((first, second)):
                s2, t2 = (s ^ (1 << k), t) if axis == "seq" else (s, t ^ (1 << k))
                route.append(((s * n_ctx + t) * 2 + core, (s2 * n_ctx + t2) * 2 + core))
    return lax.ppermute(block, ("seq", "ctx", "wsh"), route)


def swap_cores(block):
    return lax.ppermute(block, "wsh", [(0, 1), (1, 0)])


def gather_orders():
    bits = bits_of("ctx")
    return bits[::-1], bits[:1] + bits[:0:-1]


def gather_context(block):
    stages = list(zip(*gather_orders()))
    for first, second in stages[:-1]:
        block = jnp.concatenate([block, flip(block, first, second)], axis=0)
    return block, flip(block, *stages[-1])


class ContextSum:
    def __init__(self, rows):
        self.parts = [rows]
        self.stages = list(zip(*gather_orders()))[::-1]

    def step(self):
        half = self.parts[0].shape[0] // 2
        away, kept = (
            sum(part[at : at + half].astype(F32) for part in self.parts).astype(BF16)
            for at in (half, 0)
        )
        self.parts = [kept, flip(away, *self.stages.pop(0))]

    @property
    def left(self):
        return len(self.stages)


def gathered_blocks():
    tables = []
    for order in gather_orders():
        slots = [0]
        for _, k in order:
            slots = slots + [slot | (1 << k) for slot in slots]
        tables.append(slots)
    mine = jnp.where(lax.axis_index("wsh") == 0, jnp.array(tables[0]), jnp.array(tables[1]))
    return mine ^ lax.axis_index("ctx")


def sum_orders(orders):
    ctx = bits_of("ctx")
    bits = {"x": bits_of("seq"), "y": ctx[:1], "a": ctx[1:2], "b": ctx[2:]}
    return list(zip(*[sum((bits[letter] for letter in order), []) for order in orders]))


def stage_bit(first, second):
    return jnp.where(lax.axis_index("wsh") == 0, my_bit(*first), my_bit(*second))


def after(arrays, *made):
    return lax.optimization_barrier((*arrays, *made))[: len(arrays)]


class RowsSum:
    def __init__(self, parts, orders):
        self.parts = parts
        self.starts = [0] * len(parts)
        self.size = parts[0].shape[0]
        self.stages = sum_orders(orders)
        self.at = 0

    def summed(self, start, size):
        cut = [
            lax.dynamic_slice_in_dim(part, first + start, size, 0).astype(F32)
            for part, first in zip(self.parts, self.starts)
        ]
        return sum(cut[1:], cut[0]).astype(BF16)

    def first_away(self):
        return self.summed((1 - stage_bit(*self.stages[0])) * (self.size // 2), self.size // 2)

    def step(self, away=None):
        count, at = len(self.stages), self.at
        self.at += 1
        if at < count:
            stage = self.stages[at]
            bit = stage_bit(*stage)
            self.size //= 2
            if away is None:
                away = self.summed((1 - bit) * self.size, self.size)
            if at == 0:
                kept, starts = self.parts, [start + bit * self.size for start in self.starts]
            else:
                kept, starts = [self.summed(bit * self.size, self.size)], [0]
            self.parts = [*kept, flip(away, *stage)]
            self.starts = [*starts, 0]
            return
        stage = self.stages[2 * count - 1 - at]
        if at == count:
            rows = self.summed(0, self.size)
        else:
            own, other = self.parts
            low = jnp.where(self.bit == 0, own, other)
            high = jnp.where(self.bit == 0, other, own)
            rows = jnp.concatenate([low, high], axis=0)
        self.bit = stage_bit(*stage)
        self.parts = [rows, flip(rows, *stage)]

    @property
    def left(self):
        return 2 * len(self.stages) - self.at


def both_halves(block):
    other = swap_cores(block)
    core = lax.axis_index("wsh")
    return jnp.concatenate(
        [jnp.where(core == 0, block, other), jnp.where(core == 0, other, block)], axis=0
    )


def dot_nn(a, b):
    return lax.dot_general(a, b, (((1,), (0,)), ((), ())), preferred_element_type=F32)


def dot_nt(a, b):
    return lax.dot_general(a, b, (((1,), (1,)), ((), ())), preferred_element_type=F32)


def dot_tn(a, b):
    return lax.dot_general(a, b, (((0,), (0,)), ((), ())), preferred_element_type=F32)


SMEM_SPEC = pl.BlockSpec(memory_space=pltpu.SMEM)
WHOLE = pl.BlockSpec()


def cost(flops, moved):
    return pl.CostEstimate(flops=int(flops), bytes_accessed=int(moved), transcendentals=0)


def params(mib):
    return pltpu.CompilerParams(vmem_limit_bytes=mib * MIB)


def normalize(inputs):
    average = jnp.mean(inputs, axis=-1, keepdims=True)
    centred = inputs - average
    variance = jnp.mean(centred * centred, axis=-1, keepdims=True)
    rstd = lax.rsqrt(variance + EPSILON)
    return centred * rstd, rstd


def norm_back(grad_rows, normed, rstd, gain):
    scaled = grad_rows * gain
    inner = jnp.mean(scaled * normed, axis=-1, keepdims=True)
    return rstd * (scaled - jnp.mean(scaled, axis=-1, keepdims=True) - normed * inner)


def lane_of(shape):
    return lax.broadcasted_iota(jnp.int32, shape, len(shape) - 1)


def halves_swapped(vectors):
    first = (lane_of(vectors.shape) & 63) < 32
    return jnp.where(first, pltpu.roll(vectors, LANES - 32, 1), pltpu.roll(vectors, 32, 1))


def project_kernel(core, tokens, weights, other, gain, cos, sin, out, out_low, *more):
    width = tokens.shape[1]
    half = width // 2
    if more:
        queries, joined = more

        @pl.when(pl.program_id(0) == 0)
        def _():
            joined[pl.ds(pl.multiple_of(core[0] * half, half), half), :] = weights[...]
            joined[pl.ds(pl.multiple_of((1 - core[0]) * half, half), half), :] = other[...]

        weights = joined
    normed, _ = normalize(tokens[...].astype(F32))
    low = (normed * gain[...].astype(F32)).astype(BF16)
    out_low[...] = low

    def put(ref, start, rows, columns, turned, scale):
        for j in range(width // LANES):
            piece = columns[:, j * LANES : (j + 1) * LANES]
            if turned:
                piece = piece * cos[:rows, :] + halves_swapped(piece) * sin[:rows, :]
            ref[:, start + j * LANES : start + (j + 1) * LANES] = (piece * scale).astype(BF16)

    rows = tokens.shape[0]
    put(out, 0, rows, dot_nn(low, weights[:, width : 2 * width]), True, 1.0)
    put(out, width, rows, dot_nn(low, weights[:, 2 * width :]), False, 1.0)
    if more:

        @pl.when(pl.program_id(0) == 0)
        def _():
            own = queries.shape[0]
            put(queries, 0, own, dot_nn(low[:own], weights[:, :width]), True, 0.125)


def project(core, tokens, weights, other, gain, cos, sin, own_rows):
    rows, width = tokens.shape
    step = min(rows, 256)

    def fixed(shape):
        return pl.BlockSpec(shape, lambda i: (0, 0))

    out_specs = [
        pl.BlockSpec((step, 2 * width), lambda i: (i, 0)),
        pl.BlockSpec((step, width), lambda i: (i, 0)),
    ]
    out_shape = [
        jax.ShapeDtypeStruct((rows, 2 * width), BF16),
        jax.ShapeDtypeStruct((rows, width), BF16),
    ]
    if own_rows:
        out_specs += [fixed((own_rows, width)), fixed((width, 3 * width))]
        out_shape.append(jax.ShapeDtypeStruct((own_rows, width), BF16))
        out_shape.append(jax.ShapeDtypeStruct((width, 3 * width), BF16))
    return pl.pallas_call(
        project_kernel,
        grid=(rows // step,),
        in_specs=[
            SMEM_SPEC,
            pl.BlockSpec((step, width), lambda i: (i, 0)),
            fixed(weights.shape),
            fixed(other.shape),
            fixed((1, width)),
            pl.BlockSpec((step, LANES), lambda i: (i, 0)),
            pl.BlockSpec((step, LANES), lambda i: (i, 0)),
        ],
        out_specs=out_specs,
        out_shape=out_shape,
        compiler_params=params(28),
        cost_estimate=cost(4 * rows * width * width, 8 * rows * width),
        name="project",
    )(core, tokens, weights, other, gain, cos, sin)


def two_heads(block):
    first = lane_of(block.shape) < 64
    zero = jnp.zeros_like(block)
    return jnp.concatenate([jnp.where(first, block, zero), jnp.where(first, zero, block)], axis=0)


def one_pair(stacked):
    rows = stacked.shape[0] // 2
    return jnp.where(lane_of((rows, LANES)) < 64, stacked[:rows], stacked[rows:])


def column_pair(columns, at):
    lanes = lane_of(columns.shape)
    picked = [
        jnp.sum(jnp.where(lanes == at + k, columns, 0.0), axis=1, keepdims=True) for k in (0, 1)
    ]
    return jnp.concatenate(picked, axis=0)


def put_pair(ref, pair, values):
    rows = ref.shape[0]

    @pl.when(pair == 0)
    def _():
        ref[...] = jnp.zeros_like(ref)

    lanes = lane_of((rows, LANES))
    kept = jnp.where(lanes == 2 * pair, values[:rows], ref[...])
    ref[...] = jnp.where(lanes == 2 * pair + 1, values[rows:], kept)


def chunks_of(count):
    step = min(count, 1024)
    return [slice(at, at + step) for at in range(0, count, step)]


def attend_over(stacked, keys, values, peak, total, mixed):
    for at in chunks_of(keys.shape[0]):
        logits = dot_nt(stacked, keys[at, :])
        top = jnp.max(logits, axis=1, keepdims=True)
        if peak is None:
            weights = jnp.exp(logits - top)
            total = jnp.sum(weights, axis=1, keepdims=True)
            mixed = dot_nn(weights.astype(BF16), values[at, :])
        else:
            top = jnp.maximum(peak, top)
            weights = jnp.exp(logits - top)
            factor = jnp.exp(peak - top)
            total = total * factor + jnp.sum(weights, axis=1, keepdims=True)
            mixed = mixed * factor + dot_nn(weights.astype(BF16), values[at, :])
        peak = top
    return peak, total, mixed


def attend_first_kernel(queries, keys, values, out_mixed, out_peak, out_total):
    pair = pl.program_id(0)
    stacked = two_heads(queries[...])
    peak, total, mixed = attend_over(stacked, keys, values, None, None, None)
    out_mixed[...] = one_pair(mixed)
    put_pair(out_peak, pair, peak)
    put_pair(out_total, pair, total)


def attend_last_kernel(
    queries, keys, values, in_mixed, in_peak, in_total, attended, log_total
):
    pair = pl.program_id(0)
    stacked = two_heads(queries[...])
    peak = column_pair(in_peak[...], 2 * pair)
    total = column_pair(in_total[...], 2 * pair)
    mixed = jnp.concatenate([in_mixed[...]] * 2, axis=0)
    peak, total, mixed = attend_over(stacked, keys, values, peak, total, mixed)
    attended[...] = one_pair(mixed / total)
    put_pair(log_total, pair, peak + jnp.log(total))


def attend(own_queries, halves):
    count = halves[0].shape[0]
    rows, width = own_queries.shape
    pairs = width // LANES
    queries = pl.BlockSpec((rows, LANES), lambda j: (0, j))
    shared = pl.BlockSpec((rows, LANES), lambda j: (0, 0))
    keys = pl.BlockSpec((count, LANES), lambda j: (0, j))
    values = pl.BlockSpec((count, LANES), lambda j: (0, pairs + j))
    wide = jax.ShapeDtypeStruct((rows, width), F32)
    thin = jax.ShapeDtypeStruct((rows, LANES), F32)
    work = cost(8 * rows * count * width, 6 * count * width)
    mixed, peak, total = pl.pallas_call(
        attend_first_kernel,
        grid=(pairs,),
        in_specs=[queries, keys, values],
        out_specs=[queries, shared, shared],
        out_shape=[wide, thin, thin],
        compiler_params=params(24),
        cost_estimate=work,
        name="attend_first",
    )(own_queries, halves[0], halves[0])
    return pl.pallas_call(
        attend_last_kernel,
        grid=(pairs,),
        in_specs=[queries, keys, values, queries, shared, shared],
        out_specs=[queries, shared],
        out_shape=[wide, thin],
        compiler_params=params(24),
        cost_estimate=work,
        name="attend_last",
    )(own_queries, halves[1], halves[1], mixed, peak, total)


def middle_kernel(
    core, tokens, attended, log_total, cotangent, w_out, w_in, w_mlp, gain,
    layer_out, own_halves, other_halves, whole, grad_middle, grads, logs_deltas,
):

    rows, width = tokens.shape
    first = core[0] == 0

    def put_halves(at, block):
        half = block.shape[1] // 2
        left, right = block[:, :half], block[:, half:]
        own_halves[:, at : at + half] = jnp.where(first, left, right)
        other_halves[:, at : at + half] = jnp.where(first, right, left)

    mixed = attended[...]
    mixed_low = mixed.astype(BF16)
    put_halves(ATTENDED_AT, mixed_low)
    middle = tokens[...].astype(F32) + dot_nn(mixed_low, w_out[...])
    normed, rstd = normalize(middle)
    gain_row = gain[...].astype(F32)
    second = (normed * gain_row).astype(BF16)
    put_halves(NORMED_AT, second)
    gate = dot_nn(second, w_in[:, :FF])
    up = dot_nn(second, w_in[:, FF:])
    cdf = 0.5 * (1.0 + lax.erf(gate * (0.5**0.5)))
    activated = gate * cdf
    hidden = (activated * up).astype(BF16)
    put_halves(0, hidden)
    layer_out[...] = (middle + dot_nn(hidden, w_mlp[...])).astype(BF16)
    upstream = cotangent[...]
    grad_hidden = dot_nt(upstream, w_mlp[...]).astype(BF16).astype(F32)
    density = jnp.exp(-0.5 * gate * gate) * 0.3989422804014327
    grad_gate = (grad_hidden * up * (cdf + gate * density)).astype(BF16)
    grad_up = (grad_hidden * activated).astype(BF16)
    whole[:, :FF] = grad_gate
    whole[:, FF : 2 * FF] = grad_up
    grad_second = dot_nt(grad_gate, w_in[:, :FF]) + dot_nt(grad_up, w_in[:, FF:])
    grad_mid = upstream.astype(F32) + norm_back(grad_second, normed, rstd, gain_row)
    grad_middle[...] = grad_mid
    branch = grad_mid.astype(BF16)
    whole[:, 2 * FF :] = branch
    grad_attended = dot_nt(branch, w_out[...]).astype(BF16)
    grads[...] = grad_attended
    products = grad_attended.astype(F32) * mixed
    head = lax.broadcasted_iota(jnp.int32, (width, LANES), 0) // 64
    to_lane = (lane_of((width, LANES)) == head + HEADS).astype(F32)
    both = log_total[...] + lax.dot_general(
        products,
        to_lane,
        (((1,), (0,)), ((), ())),
        precision=lax.Precision.HIGHEST,
        preferred_element_type=F32,
    )
    logs_deltas[...] = both.T


def middle_part(core, tokens, attended, log_total, cotangent, w_out, w_in, w_mlp, gain):
    rows, width = tokens.shape
    wide, halves = (rows, width), (rows, HALVES_WIDTH)
    shapes = [
        (wide, BF16), (halves, BF16), (halves, BF16), ((rows, 2 * FF + width), BF16),
        (wide, F32), (wide, BF16), ((LANES, rows), F32),
    ]
    return pl.pallas_call(
        middle_kernel,
        in_specs=[SMEM_SPEC] + [WHOLE] * 8,
        out_shape=[jax.ShapeDtypeStruct(*shape) for shape in shapes],
        compiler_params=params(32),
        cost_estimate=cost(4 * rows * width * (2 * width + 6 * FF), 24 * MIB),
        name="middle",
    )(core, tokens, attended, log_total, cotangent, w_out, w_in, w_mlp, gain)


def rows_kernel(own, other, upstream, upstream_other, whole, whole_other, out_mlp, out_in):
    width = out_mlp.shape[1]
    half, half_ff = width // 2, FF // 2
    both = jnp.concatenate([own[...], other[...]], axis=0)
    right = jnp.concatenate([upstream[...], upstream_other[...]], axis=0)
    out_mlp[:half_ff, :] = dot_tn(both[:, :half_ff], right).astype(BF16)
    branch = jnp.concatenate([whole[:, 2 * FF :], whole_other[:, 2 * FF :]], axis=0)
    left = both[:, ATTENDED_AT : ATTENDED_AT + half]
    out_mlp[half_ff : half_ff + half, :] = dot_tn(left, branch).astype(BF16)
    turned = both[:, NORMED_AT : NORMED_AT + half].T
    for k in range(2 * FF // width):
        lanes = slice(k * width, (k + 1) * width)
        right = jnp.concatenate([whole[:, lanes], whole_other[:, lanes]], axis=0)
        out_in[k * half : (k + 1) * half, :] = dot_nn(turned, right).astype(BF16)
    for out, used in ((out_mlp, half_ff + half), (out_in, 2 * FF // width * half)):
        if used < out.shape[0]:
            out[used:, :] = jnp.zeros((out.shape[0] - used, width), BF16)


def padded(rows, pieces):
    unit = 8 * pieces
    return (rows + unit - 1) // unit * unit


def grad_rows(pieces, width, *arrays):
    sizes = padded((FF + width) // 2, pieces), padded(FF, pieces)
    return pl.pallas_call(
        rows_kernel,
        out_shape=[jax.ShapeDtypeStruct((size, width), BF16) for size in sizes],
        compiler_params=params(16),
        cost_estimate=cost(512 * 1728 * width, 12 * MIB),
        name="grad_rows",
    )(*arrays)


def unpack_kernel(places, gained, bit, own, other, *refs):
    half = own.shape[0]
    if gained:
        weights, gain = refs[:2]
    outs = refs[2:] if gained else refs

    def put(low, high):
        at = 0
        for out, blocks in places:
            ref = outs[out]
            made = ref.shape[0]
            for k in range(blocks):
                columns = slice(k * low.shape[1], (k + 1) * low.shape[1])
                cut = min(max(half - at, 0), made)
                if cut > 0:
                    ref[:cut, columns] = low[at : at + cut, :].astype(F32)
                if cut < made:
                    start = at + cut - half
                    ref[cut:, columns] = high[start : start + made - cut, :].astype(F32)
                at += made

    @pl.when(bit[0] == 0)
    def _():
        put(own, other)

    @pl.when(bit[0] != 0)
    def _():
        put(other, own)

    if gained:
        products = outs[0][...] * weights[...].astype(F32)
        sums = jnp.sum(products, axis=1, keepdims=True)
        row = jnp.broadcast_to(sums, (sums.shape[0], LANES)).T[:1]
        outs[-1][...] = (row / gain[...].astype(F32)).reshape(outs[-1].shape)


def unpack(chain, shapes, gained=()):
    own, other = chain.parts
    width = own.shape[1]
    places = [(k, shape[1] // width) for k, shape in enumerate(shapes)]
    if gained:
        shapes = shapes + [gained[1].shape[1:]]
    return pl.pallas_call(
        partial(unpack_kernel, places, bool(gained)),
        in_specs=[SMEM_SPEC] + [WHOLE] * (2 + len(gained)),
        out_shape=[jax.ShapeDtypeStruct(shape, F32) for shape in shapes],
        compiler_params=params(24),
        cost_estimate=cost(0, 12 * own.size),
        name="unpack",
    )(chain.bit.reshape(1), own, other, *gained)


def unrotated(block, cos, sin):
    return block * cos - halves_swapped(block) * sin


def row_pair(rows, at):
    index = lax.broadcasted_iota(jnp.int32, rows.shape, 0)
    picked = [
        jnp.sum(jnp.where(index == at + k, rows, 0.0), axis=0, keepdims=True) for k in (0, 1)
    ]
    return jnp.concatenate(picked, axis=1)


def attend_back_kernel(
    queries, keys_a, values_a, keys_b, values_b, grads, logs_deltas, cos, sin,
    out_queries, out_keys, out_values,
):
    pair = pl.program_id(0)
    rows, count = queries.shape[0], keys_a.shape[0]
    queries_two = two_heads(queries[...])
    grads_two = two_heads(grads[...])
    logs = row_pair(logs_deltas[...], 2 * pair)
    deltas = row_pair(logs_deltas[...], HEADS + 2 * pair)
    total = jnp.zeros((2 * rows, LANES), F32)
    for base, keys, values in ((0, keys_a, values_a), (count, keys_b, values_b)):
        for at in chunks_of(count):
            to = slice(base + at.start, base + at.stop)
            key_rows = keys[at, :]
            probs = jnp.exp(dot_nt(key_rows, queries_two) - logs)
            grad_probs = dot_nt(values[at, :], grads_two)
            grad_scores = (probs * (grad_probs - deltas)).astype(BF16)
            out_values[to, :] = dot_nn(probs.astype(BF16), grads_two).astype(BF16)
            grad_keys = dot_nn(grad_scores, queries_two)
            out_keys[to, :] = unrotated(grad_keys, cos[to, :], sin[to, :]).astype(BF16)
            total = total + dot_tn(grad_scores, key_rows)
    grad = one_pair(total) * 0.125
    out_queries[...] = unrotated(grad, cos[:rows, :], sin[:rows, :]).astype(BF16)


def attend_back(own_queries, halves, grads, logs_deltas, cos, sin):
    count = halves[0].shape[0]
    rows, width = own_queries.shape
    pairs = width // LANES
    queries = pl.BlockSpec((rows, LANES), lambda j: (0, j))
    shared = pl.BlockSpec((LANES, rows), lambda j: (0, 0))
    keys = pl.BlockSpec((count, LANES), lambda j: (0, j))
    values = pl.BlockSpec((count, LANES), lambda j: (0, pairs + j))
    table = pl.BlockSpec((2 * count, LANES), lambda j: (0, 0))
    made = pl.BlockSpec((2 * count, LANES), lambda j: (0, j))
    return pl.pallas_call(
        attend_back_kernel,
        grid=(pairs,),
        in_specs=[queries, keys, values, keys, values, queries, shared, table, table],
        out_specs=[queries, made, made],
        out_shape=[
            jax.ShapeDtypeStruct((rows, width), BF16),
            jax.ShapeDtypeStruct((2 * count, width), BF16),
            jax.ShapeDtypeStruct((2 * count, width), BF16),
        ],
        compiler_params=params(16 if count <= 1024 else 48),
        cost_estimate=cost(40 * rows * count * width, 20 * count * width),
        name="attend_back",
    )(
        own_queries, halves[0], halves[0], halves[1], halves[1],
        grads, logs_deltas, cos, sin,
    )


def late_rows_kernel(
    core, low_a, low_b, grad_q, grad_k, grad_v, out_own, out_other, total
):
    step, steps = pl.program_id(0), pl.num_programs(0)
    own_rows, width = grad_q.shape
    half = width // 2
    low = jnp.where(2 * step < steps, low_a[...], low_b[...])
    turned = low.T
    made_k, made_v = dot_nn(turned, grad_k[...]), dot_nn(turned, grad_v[...])

    @pl.when(step == 0)
    def _():
        total[:, :width] = dot_nn(turned[:, :own_rows], grad_q[...])
        total[:, width : 2 * width] = made_k
        total[:, 2 * width :] = made_v

    @pl.when(step > 0)
    def _():
        total[:, width : 2 * width] += made_k
        total[:, 2 * width :] += made_v

    @pl.when(step == steps - 1)
    def _():
        for out, side in ((out_own, core[0]), (out_other, 1 - core[0])):
            start = pl.multiple_of(side * half, half)
            for k in range(3):
                columns = slice(k * width, (k + 1) * width)
                out[k * half : (k + 1) * half, :] = total[pl.ds(start, half), columns].astype(BF16)
            if out.shape[0] > 3 * half:
                out[3 * half :, :] = jnp.zeros((out.shape[0] - 3 * half, width), BF16)


def late_rows(core, pieces, lows, grad_q, grad_k, grad_v):
    count, width = lows[0].shape
    own_rows = grad_q.shape[0]
    step = min(count, 512)
    each = count // step
    total = padded(3 * width // 2, pieces)
    grads = pl.BlockSpec((step, width), lambda i: (i, 0))
    fixed = pl.BlockSpec((own_rows, width), lambda i: (0, 0))
    made = pl.BlockSpec((total, width), lambda i: (0, 0))
    return pl.pallas_call(
        late_rows_kernel,
        grid=(2 * each,),
        in_specs=[
            SMEM_SPEC,
            pl.BlockSpec((step, width), lambda i: (jnp.minimum(i, each - 1), 0)),
            pl.BlockSpec((step, width), lambda i: (jnp.maximum(i - each, 0), 0)),
            fixed, grads, grads,
        ],
        out_specs=[made, made],
        out_shape=[jax.ShapeDtypeStruct((total, width), BF16)] * 2,
        scratch_shapes=[pltpu.VMEM((width, 3 * width), F32)],
        compiler_params=params(36),
        cost_estimate=cost(4 * count * width * width, 8 * count * width),
        name="late_rows",
    )(core, *lows, grad_q, grad_k, grad_v)


def first_rows_kernel(grad_q, grad_k, grad_v, weights, out):
    width = grad_q.shape[1]
    own_rows = grad_q.shape[0]
    made = dot_nt(grad_k[...], weights[:, width : 2 * width])
    made = made + dot_nt(grad_v[...], weights[:, 2 * width :])

    @pl.when(pl.program_id(0) == 0)
    def _():
        own = made[:own_rows] + dot_nt(grad_q[...], weights[:, :width])
        out[:own_rows, :] = own.astype(BF16)
        out[own_rows:, :] = made[own_rows:].astype(BF16)

    @pl.when(pl.program_id(0) > 0)
    def _():
        out[...] = made.astype(BF16)


def first_rows(grad_q, grad_k, grad_v, weights):
    rows, width = grad_k.shape
    own_rows = grad_q.shape[0]
    step = min(rows, 2 * own_rows)
    block = pl.BlockSpec((step, width), lambda i: (i, 0))
    return pl.pallas_call(
        first_rows_kernel,
        grid=(rows // step,),
        in_specs=[
            pl.BlockSpec((own_rows, width), lambda i: (0, 0)),
            block,
            block,
            pl.BlockSpec((width, 3 * width), lambda i: (0, 0)),
        ],
        out_specs=block,
        out_shape=jax.ShapeDtypeStruct((rows, width), BF16),
        compiler_params=params(16),
        cost_estimate=cost(4 * rows * width * width, 8 * rows * width),
        name="first_rows",
    )(grad_q, grad_k, grad_v, weights)


def last_kernel(tokens, grad_middle, part_a, part_b, gain, out):
    normed, rstd = normalize(tokens[...].astype(F32))
    grad_first = part_a[...].astype(F32) + part_b[...].astype(F32)
    back = norm_back(grad_first, normed, rstd, gain[...].astype(F32))
    out[...] = (grad_middle[...] + back).astype(BF16)


def last_part(tokens, grad_middle, parts, gain):
    return pl.pallas_call(
        last_kernel,
        out_shape=jax.ShapeDtypeStruct(tokens.shape, BF16),
        compiler_params=params(24),
        cost_estimate=cost(20 * tokens.size, 12 * tokens.size),
        name="last",
    )(tokens, grad_middle, *parts, gain)


def rotary_tables(positions, head_dim):
    half = head_dim // 2
    inverse = jnp.power(F32(THETA), -(jnp.arange(half, dtype=F32) * (2.0 / head_dim)))
    angles = positions[:, None] * inverse[None, :]
    cos, sin = jnp.cos(angles), jnp.sin(angles)
    return (
        jnp.concatenate([cos, cos, cos, cos], axis=1),
        jnp.concatenate([-sin, sin, -sin, sin], axis=1),
    )


def local(tokens, w_qkv, w_out, w_in, w_mlp, gain_attn, gain_mlp, cotangent):
    seqs_here, rows, width = tokens.shape
    half, half_ff = width // 2, FF // 2
    core = lax.axis_index("wsh")
    own = tokens.reshape(rows, width)
    upstream = cotangent.reshape(rows, width)
    pieces = lax.axis_size("seq") * lax.axis_size("ctx")

    gathered = gather_context(own)
    qkv_other = swap_cores(w_qkv)
    gains = jnp.stack([gain_attn, gain_mlp])
    gains_other = swap_cores(gains)
    gains_all = jnp.concatenate(
        [jnp.where(core == 0, gains, gains_other), jnp.where(core == 0, gains_other, gains)], axis=1
    )
    attn_gain, mlp_gain = gains_all[:1], gains_all[1:]
    full_out = both_halves(w_out)
    full_in = both_halves(w_in)
    full_mlp = both_halves(w_mlp)
    upstream_other = swap_cores(upstream)

    blocks = gathered_blocks()
    positions = (blocks[:, None] * rows + jnp.arange(rows, dtype=jnp.int32)[None, :]).reshape(-1)
    cos, sin = rotary_tables(positions.astype(F32), 64)
    count = gathered[0].shape[0]
    core_at = core.reshape(1)
    first_half, first_low, queries, full_qkv = project(
        core_at, gathered[0], w_qkv, qkv_other, attn_gain, cos[:count], sin[:count], rows
    )
    last_half, last_low = project(
        core_at, gathered[1], full_qkv, attn_gain, attn_gain, cos[count:], sin[count:], 0
    )
    halves = first_half, last_half
    attended, log_total = attend(queries, halves)
    (
        layer_out, own_halves, other_halves, whole, grad_middle, grads, logs_deltas,
    ) = middle_part(
        core_at, own, attended, log_total, upstream, full_out, full_in, full_mlp, mlp_gain
    )

    grad_q, grad_k, grad_v = attend_back(queries, halves, grads, logs_deltas, cos, sin)
    other_halves, whole_other = swap_cores(other_halves), swap_cores(whole)
    own_halves, grad_q = lax.optimization_barrier((own_halves, grad_q))
    mlp_rows, in_rows = grad_rows(
        pieces, width, own_halves, other_halves, upstream, upstream_other,
        whole, whole_other,
    )
    (grad_q,) = after([grad_q], mlp_rows, in_rows)
    late_own, late_other = late_rows(
        core_at, pieces, (first_low, last_low), grad_q, grad_k, grad_v
    )
    chains = [
        RowsSum([mlp_rows], MLP_ORDERS),
        RowsSum([in_rows], IN_ORDERS),
        RowsSum([late_own, swap_cores(late_other)], LATE_ORDERS),
    ]
    aways = lax.optimization_barrier(tuple(chain.first_away() for chain in chains))
    for chain, away in zip(chains, aways):
        chain.step(away)
    (grad_q,) = after([grad_q], *aways)
    chains.append(ContextSum(first_rows(grad_q, grad_k, grad_v, full_qkv)))
    while any(chain.left for chain in chains):
        for chain in chains:
            if chain.left:
                chain.step()
    mlp_grad, out_grad = unpack(chains[0], [(half_ff, width), (half, width)])
    in_grad, gain_mlp_grad = unpack(
        chains[1], [(half, 2 * FF)], (w_in, gain_mlp.reshape(1, half))
    )
    qkv_grad, gain_attn_grad = unpack(
        chains[2], [(half, 3 * width)], (w_qkv, gain_attn.reshape(1, half))
    )
    tokens_grad = last_part(own, grad_middle, chains[3].parts, attn_gain)
    return (
        layer_out.reshape(seqs_here, rows, width),
        tokens_grad.reshape(seqs_here, rows, width),
        qkv_grad,
        out_grad,
        in_grad,
        mlp_grad,
        gain_attn_grad,
        gain_mlp_grad,
    )


def solution(mesh):
    placed = (
        P(("seq", "wsh"), "ctx", None),
        P("wsh", None),
        P("wsh", None),
        P("wsh", None),
        P("wsh", None),
        P("wsh"),
        P("wsh"),
        P(("seq", "wsh"), "ctx", None),
    )
    return jax.shard_map(
        local,
        mesh=mesh,
        in_specs=placed,
        out_specs=(
            P(("seq", "wsh"), "ctx", None),
            P(("seq", "wsh"), "ctx", None),
            P("wsh", None),
            P("wsh", None),
            P("wsh", None),
            P("wsh", None),
            P("wsh"),
            P("wsh"),
        ),
        check_vma=False,
    )
```

```python
from functools import partial

import jax
import jax.numpy as jnp
from jax import lax
from jax.experimental import pallas as pl
from jax.experimental.pallas import tpu as pltpu
from jax.sharding import PartitionSpec as P

HEADS = 12
FF = 1152
EPSILON = 1e-05
THETA = 160000.0
LANES = 128
NORMED_AT = 640
ATTENDED_AT = 1024
HALVES_WIDTH = 1408
MLP_ORDERS = ("axyb", "byxa")
IN_ORDERS = ("xyab", "yxba")
LATE_ORDERS = ("xayb", "ybxa")
MIB = 1 << 20
BF16 = jnp.bfloat16
F32 = jnp.float32


def bits_of(axis):
    return [(axis, k) for k in range((lax.axis_size(axis) - 1).bit_length())]


def my_bit(axis, k):
    return (lax.axis_index(axis) >> k) & 1


def flip(block, first, second):
    n_seq, n_ctx = lax.axis_size("seq"), lax.axis_size("ctx")
    route = []
    for s in range(n_seq):
        for t in range(n_ctx):
            for core, (axis, k) in enumerate((first, second)):
                s2, t2 = (s ^ (1 << k), t) if axis == "seq" else (s, t ^ (1 << k))
                route.append(((s * n_ctx + t) * 2 + core, (s2 * n_ctx + t2) * 2 + core))
    return lax.ppermute(block, ("seq", "ctx", "wsh"), route)


def swap_cores(block):
    return lax.ppermute(block, "wsh", [(0, 1), (1, 0)])


def gather_orders():
    bits = bits_of("ctx")
    return bits[::-1], bits[:1] + bits[:0:-1]


def gather_context(block):
    stages = list(zip(*gather_orders()))
    for first, second in stages[:-1]:
        block = jnp.concatenate([block, flip(block, first, second)], axis=0)
    return block, flip(block, *stages[-1])


class ContextSum:
    def __init__(self, rows):
        self.parts = [rows]
        self.stages = list(zip(*gather_orders()))[::-1]

    def step(self):
        half = self.parts[0].shape[0] // 2
        away, kept = (
            sum(part[at : at + half].astype(F32) for part in self.parts).astype(BF16)
            for at in (half, 0)
        )
        self.parts = [kept, flip(away, *self.stages.pop(0))]

    @property
    def left(self):
        return len(self.stages)


def gathered_blocks():
    tables = []
    for order in gather_orders():
        slots = [0]
        for _, k in order:
            slots = slots + [slot | (1 << k) for slot in slots]
        tables.append(slots)
    mine = jnp.where(lax.axis_index("wsh") == 0, jnp.array(tables[0]), jnp.array(tables[1]))
    return mine ^ lax.axis_index("ctx")


def sum_orders(orders):
    ctx = bits_of("ctx")
    bits = {"x": bits_of("seq"), "y": ctx[:1], "a": ctx[1:2], "b": ctx[2:]}
    return list(zip(*[sum((bits[letter] for letter in order), []) for order in orders]))


def stage_bit(first, second):
    return jnp.where(lax.axis_index("wsh") == 0, my_bit(*first), my_bit(*second))


def after(arrays, *made):
    return lax.optimization_barrier((*arrays, *made))[: len(arrays)]


class RowsSum:
    def __init__(self, parts, orders):
        self.parts = parts
        self.starts = [0] * len(parts)
        self.size = parts[0].shape[0]
        self.stages = sum_orders(orders)
        self.at = 0

    def summed(self, start, size):
        cut = [
            lax.dynamic_slice_in_dim(part, first + start, size, 0).astype(F32)
            for part, first in zip(self.parts, self.starts)
        ]
        return sum(cut[1:], cut[0]).astype(BF16)

    def first_away(self):
        return self.summed((1 - stage_bit(*self.stages[0])) * (self.size // 2), self.size // 2)

    def step(self, away=None):
        count, at = len(self.stages), self.at
        self.at += 1
        if at < count:
            stage = self.stages[at]
            bit = stage_bit(*stage)
            self.size //= 2
            if away is None:
                away = self.summed((1 - bit) * self.size, self.size)
            if at == 0:
                kept, starts = self.parts, [start + bit * self.size for start in self.starts]
            else:
                kept, starts = [self.summed(bit * self.size, self.size)], [0]
            self.parts = [*kept, flip(away, *stage)]
            self.starts = [*starts, 0]
            return
        stage = self.stages[2 * count - 1 - at]
        if at == count:
            rows = self.summed(0, self.size)
        else:
            own, other = self.parts
            low = jnp.where(self.bit == 0, own, other)
            high = jnp.where(self.bit == 0, other, own)
            rows = jnp.concatenate([low, high], axis=0)
        self.bit = stage_bit(*stage)
        self.parts = [rows, flip(rows, *stage)]

    @property
    def left(self):
        return 2 * len(self.stages) - self.at


def both_halves(block):
    other = swap_cores(block)
    core = lax.axis_index("wsh")
    return jnp.concatenate(
        [jnp.where(core == 0, block, other), jnp.where(core == 0, other, block)], axis=0
    )


def dot_nn(a, b):
    return lax.dot_general(a, b, (((1,), (0,)), ((), ())), preferred_element_type=F32)


def dot_nt(a, b):
    return lax.dot_general(a, b, (((1,), (1,)), ((), ())), preferred_element_type=F32)


def dot_tn(a, b):
    return lax.dot_general(a, b, (((0,), (0,)), ((), ())), preferred_element_type=F32)


SMEM_SPEC = pl.BlockSpec(memory_space=pltpu.SMEM)
WHOLE = pl.BlockSpec()


def cost(flops, moved):
    return pl.CostEstimate(flops=int(flops), bytes_accessed=int(moved), transcendentals=0)


def params(mib):
    return pltpu.CompilerParams(vmem_limit_bytes=mib * MIB)


def normalize(inputs):
    average = jnp.mean(inputs, axis=-1, keepdims=True)
    centred = inputs - average
    variance = jnp.mean(centred * centred, axis=-1, keepdims=True)
    rstd = lax.rsqrt(variance + EPSILON)
    return centred * rstd, rstd


def norm_back(grad_rows, normed, rstd, gain):
    scaled = grad_rows * gain
    inner = jnp.mean(scaled * normed, axis=-1, keepdims=True)
    return rstd * (scaled - jnp.mean(scaled, axis=-1, keepdims=True) - normed * inner)


def lane_of(shape):
    return lax.broadcasted_iota(jnp.int32, shape, len(shape) - 1)


def halves_swapped(vectors):
    first = (lane_of(vectors.shape) & 63) < 32
    return jnp.where(first, pltpu.roll(vectors, LANES - 32, 1), pltpu.roll(vectors, 32, 1))


def project_kernel(core, tokens, weights, other, gain, cos, sin, out, out_low, *more):
    width = tokens.shape[1]
    half = width // 2
    if more:
        queries, joined = more

        @pl.when(pl.program_id(0) == 0)
        def _():
            joined[pl.ds(pl.multiple_of(core[0] * half, half), half), :] = weights[...]
            joined[pl.ds(pl.multiple_of((1 - core[0]) * half, half), half), :] = other[...]

        weights = joined
    normed, _ = normalize(tokens[...].astype(F32))
    low = (normed * gain[...].astype(F32)).astype(BF16)
    out_low[...] = low

    def put(ref, start, rows, columns, turned, scale):
        for j in range(width // LANES):
            piece = columns[:, j * LANES : (j + 1) * LANES]
            if turned:
                piece = piece * cos[:rows, :] + halves_swapped(piece) * sin[:rows, :]
            ref[:, start + j * LANES : start + (j + 1) * LANES] = (piece * scale).astype(BF16)

    rows = tokens.shape[0]
    put(out, 0, rows, dot_nn(low, weights[:, width : 2 * width]), True, 1.0)
    put(out, width, rows, dot_nn(low, weights[:, 2 * width :]), False, 1.0)
    if more:

        @pl.when(pl.program_id(0) == 0)
        def _():
            own = queries.shape[0]
            put(queries, 0, own, dot_nn(low[:own], weights[:, :width]), True, 0.125)


def project(core, tokens, weights, other, gain, cos, sin, own_rows):
    rows, width = tokens.shape
    step = min(rows, 256)

    def fixed(shape):
        return pl.BlockSpec(shape, lambda i: (0, 0))

    out_specs = [
        pl.BlockSpec((step, 2 * width), lambda i: (i, 0)),
        pl.BlockSpec((step, width), lambda i: (i, 0)),
    ]
    out_shape = [
        jax.ShapeDtypeStruct((rows, 2 * width), BF16),
        jax.ShapeDtypeStruct((rows, width), BF16),
    ]
    if own_rows:
        out_specs += [fixed((own_rows, width)), fixed((width, 3 * width))]
        out_shape.append(jax.ShapeDtypeStruct((own_rows, width), BF16))
        out_shape.append(jax.ShapeDtypeStruct((width, 3 * width), BF16))
    return pl.pallas_call(
        project_kernel,
        grid=(rows // step,),
        in_specs=[
            SMEM_SPEC,
            pl.BlockSpec((step, width), lambda i: (i, 0)),
            fixed(weights.shape),
            fixed(other.shape),
            fixed((1, width)),
            pl.BlockSpec((step, LANES), lambda i: (i, 0)),
            pl.BlockSpec((step, LANES), lambda i: (i, 0)),
        ],
        out_specs=out_specs,
        out_shape=out_shape,
        compiler_params=params(28),
        cost_estimate=cost(4 * rows * width * width, 8 * rows * width),
        name="project",
    )(core, tokens, weights, other, gain, cos, sin)


def two_heads(block):
    first = lane_of(block.shape) < 64
    zero = jnp.zeros_like(block)
    return jnp.concatenate([jnp.where(first, block, zero), jnp.where(first, zero, block)], axis=0)


def one_pair(stacked):
    rows = stacked.shape[0] // 2
    return jnp.where(lane_of((rows, LANES)) < 64, stacked[:rows], stacked[rows:])


def column_pair(columns, at):
    lanes = lane_of(columns.shape)
    picked = [
        jnp.sum(jnp.where(lanes == at + k, columns, 0.0), axis=1, keepdims=True) for k in (0, 1)
    ]
    return jnp.concatenate(picked, axis=0)


def put_pair(ref, pair, values):
    rows = ref.shape[0]

    @pl.when(pair == 0)
    def _():
        ref[...] = jnp.zeros_like(ref)

    lanes = lane_of((rows, LANES))
    kept = jnp.where(lanes == 2 * pair, values[:rows], ref[...])
    ref[...] = jnp.where(lanes == 2 * pair + 1, values[rows:], kept)


def chunks_of(count):
    step = min(count, 1024)
    return [slice(at, at + step) for at in range(0, count, step)]


def attend_over(stacked, keys, values, peak, total, mixed):
    for at in chunks_of(keys.shape[0]):
        logits = dot_nt(stacked, keys[at, :])
        top = jnp.max(logits, axis=1, keepdims=True)
        if peak is None:
            weights = jnp.exp(logits - top)
            total = jnp.sum(weights, axis=1, keepdims=True)
            mixed = dot_nn(weights.astype(BF16), values[at, :])
        else:
            top = jnp.maximum(peak, top)
            weights = jnp.exp(logits - top)
            factor = jnp.exp(peak - top)
            total = total * factor + jnp.sum(weights, axis=1, keepdims=True)
            mixed = mixed * factor + dot_nn(weights.astype(BF16), values[at, :])
        peak = top
    return peak, total, mixed


def attend_first_kernel(queries, keys, values, out_mixed, out_peak, out_total):
    pair = pl.program_id(0)
    stacked = two_heads(queries[...])
    peak, total, mixed = attend_over(stacked, keys, values, None, None, None)
    out_mixed[...] = one_pair(mixed)
    put_pair(out_peak, pair, peak)
    put_pair(out_total, pair, total)


def attend_last_kernel(
    queries, keys, values, in_mixed, in_peak, in_total, attended, log_total
):
    pair = pl.program_id(0)
    stacked = two_heads(queries[...])
    peak = column_pair(in_peak[...], 2 * pair)
    total = column_pair(in_total[...], 2 * pair)
    mixed = jnp.concatenate([in_mixed[...]] * 2, axis=0)
    peak, total, mixed = attend_over(stacked, keys, values, peak, total, mixed)
    attended[...] = one_pair(mixed / total)
    put_pair(log_total, pair, peak + jnp.log(total))


def attend(own_queries, halves):
    count = halves[0].shape[0]
    rows, width = own_queries.shape
    pairs = width // LANES
    queries = pl.BlockSpec((rows, LANES), lambda j: (0, j))
    shared = pl.BlockSpec((rows, LANES), lambda j: (0, 0))
    keys = pl.BlockSpec((count, LANES), lambda j: (0, j))
    values = pl.BlockSpec((count, LANES), lambda j: (0, pairs + j))
    wide = jax.ShapeDtypeStruct((rows, width), F32)
    thin = jax.ShapeDtypeStruct((rows, LANES), F32)
    work = cost(8 * rows * count * width, 6 * count * width)
    mixed, peak, total = pl.pallas_call(
        attend_first_kernel,
        grid=(pairs,),
        in_specs=[queries, keys, values],
        out_specs=[queries, shared, shared],
        out_shape=[wide, thin, thin],
        compiler_params=params(24),
        cost_estimate=work,
        name="attend_first",
    )(own_queries, halves[0], halves[0])
    return pl.pallas_call(
        attend_last_kernel,
        grid=(pairs,),
        in_specs=[queries, keys, values, queries, shared, shared],
        out_specs=[queries, shared],
        out_shape=[wide, thin],
        compiler_params=params(24),
        cost_estimate=work,
        name="attend_last",
    )(own_queries, halves[1], halves[1], mixed, peak, total)


def middle_kernel(
    core, tokens, attended, log_total, cotangent, w_out, w_in, w_mlp, gain,
    layer_out, own_halves, other_halves, whole, grad_middle, grads, logs_deltas,
):

    rows, width = tokens.shape
    first = core[0] == 0

    def put_halves(at, block):
        half = block.shape[1] // 2
        left, right = block[:, :half], block[:, half:]
        own_halves[:, at : at + half] = jnp.where(first, left, right)
        other_halves[:, at : at + half] = jnp.where(first, right, left)

    mixed = attended[...]
    mixed_low = mixed.astype(BF16)
    put_halves(ATTENDED_AT, mixed_low)
    middle = tokens[...].astype(F32) + dot_nn(mixed_low, w_out[...])
    normed, rstd = normalize(middle)
    gain_row = gain[...].astype(F32)
    second = (normed * gain_row).astype(BF16)
    put_halves(NORMED_AT, second)
    gate = dot_nn(second, w_in[:, :FF])
    up = dot_nn(second, w_in[:, FF:])
    cdf = 0.5 * (1.0 + lax.erf(gate * (0.5**0.5)))
    activated = gate * cdf
    hidden = (activated * up).astype(BF16)
    put_halves(0, hidden)
    layer_out[...] = (middle + dot_nn(hidden, w_mlp[...])).astype(BF16)
    upstream = cotangent[...]
    grad_hidden = dot_nt(upstream, w_mlp[...]).astype(BF16).astype(F32)
    density = jnp.exp(-0.5 * gate * gate) * 0.3989422804014327
    grad_gate = (grad_hidden * up * (cdf + gate * density)).astype(BF16)
    grad_up = (grad_hidden * activated).astype(BF16)
    whole[:, :FF] = grad_gate
    whole[:, FF : 2 * FF] = grad_up
    grad_second = dot_nt(grad_gate, w_in[:, :FF]) + dot_nt(grad_up, w_in[:, FF:])
    grad_mid = upstream.astype(F32) + norm_back(grad_second, normed, rstd, gain_row)
    grad_middle[...] = grad_mid
    branch = grad_mid.astype(BF16)
    whole[:, 2 * FF :] = branch
    grad_attended = dot_nt(branch, w_out[...]).astype(BF16)
    grads[...] = grad_attended
    products = grad_attended.astype(F32) * mixed
    head = lax.broadcasted_iota(jnp.int32, (width, LANES), 0) // 64
    to_lane = (lane_of((width, LANES)) == head + HEADS).astype(F32)
    both = log_total[...] + lax.dot_general(
        products,
        to_lane,
        (((1,), (0,)), ((), ())),
        precision=lax.Precision.HIGHEST,
        preferred_element_type=F32,
    )
    logs_deltas[...] = both.T


def middle_part(core, tokens, attended, log_total, cotangent, w_out, w_in, w_mlp, gain):
    rows, width = tokens.shape
    wide, halves = (rows, width), (rows, HALVES_WIDTH)
    shapes = [
        (wide, BF16), (halves, BF16), (halves, BF16), ((rows, 2 * FF + width), BF16),
        (wide, F32), (wide, BF16), ((LANES, rows), F32),
    ]
    return pl.pallas_call(
        middle_kernel,
        in_specs=[SMEM_SPEC] + [WHOLE] * 8,
        out_shape=[jax.ShapeDtypeStruct(*shape) for shape in shapes],
        compiler_params=params(32),
        cost_estimate=cost(4 * rows * width * (2 * width + 6 * FF), 24 * MIB),
        name="middle",
    )(core, tokens, attended, log_total, cotangent, w_out, w_in, w_mlp, gain)


def rows_kernel(own, other, upstream, upstream_other, whole, whole_other, out_mlp, out_in):
    width = out_mlp.shape[1]
    half, half_ff = width // 2, FF // 2
    both = jnp.concatenate([own[...], other[...]], axis=0)
    right = jnp.concatenate([upstream[...], upstream_other[...]], axis=0)
    out_mlp[:half_ff, :] = dot_tn(both[:, :half_ff], right).astype(BF16)
    branch = jnp.concatenate([whole[:, 2 * FF :], whole_other[:, 2 * FF :]], axis=0)
    left = both[:, ATTENDED_AT : ATTENDED_AT + half]
    out_mlp[half_ff : half_ff + half, :] = dot_tn(left, branch).astype(BF16)
    turned = both[:, NORMED_AT : NORMED_AT + half].T
    for k in range(2 * FF // width):
        lanes = slice(k * width, (k + 1) * width)
        right = jnp.concatenate([whole[:, lanes], whole_other[:, lanes]], axis=0)
        out_in[k * half : (k + 1) * half, :] = dot_nn(turned, right).astype(BF16)
    for out, used in ((out_mlp, half_ff + half), (out_in, 2 * FF // width * half)):
        if used < out.shape[0]:
            out[used:, :] = jnp.zeros((out.shape[0] - used, width), BF16)


def padded(rows, pieces):
    unit = 8 * pieces
    return (rows + unit - 1) // unit * unit


def grad_rows(pieces, width, *arrays):
    sizes = padded((FF + width) // 2, pieces), padded(FF, pieces)
    return pl.pallas_call(
        rows_kernel,
        out_shape=[jax.ShapeDtypeStruct((size, width), BF16) for size in sizes],
        compiler_params=params(16),
        cost_estimate=cost(512 * 1728 * width, 12 * MIB),
        name="grad_rows",
    )(*arrays)


def unpack_kernel(places, gained, bit, own, other, *refs):
    half = own.shape[0]
    if gained:
        weights, gain = refs[:2]
    outs = refs[2:] if gained else refs

    def put(low, high):
        at = 0
        for out, blocks in places:
            ref = outs[out]
            made = ref.shape[0]
            for k in range(blocks):
                columns = slice(k * low.shape[1], (k + 1) * low.shape[1])
                cut = min(max(half - at, 0), made)
                if cut > 0:
                    ref[:cut, columns] = low[at : at + cut, :].astype(F32)
                if cut < made:
                    start = at + cut - half
                    ref[cut:, columns] = high[start : start + made - cut, :].astype(F32)
                at += made

    @pl.when(bit[0] == 0)
    def _():
        put(own, other)

    @pl.when(bit[0] != 0)
    def _():
        put(other, own)

    if gained:
        products = outs[0][...] * weights[...].astype(F32)
        sums = jnp.sum(products, axis=1, keepdims=True)
        row = jnp.broadcast_to(sums, (sums.shape[0], LANES)).T[:1]
        outs[-1][...] = (row / gain[...].astype(F32)).reshape(outs[-1].shape)


def unpack(chain, shapes, gained=()):
    own, other = chain.parts
    width = own.shape[1]
    places = [(k, shape[1] // width) for k, shape in enumerate(shapes)]
    if gained:
        shapes = shapes + [gained[1].shape[1:]]
    return pl.pallas_call(
        partial(unpack_kernel, places, bool(gained)),
        in_specs=[SMEM_SPEC] + [WHOLE] * (2 + len(gained)),
        out_shape=[jax.ShapeDtypeStruct(shape, F32) for shape in shapes],
        compiler_params=params(24),
        cost_estimate=cost(0, 12 * own.size),
        name="unpack",
    )(chain.bit.reshape(1), own, other, *gained)


def unrotated(block, cos, sin):
    return block * cos - halves_swapped(block) * sin


def row_pair(rows, at):
    index = lax.broadcasted_iota(jnp.int32, rows.shape, 0)
    picked = [
        jnp.sum(jnp.where(index == at + k, rows, 0.0), axis=0, keepdims=True) for k in (0, 1)
    ]
    return jnp.concatenate(picked, axis=1)


def attend_back_kernel(
    queries, keys_a, values_a, keys_b, values_b, grads, logs_deltas, cos, sin,
    out_queries, out_keys, out_values,
):
    pair = pl.program_id(0)
    rows, count = queries.shape[0], keys_a.shape[0]
    queries_two = two_heads(queries[...])
    grads_two = two_heads(grads[...])
    logs = row_pair(logs_deltas[...], 2 * pair)
    deltas = row_pair(logs_deltas[...], HEADS + 2 * pair)
    total = jnp.zeros((2 * rows, LANES), F32)
    for base, keys, values in ((0, keys_a, values_a), (count, keys_b, values_b)):
        for at in chunks_of(count):
            to = slice(base + at.start, base + at.stop)
            key_rows = keys[at, :]
            probs = jnp.exp(dot_nt(key_rows, queries_two) - logs)
            grad_probs = dot_nt(values[at, :], grads_two)
            grad_scores = (probs * (grad_probs - deltas)).astype(BF16)
            out_values[to, :] = dot_nn(probs.astype(BF16), grads_two).astype(BF16)
            grad_keys = dot_nn(grad_scores, queries_two)
            out_keys[to, :] = unrotated(grad_keys, cos[to, :], sin[to, :]).astype(BF16)
            total = total + dot_tn(grad_scores, key_rows)
    grad = one_pair(total) * 0.125
    out_queries[...] = unrotated(grad, cos[:rows, :], sin[:rows, :]).astype(BF16)


def attend_back(own_queries, halves, grads, logs_deltas, cos, sin):
    count = halves[0].shape[0]
    rows, width = own_queries.shape
    pairs = width // LANES
    queries = pl.BlockSpec((rows, LANES), lambda j: (0, j))
    shared = pl.BlockSpec((LANES, rows), lambda j: (0, 0))
    keys = pl.BlockSpec((count, LANES), lambda j: (0, j))
    values = pl.BlockSpec((count, LANES), lambda j: (0, pairs + j))
    table = pl.BlockSpec((2 * count, LANES), lambda j: (0, 0))
    made = pl.BlockSpec((2 * count, LANES), lambda j: (0, j))
    return pl.pallas_call(
        attend_back_kernel,
        grid=(pairs,),
        in_specs=[queries, keys, values, keys, values, queries, shared, table, table],
        out_specs=[queries, made, made],
        out_shape=[
            jax.ShapeDtypeStruct((rows, width), BF16),
            jax.ShapeDtypeStruct((2 * count, width), BF16),
            jax.ShapeDtypeStruct((2 * count, width), BF16),
        ],
        compiler_params=params(16 if count <= 1024 else 48),
        cost_estimate=cost(40 * rows * count * width, 20 * count * width),
        name="attend_back",
    )(
        own_queries, halves[0], halves[0], halves[1], halves[1],
        grads, logs_deltas, cos, sin,
    )


def late_rows_kernel(
    core, low_a, low_b, grad_q, grad_k, grad_v, out_own, out_other, total
):
    step, steps = pl.program_id(0), pl.num_programs(0)
    own_rows, width = grad_q.shape
    half = width // 2
    low = jnp.where(2 * step < steps, low_a[...], low_b[...])
    turned = low.T
    made_k, made_v = dot_nn(turned, grad_k[...]), dot_nn(turned, grad_v[...])

    @pl.when(step == 0)
    def _():
        total[:, :width] = dot_nn(turned[:, :own_rows], grad_q[...])
        total[:, width : 2 * width] = made_k
        total[:, 2 * width :] = made_v

    @pl.when(step > 0)
    def _():
        total[:, width : 2 * width] += made_k
        total[:, 2 * width :] += made_v

    @pl.when(step == steps - 1)
    def _():
        for out, side in ((out_own, core[0]), (out_other, 1 - core[0])):
            start = pl.multiple_of(side * half, half)
            for k in range(3):
                columns = slice(k * width, (k + 1) * width)
                out[k * half : (k + 1) * half, :] = total[pl.ds(start, half), columns].astype(BF16)
            if out.shape[0] > 3 * half:
                out[3 * half :, :] = jnp.zeros((out.shape[0] - 3 * half, width), BF16)


def late_rows(core, pieces, lows, grad_q, grad_k, grad_v):
    count, width = lows[0].shape
    own_rows = grad_q.shape[0]
    step = min(count, 512)
    each = count // step
    total = padded(3 * width // 2, pieces)
    grads = pl.BlockSpec((step, width), lambda i: (i, 0))
    fixed = pl.BlockSpec((own_rows, width), lambda i: (0, 0))
    made = pl.BlockSpec((total, width), lambda i: (0, 0))
    return pl.pallas_call(
        late_rows_kernel,
        grid=(2 * each,),
        in_specs=[
            SMEM_SPEC,
            pl.BlockSpec((step, width), lambda i: (jnp.minimum(i, each - 1), 0)),
            pl.BlockSpec((step, width), lambda i: (jnp.maximum(i - each, 0), 0)),
            fixed, grads, grads,
        ],
        out_specs=[made, made],
        out_shape=[jax.ShapeDtypeStruct((total, width), BF16)] * 2,
        scratch_shapes=[pltpu.VMEM((width, 3 * width), F32)],
        compiler_params=params(24),
        cost_estimate=cost(4 * count * width * width, 8 * count * width),
        name="late_rows",
    )(core, *lows, grad_q, grad_k, grad_v)


def first_rows_kernel(grad_q, grad_k, grad_v, weights, out):
    width = grad_q.shape[1]
    own_rows = grad_q.shape[0]
    made = dot_nt(grad_k[...], weights[:, width : 2 * width])
    made = made + dot_nt(grad_v[...], weights[:, 2 * width :])

    @pl.when(pl.program_id(0) == 0)
    def _():
        own = made[:own_rows] + dot_nt(grad_q[...], weights[:, :width])
        out[:own_rows, :] = own.astype(BF16)
        out[own_rows:, :] = made[own_rows:].astype(BF16)

    @pl.when(pl.program_id(0) > 0)
    def _():
        out[...] = made.astype(BF16)


def first_rows(grad_q, grad_k, grad_v, weights):
    rows, width = grad_k.shape
    own_rows = grad_q.shape[0]
    step = min(rows, 2 * own_rows)
    block = pl.BlockSpec((step, width), lambda i: (i, 0))
    return pl.pallas_call(
        first_rows_kernel,
        grid=(rows // step,),
        in_specs=[
            pl.BlockSpec((own_rows, width), lambda i: (0, 0)),
            block,
            block,
            pl.BlockSpec((width, 3 * width), lambda i: (0, 0)),
        ],
        out_specs=block,
        out_shape=jax.ShapeDtypeStruct((rows, width), BF16),
        compiler_params=params(16),
        cost_estimate=cost(4 * rows * width * width, 8 * rows * width),
        name="first_rows",
    )(grad_q, grad_k, grad_v, weights)


def last_kernel(tokens, grad_middle, part_a, part_b, gain, out):
    normed, rstd = normalize(tokens[...].astype(F32))
    grad_first = part_a[...].astype(F32) + part_b[...].astype(F32)
    back = norm_back(grad_first, normed, rstd, gain[...].astype(F32))
    out[...] = (grad_middle[...] + back).astype(BF16)


def last_part(tokens, grad_middle, parts, gain):
    return pl.pallas_call(
        last_kernel,
        out_shape=jax.ShapeDtypeStruct(tokens.shape, BF16),
        compiler_params=params(24),
        cost_estimate=cost(20 * tokens.size, 12 * tokens.size),
        name="last",
    )(tokens, grad_middle, *parts, gain)


def rotary_tables(positions, head_dim):
    half = head_dim // 2
    inverse = jnp.power(F32(THETA), -(jnp.arange(half, dtype=F32) * (2.0 / head_dim)))
    angles = positions[:, None] * inverse[None, :]
    cos, sin = jnp.cos(angles), jnp.sin(angles)
    return (
        jnp.concatenate([cos, cos, cos, cos], axis=1),
        jnp.concatenate([-sin, sin, -sin, sin], axis=1),
    )


def local(tokens, w_qkv, w_out, w_in, w_mlp, gain_attn, gain_mlp, cotangent):
    seqs_here, rows, width = tokens.shape
    half, half_ff = width // 2, FF // 2
    core = lax.axis_index("wsh")
    own = tokens.reshape(rows, width)
    upstream = cotangent.reshape(rows, width)
    pieces = lax.axis_size("seq") * lax.axis_size("ctx")

    gathered = gather_context(own)
    qkv_other = swap_cores(w_qkv)
    gains = jnp.stack([gain_attn, gain_mlp])
    gains_other = swap_cores(gains)
    gains_all = jnp.concatenate(
        [jnp.where(core == 0, gains, gains_other), jnp.where(core == 0, gains_other, gains)], axis=1
    )
    attn_gain, mlp_gain = gains_all[:1], gains_all[1:]
    full_out = both_halves(w_out)
    full_in = both_halves(w_in)
    full_mlp = both_halves(w_mlp)
    upstream_other = swap_cores(upstream)

    blocks = gathered_blocks()
    positions = (blocks[:, None] * rows + jnp.arange(rows, dtype=jnp.int32)[None, :]).reshape(-1)
    cos, sin = rotary_tables(positions.astype(F32), 64)
    count = gathered[0].shape[0]
    core_at = core.reshape(1)
    first_half, first_low, queries, full_qkv = project(
        core_at, gathered[0], w_qkv, qkv_other, attn_gain, cos[:count], sin[:count], rows
    )
    last_half, last_low = project(
        core_at, gathered[1], full_qkv, attn_gain, attn_gain, cos[count:], sin[count:], 0
    )
    halves = first_half, last_half
    attended, log_total = attend(queries, halves)
    (
        layer_out, own_halves, other_halves, whole, grad_middle, grads, logs_deltas,
    ) = middle_part(
        core_at, own, attended, log_total, upstream, full_out, full_in, full_mlp, mlp_gain
    )

    grad_q, grad_k, grad_v = attend_back(queries, halves, grads, logs_deltas, cos, sin)
    other_halves, whole_other = swap_cores(other_halves), swap_cores(whole)
    own_halves, grad_q = lax.optimization_barrier((own_halves, grad_q))
    mlp_rows, in_rows = grad_rows(
        pieces, width, own_halves, other_halves, upstream, upstream_other,
        whole, whole_other,
    )
    (grad_q,) = after([grad_q], mlp_rows, in_rows)
    late_own, late_other = late_rows(
        core_at, pieces, (first_low, last_low), grad_q, grad_k, grad_v
    )
    chains = [
        RowsSum([mlp_rows], MLP_ORDERS),
        RowsSum([in_rows], IN_ORDERS),
        RowsSum([late_own, swap_cores(late_other)], LATE_ORDERS),
    ]
    aways = lax.optimization_barrier(tuple(chain.first_away() for chain in chains))
    for chain, away in zip(chains, aways):
        chain.step(away)
    (grad_q,) = after([grad_q], *aways)
    chains.append(ContextSum(first_rows(grad_q, grad_k, grad_v, full_qkv)))
    while any(chain.left for chain in chains):
        for chain in chains:
            if chain.left:
                chain.step()
    mlp_grad, out_grad = unpack(chains[0], [(half_ff, width), (half, width)])
    in_grad, gain_mlp_grad = unpack(
        chains[1], [(half, 2 * FF)], (w_in, gain_mlp.reshape(1, half))
    )
    qkv_grad, gain_attn_grad = unpack(
        chains[2], [(half, 3 * width)], (w_qkv, gain_attn.reshape(1, half))
    )
    tokens_grad = last_part(own, grad_middle, chains[3].parts, attn_gain)
    return (
        layer_out.reshape(seqs_here, rows, width),
        tokens_grad.reshape(seqs_here, rows, width),
        qkv_grad,
        out_grad,
        in_grad,
        mlp_grad,
        gain_attn_grad,
        gain_mlp_grad,
    )


def solution(mesh):
    placed = (
        P(("seq", "wsh"), "ctx", None),
        P("wsh", None),
        P("wsh", None),
        P("wsh", None),
        P("wsh", None),
        P("wsh"),
        P("wsh"),
        P(("seq", "wsh"), "ctx", None),
    )
    return jax.shard_map(
        local,
        mesh=mesh,
        in_specs=placed,
        out_specs=(
            P(("seq", "wsh"), "ctx", None),
            P(("seq", "wsh"), "ctx", None),
            P("wsh", None),
            P("wsh", None),
            P("wsh", None),
            P("wsh", None),
            P("wsh"),
            P("wsh"),
        ),
        check_vma=False,
    )
```

```python
from functools import partial

import jax
import jax.numpy as jnp
from jax import lax
from jax.experimental import pallas as pl
from jax.experimental.pallas import tpu as pltpu
from jax.sharding import PartitionSpec as P

HEADS = 12
FF = 1152
EPSILON = 1e-05
THETA = 160000.0
LANES = 128
NORMED_AT = 640
ATTENDED_AT = 1024
HALVES_WIDTH = 1408
MLP_ORDERS = ("xyab", "yxba")
IN_ORDERS = ("yxab", "xyab")
LATE_ORDERS = ("ayxb", "bxya")
MIB = 1 << 20
BF16 = jnp.bfloat16
F32 = jnp.float32


def bits_of(axis):
    return [(axis, k) for k in range((lax.axis_size(axis) - 1).bit_length())]


def my_bit(axis, k):
    return (lax.axis_index(axis) >> k) & 1


def flip(block, first, second):
    n_seq, n_ctx = lax.axis_size("seq"), lax.axis_size("ctx")
    route = []
    for s in range(n_seq):
        for t in range(n_ctx):
            for core, (axis, k) in enumerate((first, second)):
                s2, t2 = (s ^ (1 << k), t) if axis == "seq" else (s, t ^ (1 << k))
                route.append(((s * n_ctx + t) * 2 + core, (s2 * n_ctx + t2) * 2 + core))
    return lax.ppermute(block, ("seq", "ctx", "wsh"), route)


def swap_cores(block):
    return lax.ppermute(block, "wsh", [(0, 1), (1, 0)])


def gather_orders():
    bits = bits_of("ctx")
    return bits[::-1], bits[:1] + bits[:0:-1]


def gather_context(block):
    stages = list(zip(*gather_orders()))
    for first, second in stages[:-1]:
        block = jnp.concatenate([block, flip(block, first, second)], axis=0)
    return block, flip(block, *stages[-1])


class ContextSum:
    def __init__(self, rows):
        self.parts = [rows]
        self.stages = list(zip(*gather_orders()))[::-1]

    def step(self):
        half = self.parts[0].shape[0] // 2
        away, kept = (
            sum(part[at : at + half].astype(F32) for part in self.parts).astype(BF16)
            for at in (half, 0)
        )
        self.parts = [kept, flip(away, *self.stages.pop(0))]

    @property
    def left(self):
        return len(self.stages)


def gathered_blocks():
    tables = []
    for order in gather_orders():
        slots = [0]
        for _, k in order:
            slots = slots + [slot | (1 << k) for slot in slots]
        tables.append(slots)
    mine = jnp.where(lax.axis_index("wsh") == 0, jnp.array(tables[0]), jnp.array(tables[1]))
    return mine ^ lax.axis_index("ctx")


def sum_orders(orders):
    ctx = bits_of("ctx")
    bits = {"x": bits_of("seq"), "y": ctx[:1], "a": ctx[1:2], "b": ctx[2:]}
    return list(zip(*[sum((bits[letter] for letter in order), []) for order in orders]))


def stage_bit(first, second):
    return jnp.where(lax.axis_index("wsh") == 0, my_bit(*first), my_bit(*second))


def after(arrays, *made):
    return lax.optimization_barrier((*arrays, *made))[: len(arrays)]


class RowsSum:
    def __init__(self, parts, orders):
        self.parts = parts
        self.starts = [0] * len(parts)
        self.size = parts[0].shape[0]
        self.stages = sum_orders(orders)
        self.at = 0

    def summed(self, start, size):
        cut = [
            lax.dynamic_slice_in_dim(part, first + start, size, 0).astype(F32)
            for part, first in zip(self.parts, self.starts)
        ]
        return sum(cut[1:], cut[0]).astype(BF16)

    def first_away(self):
        return self.summed((1 - stage_bit(*self.stages[0])) * (self.size // 2), self.size // 2)

    def step(self, away=None):
        count, at = len(self.stages), self.at
        self.at += 1
        if at < count:
            stage = self.stages[at]
            bit = stage_bit(*stage)
            self.size //= 2
            if away is None:
                away = self.summed((1 - bit) * self.size, self.size)
            if at == 0:
                kept, starts = self.parts, [start + bit * self.size for start in self.starts]
            else:
                kept, starts = [self.summed(bit * self.size, self.size)], [0]
            self.parts = [*kept, flip(away, *stage)]
            self.starts = [*starts, 0]
            return
        stage = self.stages[2 * count - 1 - at]
        if at == count:
            rows = self.summed(0, self.size)
        else:
            own, other = self.parts
            low = jnp.where(self.bit == 0, own, other)
            high = jnp.where(self.bit == 0, other, own)
            rows = jnp.concatenate([low, high], axis=0)
        self.bit = stage_bit(*stage)
        self.parts = [rows, flip(rows, *stage)]

    @property
    def left(self):
        return 2 * len(self.stages) - self.at


def both_halves(block):
    other = swap_cores(block)
    core = lax.axis_index("wsh")
    return jnp.concatenate(
        [jnp.where(core == 0, block, other), jnp.where(core == 0, other, block)], axis=0
    )


def dot_nn(a, b):
    return lax.dot_general(a, b, (((1,), (0,)), ((), ())), preferred_element_type=F32)


def dot_nt(a, b):
    return lax.dot_general(a, b, (((1,), (1,)), ((), ())), preferred_element_type=F32)


def dot_tn(a, b):
    return lax.dot_general(a, b, (((0,), (0,)), ((), ())), preferred_element_type=F32)


SMEM_SPEC = pl.BlockSpec(memory_space=pltpu.SMEM)
WHOLE = pl.BlockSpec()


def cost(flops, moved):
    return pl.CostEstimate(flops=int(flops), bytes_accessed=int(moved), transcendentals=0)


def params(mib):
    return pltpu.CompilerParams(vmem_limit_bytes=mib * MIB)


def normalize(inputs):
    average = jnp.mean(inputs, axis=-1, keepdims=True)
    centred = inputs - average
    variance = jnp.mean(centred * centred, axis=-1, keepdims=True)
    rstd = lax.rsqrt(variance + EPSILON)
    return centred * rstd, rstd


def norm_back(grad_rows, normed, rstd, gain):
    scaled = grad_rows * gain
    inner = jnp.mean(scaled * normed, axis=-1, keepdims=True)
    return rstd * (scaled - jnp.mean(scaled, axis=-1, keepdims=True) - normed * inner)


def lane_of(shape):
    return lax.broadcasted_iota(jnp.int32, shape, len(shape) - 1)


def halves_swapped(vectors):
    first = (lane_of(vectors.shape) & 63) < 32
    return jnp.where(first, pltpu.roll(vectors, LANES - 32, 1), pltpu.roll(vectors, 32, 1))


def project_kernel(core, tokens, weights, other, gain, cos, sin, out, out_low, *more):
    width = tokens.shape[1]
    half = width // 2
    if more:
        queries, joined = more

        @pl.when(pl.program_id(0) == 0)
        def _():
            joined[pl.ds(pl.multiple_of(core[0] * half, half), half), :] = weights[...]
            joined[pl.ds(pl.multiple_of((1 - core[0]) * half, half), half), :] = other[...]

        weights = joined
    normed, _ = normalize(tokens[...].astype(F32))
    low = (normed * gain[...].astype(F32)).astype(BF16)
    out_low[...] = low

    def put(ref, start, rows, columns, turned, scale):
        for j in range(width // LANES):
            piece = columns[:, j * LANES : (j + 1) * LANES]
            if turned:
                piece = piece * cos[:rows, :] + halves_swapped(piece) * sin[:rows, :]
            ref[:, start + j * LANES : start + (j + 1) * LANES] = (piece * scale).astype(BF16)

    rows = tokens.shape[0]
    put(out, 0, rows, dot_nn(low, weights[:, width : 2 * width]), True, 1.0)
    put(out, width, rows, dot_nn(low, weights[:, 2 * width :]), False, 1.0)
    if more:

        @pl.when(pl.program_id(0) == 0)
        def _():
            own = queries.shape[0]
            put(queries, 0, own, dot_nn(low[:own], weights[:, :width]), True, 0.125)


def project(core, tokens, weights, other, gain, cos, sin, own_rows):
    rows, width = tokens.shape
    step = min(rows, 256)

    def fixed(shape):
        return pl.BlockSpec(shape, lambda i: (0, 0))

    out_specs = [
        pl.BlockSpec((step, 2 * width), lambda i: (i, 0)),
        pl.BlockSpec((step, width), lambda i: (i, 0)),
    ]
    out_shape = [
        jax.ShapeDtypeStruct((rows, 2 * width), BF16),
        jax.ShapeDtypeStruct((rows, width), BF16),
    ]
    if own_rows:
        out_specs += [fixed((own_rows, width)), fixed((width, 3 * width))]
        out_shape.append(jax.ShapeDtypeStruct((own_rows, width), BF16))
        out_shape.append(jax.ShapeDtypeStruct((width, 3 * width), BF16))
    return pl.pallas_call(
        project_kernel,
        grid=(rows // step,),
        in_specs=[
            SMEM_SPEC,
            pl.BlockSpec((step, width), lambda i: (i, 0)),
            fixed(weights.shape),
            fixed(other.shape),
            fixed((1, width)),
            pl.BlockSpec((step, LANES), lambda i: (i, 0)),
            pl.BlockSpec((step, LANES), lambda i: (i, 0)),
        ],
        out_specs=out_specs,
        out_shape=out_shape,
        compiler_params=params(28),
        cost_estimate=cost(4 * rows * width * width, 8 * rows * width),
        name="project",
    )(core, tokens, weights, other, gain, cos, sin)


def two_heads(block):
    first = lane_of(block.shape) < 64
    zero = jnp.zeros_like(block)
    return jnp.concatenate([jnp.where(first, block, zero), jnp.where(first, zero, block)], axis=0)


def one_pair(stacked):
    rows = stacked.shape[0] // 2
    return jnp.where(lane_of((rows, LANES)) < 64, stacked[:rows], stacked[rows:])


def column_pair(columns, at):
    lanes = lane_of(columns.shape)
    picked = [
        jnp.sum(jnp.where(lanes == at + k, columns, 0.0), axis=1, keepdims=True) for k in (0, 1)
    ]
    return jnp.concatenate(picked, axis=0)


def put_pair(ref, pair, values):
    rows = ref.shape[0]

    @pl.when(pair == 0)
    def _():
        ref[...] = jnp.zeros_like(ref)

    lanes = lane_of((rows, LANES))
    kept = jnp.where(lanes == 2 * pair, values[:rows], ref[...])
    ref[...] = jnp.where(lanes == 2 * pair + 1, values[rows:], kept)


def chunks_of(count):
    step = min(count, 1024)
    return [slice(at, at + step) for at in range(0, count, step)]


def attend_over(stacked, keys, values, peak, total, mixed):
    for at in chunks_of(keys.shape[0]):
        logits = dot_nt(stacked, keys[at, :])
        top = jnp.max(logits, axis=1, keepdims=True)
        if peak is None:
            weights = jnp.exp(logits - top)
            total = jnp.sum(weights, axis=1, keepdims=True)
            mixed = dot_nn(weights.astype(BF16), values[at, :])
        else:
            top = jnp.maximum(peak, top)
            weights = jnp.exp(logits - top)
            factor = jnp.exp(peak - top)
            total = total * factor + jnp.sum(weights, axis=1, keepdims=True)
            mixed = mixed * factor + dot_nn(weights.astype(BF16), values[at, :])
        peak = top
    return peak, total, mixed


def attend_first_kernel(queries, keys, values, out_mixed, out_peak, out_total):
    pair = pl.program_id(0)
    stacked = two_heads(queries[...])
    peak, total, mixed = attend_over(stacked, keys, values, None, None, None)
    out_mixed[...] = one_pair(mixed)
    put_pair(out_peak, pair, peak)
    put_pair(out_total, pair, total)


def attend_last_kernel(
    queries, keys, values, in_mixed, in_peak, in_total, attended, log_total
):
    pair = pl.program_id(0)
    stacked = two_heads(queries[...])
    peak = column_pair(in_peak[...], 2 * pair)
    total = column_pair(in_total[...], 2 * pair)
    mixed = jnp.concatenate([in_mixed[...]] * 2, axis=0)
    peak, total, mixed = attend_over(stacked, keys, values, peak, total, mixed)
    attended[...] = one_pair(mixed / total)
    put_pair(log_total, pair, peak + jnp.log(total))


def attend(own_queries, halves):
    count = halves[0].shape[0]
    rows, width = own_queries.shape
    pairs = width // LANES
    queries = pl.BlockSpec((rows, LANES), lambda j: (0, j))
    shared = pl.BlockSpec((rows, LANES), lambda j: (0, 0))
    keys = pl.BlockSpec((count, LANES), lambda j: (0, j))
    values = pl.BlockSpec((count, LANES), lambda j: (0, pairs + j))
    wide = jax.ShapeDtypeStruct((rows, width), F32)
    thin = jax.ShapeDtypeStruct((rows, LANES), F32)
    work = cost(8 * rows * count * width, 6 * count * width)
    mixed, peak, total = pl.pallas_call(
        attend_first_kernel,
        grid=(pairs,),
        in_specs=[queries, keys, values],
        out_specs=[queries, shared, shared],
        out_shape=[wide, thin, thin],
        compiler_params=params(24),
        cost_estimate=work,
        name="attend_first",
    )(own_queries, halves[0], halves[0])
    return pl.pallas_call(
        attend_last_kernel,
        grid=(pairs,),
        in_specs=[queries, keys, values, queries, shared, shared],
        out_specs=[queries, shared],
        out_shape=[wide, thin],
        compiler_params=params(24),
        cost_estimate=work,
        name="attend_last",
    )(own_queries, halves[1], halves[1], mixed, peak, total)


def middle_kernel(
    core, tokens, attended, log_total, cotangent, w_out, w_in, w_mlp, gain,
    layer_out, own_halves, other_halves, whole, grad_middle, grads, logs_deltas,
):

    rows, width = tokens.shape
    first = core[0] == 0

    def put_halves(at, block):
        half = block.shape[1] // 2
        left, right = block[:, :half], block[:, half:]
        own_halves[:, at : at + half] = jnp.where(first, left, right)
        other_halves[:, at : at + half] = jnp.where(first, right, left)

    mixed = attended[...]
    mixed_low = mixed.astype(BF16)
    put_halves(ATTENDED_AT, mixed_low)
    middle = tokens[...].astype(F32) + dot_nn(mixed_low, w_out[...])
    normed, rstd = normalize(middle)
    gain_row = gain[...].astype(F32)
    second = (normed * gain_row).astype(BF16)
    put_halves(NORMED_AT, second)
    gate = dot_nn(second, w_in[:, :FF])
    up = dot_nn(second, w_in[:, FF:])
    cdf = 0.5 * (1.0 + lax.erf(gate * (0.5**0.5)))
    activated = gate * cdf
    hidden = (activated * up).astype(BF16)
    put_halves(0, hidden)
    layer_out[...] = (middle + dot_nn(hidden, w_mlp[...])).astype(BF16)
    upstream = cotangent[...]
    grad_hidden = dot_nt(upstream, w_mlp[...]).astype(BF16).astype(F32)
    density = jnp.exp(-0.5 * gate * gate) * 0.3989422804014327
    grad_gate = (grad_hidden * up * (cdf + gate * density)).astype(BF16)
    grad_up = (grad_hidden * activated).astype(BF16)
    whole[:, :FF] = grad_gate
    whole[:, FF : 2 * FF] = grad_up
    grad_second = dot_nt(grad_gate, w_in[:, :FF]) + dot_nt(grad_up, w_in[:, FF:])
    grad_mid = upstream.astype(F32) + norm_back(grad_second, normed, rstd, gain_row)
    grad_middle[...] = grad_mid
    branch = grad_mid.astype(BF16)
    whole[:, 2 * FF :] = branch
    grad_attended = dot_nt(branch, w_out[...]).astype(BF16)
    grads[...] = grad_attended
    products = grad_attended.astype(F32) * mixed
    head = lax.broadcasted_iota(jnp.int32, (width, LANES), 0) // 64
    to_lane = (lane_of((width, LANES)) == head + HEADS).astype(F32)
    both = log_total[...] + lax.dot_general(
        products,
        to_lane,
        (((1,), (0,)), ((), ())),
        precision=lax.Precision.HIGHEST,
        preferred_element_type=F32,
    )
    logs_deltas[...] = both.T


def middle_part(core, tokens, attended, log_total, cotangent, w_out, w_in, w_mlp, gain):
    rows, width = tokens.shape
    wide, halves = (rows, width), (rows, HALVES_WIDTH)
    shapes = [
        (wide, BF16), (halves, BF16), (halves, BF16), ((rows, 2 * FF + width), BF16),
        (wide, F32), (wide, BF16), ((LANES, rows), F32),
    ]
    return pl.pallas_call(
        middle_kernel,
        in_specs=[SMEM_SPEC] + [WHOLE] * 8,
        out_shape=[jax.ShapeDtypeStruct(*shape) for shape in shapes],
        compiler_params=params(32),
        cost_estimate=cost(4 * rows * width * (2 * width + 6 * FF), 24 * MIB),
        name="middle",
    )(core, tokens, attended, log_total, cotangent, w_out, w_in, w_mlp, gain)


def rows_kernel(own, other, upstream, upstream_other, whole, whole_other, out_mlp, out_in):
    width = out_mlp.shape[1]
    half, half_ff = width // 2, FF // 2
    both = jnp.concatenate([own[...], other[...]], axis=0)
    right = jnp.concatenate([upstream[...], upstream_other[...]], axis=0)
    out_mlp[:half_ff, :] = dot_tn(both[:, :half_ff], right).astype(BF16)
    branch = jnp.concatenate([whole[:, 2 * FF :], whole_other[:, 2 * FF :]], axis=0)
    left = both[:, ATTENDED_AT : ATTENDED_AT + half]
    out_mlp[half_ff : half_ff + half, :] = dot_tn(left, branch).astype(BF16)
    turned = both[:, NORMED_AT : NORMED_AT + half].T
    for k in range(2 * FF // width):
        lanes = slice(k * width, (k + 1) * width)
        right = jnp.concatenate([whole[:, lanes], whole_other[:, lanes]], axis=0)
        out_in[k * half : (k + 1) * half, :] = dot_nn(turned, right).astype(BF16)
    for out, used in ((out_mlp, half_ff + half), (out_in, 2 * FF // width * half)):
        if used < out.shape[0]:
            out[used:, :] = jnp.zeros((out.shape[0] - used, width), BF16)


def padded(rows, pieces):
    unit = 8 * pieces
    return (rows + unit - 1) // unit * unit


def grad_rows(pieces, width, *arrays):
    sizes = padded((FF + width) // 2, pieces), padded(FF, pieces)
    return pl.pallas_call(
        rows_kernel,
        out_shape=[jax.ShapeDtypeStruct((size, width), BF16) for size in sizes],
        compiler_params=params(16),
        cost_estimate=cost(512 * 1728 * width, 12 * MIB),
        name="grad_rows",
    )(*arrays)


def unpack_kernel(places, gained, bit, own, other, *refs):
    half = own.shape[0]
    if gained:
        weights, gain = refs[:2]
    outs = refs[2:] if gained else refs

    def put(low, high):
        at = 0
        for out, blocks in places:
            ref = outs[out]
            made = ref.shape[0]
            for k in range(blocks):
                columns = slice(k * low.shape[1], (k + 1) * low.shape[1])
                cut = min(max(half - at, 0), made)
                if cut > 0:
                    ref[:cut, columns] = low[at : at + cut, :].astype(F32)
                if cut < made:
                    start = at + cut - half
                    ref[cut:, columns] = high[start : start + made - cut, :].astype(F32)
                at += made

    @pl.when(bit[0] == 0)
    def _():
        put(own, other)

    @pl.when(bit[0] != 0)
    def _():
        put(other, own)

    if gained:
        products = outs[0][...] * weights[...].astype(F32)
        sums = jnp.sum(products, axis=1, keepdims=True)
        row = jnp.broadcast_to(sums, (sums.shape[0], LANES)).T[:1]
        outs[-1][...] = (row / gain[...].astype(F32)).reshape(outs[-1].shape)


def unpack(chain, shapes, gained=()):
    own, other = chain.parts
    width = own.shape[1]
    places = [(k, shape[1] // width) for k, shape in enumerate(shapes)]
    if gained:
        shapes = shapes + [gained[1].shape[1:]]
    return pl.pallas_call(
        partial(unpack_kernel, places, bool(gained)),
        in_specs=[SMEM_SPEC] + [WHOLE] * (2 + len(gained)),
        out_shape=[jax.ShapeDtypeStruct(shape, F32) for shape in shapes],
        compiler_params=params(24),
        cost_estimate=cost(0, 12 * own.size),
        name="unpack",
    )(chain.bit.reshape(1), own, other, *gained)


def unrotated(block, cos, sin):
    return block * cos - halves_swapped(block) * sin


def row_pair(rows, at):
    index = lax.broadcasted_iota(jnp.int32, rows.shape, 0)
    picked = [
        jnp.sum(jnp.where(index == at + k, rows, 0.0), axis=0, keepdims=True) for k in (0, 1)
    ]
    return jnp.concatenate(picked, axis=1)


def attend_back_kernel(
    queries, keys_a, values_a, keys_b, values_b, grads, logs_deltas, cos, sin,
    out_queries, out_keys, out_values,
):
    pair = pl.program_id(0)
    rows, count = queries.shape[0], keys_a.shape[0]
    queries_two = two_heads(queries[...])
    grads_two = two_heads(grads[...])
    logs = row_pair(logs_deltas[...], 2 * pair)
    deltas = row_pair(logs_deltas[...], HEADS + 2 * pair)
    total = jnp.zeros((2 * rows, LANES), F32)
    for base, keys, values in ((0, keys_a, values_a), (count, keys_b, values_b)):
        for at in chunks_of(count):
            to = slice(base + at.start, base + at.stop)
            key_rows = keys[at, :]
            probs = jnp.exp(dot_nt(key_rows, queries_two) - logs)
            grad_probs = dot_nt(values[at, :], grads_two)
            grad_scores = (probs * (grad_probs - deltas)).astype(BF16)
            out_values[to, :] = dot_nn(probs.astype(BF16), grads_two).astype(BF16)
            grad_keys = dot_nn(grad_scores, queries_two)
            out_keys[to, :] = unrotated(grad_keys, cos[to, :], sin[to, :]).astype(BF16)
            total = total + dot_tn(grad_scores, key_rows)
    grad = one_pair(total) * 0.125
    out_queries[...] = unrotated(grad, cos[:rows, :], sin[:rows, :]).astype(BF16)


def attend_back(own_queries, halves, grads, logs_deltas, cos, sin):
    count = halves[0].shape[0]
    rows, width = own_queries.shape
    pairs = width // LANES
    queries = pl.BlockSpec((rows, LANES), lambda j: (0, j))
    shared = pl.BlockSpec((LANES, rows), lambda j: (0, 0))
    keys = pl.BlockSpec((count, LANES), lambda j: (0, j))
    values = pl.BlockSpec((count, LANES), lambda j: (0, pairs + j))
    table = pl.BlockSpec((2 * count, LANES), lambda j: (0, 0))
    made = pl.BlockSpec((2 * count, LANES), lambda j: (0, j))
    return pl.pallas_call(
        attend_back_kernel,
        grid=(pairs,),
        in_specs=[queries, keys, values, keys, values, queries, shared, table, table],
        out_specs=[queries, made, made],
        out_shape=[
            jax.ShapeDtypeStruct((rows, width), BF16),
            jax.ShapeDtypeStruct((2 * count, width), BF16),
            jax.ShapeDtypeStruct((2 * count, width), BF16),
        ],
        compiler_params=params(16 if count <= 1024 else 48),
        cost_estimate=cost(40 * rows * count * width, 20 * count * width),
        name="attend_back",
    )(
        own_queries, halves[0], halves[0], halves[1], halves[1],
        grads, logs_deltas, cos, sin,
    )


def late_rows_kernel(
    core, low_a, low_b, grad_q, grad_k, grad_v, out_own, out_other, total
):
    step, steps = pl.program_id(0), pl.num_programs(0)
    own_rows, width = grad_q.shape
    half = width // 2
    low = jnp.where(2 * step < steps, low_a[...], low_b[...])
    turned = low.T
    made_k, made_v = dot_nn(turned, grad_k[...]), dot_nn(turned, grad_v[...])

    @pl.when(step == 0)
    def _():
        total[:, :width] = dot_nn(turned[:, :own_rows], grad_q[...])
        total[:, width : 2 * width] = made_k
        total[:, 2 * width :] = made_v

    @pl.when(step > 0)
    def _():
        total[:, width : 2 * width] += made_k
        total[:, 2 * width :] += made_v

    @pl.when(step == steps - 1)
    def _():
        for out, side in ((out_own, core[0]), (out_other, 1 - core[0])):
            start = pl.multiple_of(side * half, half)
            for k in range(3):
                columns = slice(k * width, (k + 1) * width)
                out[k * half : (k + 1) * half, :] = total[pl.ds(start, half), columns].astype(BF16)
            if out.shape[0] > 3 * half:
                out[3 * half :, :] = jnp.zeros((out.shape[0] - 3 * half, width), BF16)


def late_rows(core, pieces, lows, grad_q, grad_k, grad_v):
    count, width = lows[0].shape
    own_rows = grad_q.shape[0]
    step = min(count, 512)
    each = count // step
    total = padded(3 * width // 2, pieces)
    grads = pl.BlockSpec((step, width), lambda i: (i, 0))
    fixed = pl.BlockSpec((own_rows, width), lambda i: (0, 0))
    made = pl.BlockSpec((total, width), lambda i: (0, 0))
    return pl.pallas_call(
        late_rows_kernel,
        grid=(2 * each,),
        in_specs=[
            SMEM_SPEC,
            pl.BlockSpec((step, width), lambda i: (jnp.minimum(i, each - 1), 0)),
            pl.BlockSpec((step, width), lambda i: (jnp.maximum(i - each, 0), 0)),
            fixed, grads, grads,
        ],
        out_specs=[made, made],
        out_shape=[jax.ShapeDtypeStruct((total, width), BF16)] * 2,
        scratch_shapes=[pltpu.VMEM((width, 3 * width), F32)],
        compiler_params=params(24),
        cost_estimate=cost(4 * count * width * width, 8 * count * width),
        name="late_rows",
    )(core, *lows, grad_q, grad_k, grad_v)


def first_rows_kernel(grad_q, grad_k, grad_v, weights, out):
    width = grad_q.shape[1]
    own_rows = grad_q.shape[0]
    made = dot_nt(grad_k[...], weights[:, width : 2 * width])
    made = made + dot_nt(grad_v[...], weights[:, 2 * width :])

    @pl.when(pl.program_id(0) == 0)
    def _():
        own = made[:own_rows] + dot_nt(grad_q[...], weights[:, :width])
        out[:own_rows, :] = own.astype(BF16)
        out[own_rows:, :] = made[own_rows:].astype(BF16)

    @pl.when(pl.program_id(0) > 0)
    def _():
        out[...] = made.astype(BF16)


def first_rows(grad_q, grad_k, grad_v, weights):
    rows, width = grad_k.shape
    own_rows = grad_q.shape[0]
    step = min(rows, 2 * own_rows)
    block = pl.BlockSpec((step, width), lambda i: (i, 0))
    return pl.pallas_call(
        first_rows_kernel,
        grid=(rows // step,),
        in_specs=[
            pl.BlockSpec((own_rows, width), lambda i: (0, 0)),
            block,
            block,
            pl.BlockSpec((width, 3 * width), lambda i: (0, 0)),
        ],
        out_specs=block,
        out_shape=jax.ShapeDtypeStruct((rows, width), BF16),
        compiler_params=params(16),
        cost_estimate=cost(4 * rows * width * width, 8 * rows * width),
        name="first_rows",
    )(grad_q, grad_k, grad_v, weights)


def last_kernel(tokens, grad_middle, part_a, part_b, gain, out):
    normed, rstd = normalize(tokens[...].astype(F32))
    grad_first = part_a[...].astype(F32) + part_b[...].astype(F32)
    back = norm_back(grad_first, normed, rstd, gain[...].astype(F32))
    out[...] = (grad_middle[...] + back).astype(BF16)


def last_part(tokens, grad_middle, parts, gain):
    return pl.pallas_call(
        last_kernel,
        out_shape=jax.ShapeDtypeStruct(tokens.shape, BF16),
        compiler_params=params(24),
        cost_estimate=cost(20 * tokens.size, 12 * tokens.size),
        name="last",
    )(tokens, grad_middle, *parts, gain)


def rotary_tables(positions, head_dim):
    half = head_dim // 2
    inverse = jnp.power(F32(THETA), -(jnp.arange(half, dtype=F32) * (2.0 / head_dim)))
    angles = positions[:, None] * inverse[None, :]
    cos, sin = jnp.cos(angles), jnp.sin(angles)
    return (
        jnp.concatenate([cos, cos, cos, cos], axis=1),
        jnp.concatenate([-sin, sin, -sin, sin], axis=1),
    )


def local(tokens, w_qkv, w_out, w_in, w_mlp, gain_attn, gain_mlp, cotangent):
    seqs_here, rows, width = tokens.shape
    half, half_ff = width // 2, FF // 2
    core = lax.axis_index("wsh")
    own = tokens.reshape(rows, width)
    upstream = cotangent.reshape(rows, width)
    pieces = lax.axis_size("seq") * lax.axis_size("ctx")

    gathered = gather_context(own)
    qkv_other = swap_cores(w_qkv)
    gains = jnp.stack([gain_attn, gain_mlp])
    gains_other = swap_cores(gains)
    gains_all = jnp.concatenate(
        [jnp.where(core == 0, gains, gains_other), jnp.where(core == 0, gains_other, gains)], axis=1
    )
    attn_gain, mlp_gain = gains_all[:1], gains_all[1:]
    full_out = both_halves(w_out)
    full_in = both_halves(w_in)
    full_mlp = both_halves(w_mlp)
    upstream_other = swap_cores(upstream)

    blocks = gathered_blocks()
    positions = (blocks[:, None] * rows + jnp.arange(rows, dtype=jnp.int32)[None, :]).reshape(-1)
    cos, sin = rotary_tables(positions.astype(F32), 64)
    count = gathered[0].shape[0]
    core_at = core.reshape(1)
    first_half, first_low, queries, full_qkv = project(
        core_at, gathered[0], w_qkv, qkv_other, attn_gain, cos[:count], sin[:count], rows
    )
    last_half, last_low = project(
        core_at, gathered[1], full_qkv, attn_gain, attn_gain, cos[count:], sin[count:], 0
    )
    halves = first_half, last_half
    attended, log_total = attend(queries, halves)
    (
        layer_out, own_halves, other_halves, whole, grad_middle, grads, logs_deltas,
    ) = middle_part(
        core_at, own, attended, log_total, upstream, full_out, full_in, full_mlp, mlp_gain
    )

    grad_q, grad_k, grad_v = attend_back(queries, halves, grads, logs_deltas, cos, sin)
    other_halves, whole_other = swap_cores(other_halves), swap_cores(whole)
    own_halves, grad_q = lax.optimization_barrier((own_halves, grad_q))
    mlp_rows, in_rows = grad_rows(
        pieces, width, own_halves, other_halves, upstream, upstream_other,
        whole, whole_other,
    )
    (grad_q,) = after([grad_q], mlp_rows, in_rows)
    late_own, late_other = late_rows(
        core_at, pieces, (first_low, last_low), grad_q, grad_k, grad_v
    )
    chains = [
        RowsSum([mlp_rows], MLP_ORDERS),
        RowsSum([in_rows], IN_ORDERS),
        RowsSum([late_own, swap_cores(late_other)], LATE_ORDERS),
    ]
    aways = lax.optimization_barrier(tuple(chain.first_away() for chain in chains))
    for chain, away in zip(chains, aways):
        chain.step(away)
    (grad_q,) = after([grad_q], *aways)
    chains.append(ContextSum(first_rows(grad_q, grad_k, grad_v, full_qkv)))
    while any(chain.left for chain in chains):
        for chain in chains:
            if chain.left:
                chain.step()
    mlp_grad, out_grad = unpack(chains[0], [(half_ff, width), (half, width)])
    in_grad, gain_mlp_grad = unpack(
        chains[1], [(half, 2 * FF)], (w_in, gain_mlp.reshape(1, half))
    )
    qkv_grad, gain_attn_grad = unpack(
        chains[2], [(half, 3 * width)], (w_qkv, gain_attn.reshape(1, half))
    )
    tokens_grad = last_part(own, grad_middle, chains[3].parts, attn_gain)
    return (
        layer_out.reshape(seqs_here, rows, width),
        tokens_grad.reshape(seqs_here, rows, width),
        qkv_grad,
        out_grad,
        in_grad,
        mlp_grad,
        gain_attn_grad,
        gain_mlp_grad,
    )


def solution(mesh):
    placed = (
        P(("seq", "wsh"), "ctx", None),
        P("wsh", None),
        P("wsh", None),
        P("wsh", None),
        P("wsh", None),
        P("wsh"),
        P("wsh"),
        P(("seq", "wsh"), "ctx", None),
    )
    return jax.shard_map(
        local,
        mesh=mesh,
        in_specs=placed,
        out_specs=(
            P(("seq", "wsh"), "ctx", None),
            P(("seq", "wsh"), "ctx", None),
            P("wsh", None),
            P("wsh", None),
            P("wsh", None),
            P("wsh", None),
            P("wsh"),
            P("wsh"),
        ),
        check_vma=False,
    )
```

```python
from functools import partial
import math

import jax
import jax.numpy as jnp
from jax import lax
from jax.experimental import pallas as pl
from jax.experimental.pallas import tpu as pltpu
from jax.sharding import PartitionSpec as P

HEADS = 12
FF = 1152
EPSILON = 1e-05
THETA = 160000.0
LANES = 128
NORMED_AT = 640
ATTENDED_AT = 1024
HALVES_WIDTH = 1408
MLP_ORDERS = ("xyab", "yxba")
IN_ORDERS = ("yxab", "xyab")
LATE_ORDERS = ("ayxb", "bxya")
MIB = 1 << 20
BF16 = jnp.bfloat16
F32 = jnp.float32


def bits_of(axis):
    return [(axis, k) for k in range((lax.axis_size(axis) - 1).bit_length())]


def my_bit(axis, k):
    return (lax.axis_index(axis) >> k) & 1


def flip(block, first, second):
    n_seq, n_ctx = lax.axis_size("seq"), lax.axis_size("ctx")
    route = []
    for s in range(n_seq):
        for t in range(n_ctx):
            for core, (axis, k) in enumerate((first, second)):
                s2, t2 = (s ^ (1 << k), t) if axis == "seq" else (s, t ^ (1 << k))
                route.append(((s * n_ctx + t) * 2 + core, (s2 * n_ctx + t2) * 2 + core))
    return lax.ppermute(block, ("seq", "ctx", "wsh"), route)


def swap_cores(block):
    return lax.ppermute(block, "wsh", [(0, 1), (1, 0)])


def gather_orders():
    bits = bits_of("ctx")
    return bits[::-1], bits[:1] + bits[:0:-1]


def gather_context(block):
    stages = list(zip(*gather_orders()))
    for first, second in stages[:-1]:
        block = jnp.concatenate([block, flip(block, first, second)], axis=0)
    return block, flip(block, *stages[-1])


class ContextSum:
    def __init__(self, rows):
        self.parts = [rows]
        self.stages = list(zip(*gather_orders()))[::-1]

    def step(self):
        half = self.parts[0].shape[0] // 2
        away, kept = (
            sum(part[at : at + half].astype(F32) for part in self.parts).astype(BF16)
            for at in (half, 0)
        )
        self.parts = [kept, flip(away, *self.stages.pop(0))]

    @property
    def left(self):
        return len(self.stages)


def gathered_blocks():
    tables = []
    for order in gather_orders():
        slots = [0]
        for _, k in order:
            slots = slots + [slot | (1 << k) for slot in slots]
        tables.append(slots)
    mine = jnp.where(lax.axis_index("wsh") == 0, jnp.array(tables[0]), jnp.array(tables[1]))
    return mine ^ lax.axis_index("ctx")


def sum_orders(orders):
    ctx = bits_of("ctx")
    bits = {"x": bits_of("seq"), "y": ctx[:1], "a": ctx[1:2], "b": ctx[2:]}
    return list(zip(*[sum((bits[letter] for letter in order), []) for order in orders]))


def stage_bit(first, second):
    return jnp.where(lax.axis_index("wsh") == 0, my_bit(*first), my_bit(*second))


def after(arrays, *made):
    return lax.optimization_barrier((*arrays, *made))[: len(arrays)]


class RowsSum:
    def __init__(self, parts, orders):
        self.parts = parts
        self.starts = [0] * len(parts)
        self.size = parts[0].shape[0]
        self.stages = sum_orders(orders)
        self.at = 0

    def summed(self, start, size):
        cut = [
            lax.dynamic_slice_in_dim(part, first + start, size, 0).astype(F32)
            for part, first in zip(self.parts, self.starts)
        ]
        return sum(cut[1:], cut[0]).astype(BF16)

    def first_away(self):
        return self.summed((1 - stage_bit(*self.stages[0])) * (self.size // 2), self.size // 2)

    def step(self, away=None):
        count, at = len(self.stages), self.at
        self.at += 1
        if at < count:
            stage = self.stages[at]
            bit = stage_bit(*stage)
            self.size //= 2
            if away is None:
                away = self.summed((1 - bit) * self.size, self.size)
            if at == 0:
                kept, starts = self.parts, [start + bit * self.size for start in self.starts]
            else:
                kept, starts = [self.summed(bit * self.size, self.size)], [0]
            self.parts = [*kept, flip(away, *stage)]
            self.starts = [*starts, 0]
            return
        stage = self.stages[2 * count - 1 - at]
        if at == count:
            rows = self.summed(0, self.size)
        else:
            own, other = self.parts
            low = jnp.where(self.bit == 0, own, other)
            high = jnp.where(self.bit == 0, other, own)
            rows = jnp.concatenate([low, high], axis=0)
        self.bit = stage_bit(*stage)
        self.parts = [rows, flip(rows, *stage)]

    @property
    def left(self):
        return 2 * len(self.stages) - self.at


def both_halves(block):
    other = swap_cores(block)
    core = lax.axis_index("wsh")
    return jnp.concatenate(
        [jnp.where(core == 0, block, other), jnp.where(core == 0, other, block)], axis=0
    )


def dot_nn(a, b):
    return lax.dot_general(a, b, (((1,), (0,)), ((), ())), preferred_element_type=F32)


def dot_nt(a, b):
    return lax.dot_general(a, b, (((1,), (1,)), ((), ())), preferred_element_type=F32)


def dot_tn(a, b):
    return lax.dot_general(a, b, (((0,), (0,)), ((), ())), preferred_element_type=F32)


SMEM_SPEC = pl.BlockSpec(memory_space=pltpu.SMEM)
WHOLE = pl.BlockSpec()


def cost(flops, moved):
    return pl.CostEstimate(flops=int(flops), bytes_accessed=int(moved), transcendentals=0)


def params(mib):
    return pltpu.CompilerParams(vmem_limit_bytes=mib * MIB)


def normalize(inputs):
    average = jnp.mean(inputs, axis=-1, keepdims=True)
    centred = inputs - average
    variance = jnp.mean(centred * centred, axis=-1, keepdims=True)
    rstd = lax.rsqrt(variance + EPSILON)
    return centred * rstd, rstd


def norm_back(grad_rows, normed, rstd, gain):
    scaled = grad_rows * gain
    inner = jnp.mean(scaled * normed, axis=-1, keepdims=True)
    return rstd * (scaled - jnp.mean(scaled, axis=-1, keepdims=True) - normed * inner)


def lane_of(shape):
    return lax.broadcasted_iota(jnp.int32, shape, len(shape) - 1)


def halves_swapped(vectors):
    first = (lane_of(vectors.shape) & 63) < 32
    return jnp.where(first, pltpu.roll(vectors, LANES - 32, 1), pltpu.roll(vectors, 32, 1))


def project_kernel(core, tokens, weights, other, gain, cos, sin, out, out_low, *more):
    width = tokens.shape[1]
    half = width // 2
    if more:
        queries, joined = more

        @pl.when(pl.program_id(0) == 0)
        def _():
            joined[pl.ds(pl.multiple_of(core[0] * half, half), half), :] = weights[...]
            joined[pl.ds(pl.multiple_of((1 - core[0]) * half, half), half), :] = other[...]

        weights = joined
    normed, _ = normalize(tokens[...].astype(F32))
    low = (normed * gain[...].astype(F32)).astype(BF16)
    out_low[...] = low

    def put(ref, start, rows, columns, turned, scale):
        for j in range(width // LANES):
            piece = columns[:, j * LANES : (j + 1) * LANES]
            if turned:
                piece = piece * cos[:rows, :] + halves_swapped(piece) * sin[:rows, :]
            ref[:, start + j * LANES : start + (j + 1) * LANES] = (piece * scale).astype(BF16)

    rows = tokens.shape[0]
    put(out, 0, rows, dot_nn(low, weights[:, width : 2 * width]), True, 1.0)
    put(out, width, rows, dot_nn(low, weights[:, 2 * width :]), False, 1.0)
    if more:

        @pl.when(pl.program_id(0) == 0)
        def _():
            own = queries.shape[0]
            put(queries, 0, own, dot_nn(low[:own], weights[:, :width]), True, 0.125)


def project(core, tokens, weights, other, gain, cos, sin, own_rows):
    rows, width = tokens.shape
    step = min(rows, 256)

    def fixed(shape):
        return pl.BlockSpec(shape, lambda i: (0, 0))

    out_specs = [
        pl.BlockSpec((step, 2 * width), lambda i: (i, 0)),
        pl.BlockSpec((step, width), lambda i: (i, 0)),
    ]
    out_shape = [
        jax.ShapeDtypeStruct((rows, 2 * width), BF16),
        jax.ShapeDtypeStruct((rows, width), BF16),
    ]
    if own_rows:
        out_specs += [fixed((own_rows, width)), fixed((width, 3 * width))]
        out_shape.append(jax.ShapeDtypeStruct((own_rows, width), BF16))
        out_shape.append(jax.ShapeDtypeStruct((width, 3 * width), BF16))
    return pl.pallas_call(
        project_kernel,
        grid=(rows // step,),
        in_specs=[
            SMEM_SPEC,
            pl.BlockSpec((step, width), lambda i: (i, 0)),
            fixed(weights.shape),
            fixed(other.shape),
            fixed((1, width)),
            pl.BlockSpec((step, LANES), lambda i: (i, 0)),
            pl.BlockSpec((step, LANES), lambda i: (i, 0)),
        ],
        out_specs=out_specs,
        out_shape=out_shape,
        compiler_params=params(28),
        cost_estimate=cost(4 * rows * width * width, 8 * rows * width),
        name="project",
    )(core, tokens, weights, other, gain, cos, sin)


def two_heads(block):
    first = lane_of(block.shape) < 64
    zero = jnp.zeros_like(block)
    return jnp.concatenate([jnp.where(first, block, zero), jnp.where(first, zero, block)], axis=0)


def one_pair(stacked):
    rows = stacked.shape[0] // 2
    return jnp.where(lane_of((rows, LANES)) < 64, stacked[:rows], stacked[rows:])


def column_pair(columns, at):
    lanes = lane_of(columns.shape)
    picked = [
        jnp.sum(jnp.where(lanes == at + k, columns, 0.0), axis=1, keepdims=True) for k in (0, 1)
    ]
    return jnp.concatenate(picked, axis=0)


def put_pair(ref, pair, values):
    rows = ref.shape[0]

    lanes = lane_of((rows, LANES))
    kept = jnp.where(lanes == 2 * pair, values[:rows], ref[...])
    ref[...] = jnp.where(lanes == 2 * pair + 1, values[rows:], kept)


def chunks_of(count):
    step = min(count, 1024)
    return [slice(at, at + step) for at in range(0, count, step)]


def attend_over(stacked, keys, values, lanes, peak, total, mixed):
    for at in chunks_of(keys.shape[0]):
        logits = dot_nt(stacked, keys[at, lanes])
        top = jnp.max(logits, axis=1, keepdims=True)
        if peak is None:
            weights = jnp.exp(logits - top)
            total = jnp.sum(weights, axis=1, keepdims=True)
            mixed = dot_nn(weights.astype(BF16), values[at, lanes])
        else:
            top = jnp.maximum(peak, top)
            weights = jnp.exp(logits - top)
            factor = jnp.exp(peak - top)
            total = total * factor + jnp.sum(weights, axis=1, keepdims=True)
            mixed = mixed * factor + dot_nn(weights.astype(BF16), values[at, lanes])
        peak = top
    return peak, total, mixed


def pairs_of(per, *shared):
    @pl.when(pl.program_id(0) == 0)
    def _():
        for ref in shared:
            ref[...] = jnp.zeros_like(ref)

    return [
        (pl.program_id(0) * per + p, slice(p * LANES, (p + 1) * LANES)) for p in range(per)
    ]


def attend_first_kernel(per, queries, keys, values, out_mixed, out_peak, out_total):
    for pair, lanes in pairs_of(per, out_peak, out_total):
        stacked = two_heads(queries[:, lanes])
        peak, total, mixed = attend_over(stacked, keys, values, lanes, None, None, None)
        out_mixed[:, lanes] = one_pair(mixed)
        put_pair(out_peak, pair, peak)
        put_pair(out_total, pair, total)


def attend_last_kernel(
    per, queries, keys, values, in_mixed, in_peak, in_total, attended, log_total
):
    for pair, lanes in pairs_of(per, log_total):
        stacked = two_heads(queries[:, lanes])
        peak = column_pair(in_peak[...], 2 * pair)
        total = column_pair(in_total[...], 2 * pair)
        mixed = jnp.concatenate([in_mixed[:, lanes]] * 2, axis=0)
        peak, total, mixed = attend_over(stacked, keys, values, lanes, peak, total, mixed)
        attended[:, lanes] = one_pair(mixed / total)
        put_pair(log_total, pair, peak + jnp.log(total))


def pairs_per_step(count, pairs):
    return pairs if count <= 1024 else 1


def attend(own_queries, halves):
    count = halves[0].shape[0]
    rows, width = own_queries.shape
    pairs = width // LANES
    per = pairs_per_step(count, pairs)
    steps, wide_lanes = pairs // per, per * LANES
    queries = pl.BlockSpec((rows, wide_lanes), lambda j: (0, j))
    shared = pl.BlockSpec((rows, LANES), lambda j: (0, 0))
    keys = pl.BlockSpec((count, wide_lanes), lambda j: (0, j))
    values = pl.BlockSpec((count, wide_lanes), lambda j: (0, steps + j))
    wide = jax.ShapeDtypeStruct((rows, width), F32)
    thin = jax.ShapeDtypeStruct((rows, LANES), F32)
    work = cost(8 * rows * count * width, 6 * count * width)
    mixed, peak, total = pl.pallas_call(
        partial(attend_first_kernel, per),
        grid=(steps,),
        in_specs=[queries, keys, values],
        out_specs=[queries, shared, shared],
        out_shape=[wide, thin, thin],
        compiler_params=params(24),
        cost_estimate=work,
        name="attend_first",
    )(own_queries, halves[0], halves[0])
    return pl.pallas_call(
        partial(attend_last_kernel, per),
        grid=(steps,),
        in_specs=[queries, keys, values, queries, shared, shared],
        out_specs=[queries, shared],
        out_shape=[wide, thin],
        compiler_params=params(24),
        cost_estimate=work,
        name="attend_last",
    )(own_queries, halves[1], halves[1], mixed, peak, total)


def middle_kernel(
    core, tokens, attended, log_total, cotangent, w_out, w_in, w_mlp, gain,
    layer_out, own_halves, other_halves, whole, grad_middle, grads, logs_deltas,
):

    rows, width = tokens.shape
    first = core[0] == 0

    def put_halves(at, block):
        half = block.shape[1] // 2
        left, right = block[:, :half], block[:, half:]
        own_halves[:, at : at + half] = jnp.where(first, left, right)
        other_halves[:, at : at + half] = jnp.where(first, right, left)

    mixed = attended[...]
    mixed_low = mixed.astype(BF16)
    put_halves(ATTENDED_AT, mixed_low)
    middle = tokens[...].astype(F32) + dot_nn(mixed_low, w_out[...])
    normed, rstd = normalize(middle)
    gain_row = gain[...].astype(F32)
    second = (normed * gain_row).astype(BF16)
    put_halves(NORMED_AT, second)
    gate = dot_nn(second, w_in[:, :FF])
    up = dot_nn(second, w_in[:, FF:])
    cdf = 0.5 * (1.0 + lax.erf(gate * (0.5**0.5)))
    activated = gate * cdf
    hidden = (activated * up).astype(BF16)
    put_halves(0, hidden)
    layer_out[...] = (middle + dot_nn(hidden, w_mlp[...])).astype(BF16)
    upstream = cotangent[...]
    grad_hidden = dot_nt(upstream, w_mlp[...]).astype(BF16).astype(F32)
    density = jnp.exp(-0.5 * gate * gate) * 0.3989422804014327
    grad_gate = (grad_hidden * up * (cdf + gate * density)).astype(BF16)
    grad_up = (grad_hidden * activated).astype(BF16)
    whole[:, :FF] = grad_gate
    whole[:, FF : 2 * FF] = grad_up
    grad_second = dot_nt(grad_gate, w_in[:, :FF]) + dot_nt(grad_up, w_in[:, FF:])
    grad_mid = upstream.astype(F32) + norm_back(grad_second, normed, rstd, gain_row)
    grad_middle[...] = grad_mid
    branch = grad_mid.astype(BF16)
    whole[:, 2 * FF :] = branch
    grad_attended = dot_nt(branch, w_out[...]).astype(BF16)
    grads[...] = grad_attended
    products = grad_attended.astype(F32) * mixed
    head = lax.broadcasted_iota(jnp.int32, (width, LANES), 0) // 64
    to_lane = (lane_of((width, LANES)) == head + HEADS).astype(F32)
    both = log_total[...] + lax.dot_general(
        products,
        to_lane,
        (((1,), (0,)), ((), ())),
        precision=lax.Precision.HIGHEST,
        preferred_element_type=F32,
    )
    logs_deltas[...] = both.T


def middle_part(core, tokens, attended, log_total, cotangent, w_out, w_in, w_mlp, gain):
    rows, width = tokens.shape
    wide, halves = (rows, width), (rows, HALVES_WIDTH)
    shapes = [
        (wide, BF16), (halves, BF16), (halves, BF16), ((rows, 2 * FF + width), BF16),
        (wide, F32), (wide, BF16), ((LANES, rows), F32),
    ]
    return pl.pallas_call(
        middle_kernel,
        in_specs=[SMEM_SPEC] + [WHOLE] * 8,
        out_shape=[jax.ShapeDtypeStruct(*shape) for shape in shapes],
        compiler_params=params(32),
        cost_estimate=cost(4 * rows * width * (2 * width + 6 * FF), 24 * MIB),
        name="middle",
    )(core, tokens, attended, log_total, cotangent, w_out, w_in, w_mlp, gain)


def rows_kernel(own, other, upstream, upstream_other, whole, whole_other, out_mlp, out_in):
    width = out_mlp.shape[1]
    half, half_ff = width // 2, FF // 2
    both = jnp.concatenate([own[...], other[...]], axis=0)
    right = jnp.concatenate([upstream[...], upstream_other[...]], axis=0)
    out_mlp[:half_ff, :] = dot_tn(both[:, :half_ff], right).astype(BF16)
    branch = jnp.concatenate([whole[:, 2 * FF :], whole_other[:, 2 * FF :]], axis=0)
    left = both[:, ATTENDED_AT : ATTENDED_AT + half]
    out_mlp[half_ff : half_ff + half, :] = dot_tn(left, branch).astype(BF16)
    turned = both[:, NORMED_AT : NORMED_AT + half].T
    for k in range(2 * FF // width):
        lanes = slice(k * width, (k + 1) * width)
        right = jnp.concatenate([whole[:, lanes], whole_other[:, lanes]], axis=0)
        out_in[k * half : (k + 1) * half, :] = dot_nn(turned, right).astype(BF16)
    for out, used in ((out_mlp, half_ff + half), (out_in, 2 * FF // width * half)):
        if used < out.shape[0]:
            out[used:, :] = jnp.zeros((out.shape[0] - used, width), BF16)


def padded(rows, pieces):
    unit = 8 * pieces
    return (rows + unit - 1) // unit * unit


def grad_rows(pieces, width, *arrays):
    sizes = padded((FF + width) // 2, pieces), padded(FF, pieces)
    return pl.pallas_call(
        rows_kernel,
        out_shape=[jax.ShapeDtypeStruct((size, width), BF16) for size in sizes],
        compiler_params=params(16),
        cost_estimate=cost(512 * 1728 * width, 12 * MIB),
        name="grad_rows",
    )(*arrays)


def unpack_kernel(places, gained, bit, own, other, *refs):
    half = own.shape[0]
    if gained:
        weights, gain = refs[:2]
    outs = refs[2:] if gained else refs

    def put(low, high):
        at = 0
        for out, blocks in places:
            ref = outs[out]
            made = ref.shape[0]
            for k in range(blocks):
                columns = slice(k * low.shape[1], (k + 1) * low.shape[1])
                cut = min(max(half - at, 0), made)
                if cut > 0:
                    ref[:cut, columns] = low[at : at + cut, :].astype(F32)
                if cut < made:
                    start = at + cut - half
                    ref[cut:, columns] = high[start : start + made - cut, :].astype(F32)
                at += made

    @pl.when(bit[0] == 0)
    def _():
        put(own, other)

    @pl.when(bit[0] != 0)
    def _():
        put(other, own)

    if gained:
        products = outs[0][...] * weights[...].astype(F32)
        sums = jnp.sum(products, axis=1, keepdims=True)
        row = jnp.broadcast_to(sums, (sums.shape[0], LANES)).T[:1]
        outs[-1][...] = (row / gain[...].astype(F32)).reshape(outs[-1].shape)


def unpack(chain, shapes, gained=()):
    own, other = chain.parts
    width = own.shape[1]
    places = [(k, shape[1] // width) for k, shape in enumerate(shapes)]
    if gained:
        shapes = shapes + [gained[1].shape[1:]]
    return pl.pallas_call(
        partial(unpack_kernel, places, bool(gained)),
        in_specs=[SMEM_SPEC] + [WHOLE] * (2 + len(gained)),
        out_shape=[jax.ShapeDtypeStruct(shape, F32) for shape in shapes],
        compiler_params=params(24),
        cost_estimate=cost(0, 12 * own.size),
        name="unpack",
    )(chain.bit.reshape(1), own, other, *gained)


def unrotated(block, cos, sin):
    return block * cos - halves_swapped(block) * sin


def row_pair(rows, at):
    index = lax.broadcasted_iota(jnp.int32, rows.shape, 0)
    picked = [
        jnp.sum(jnp.where(index == at + k, rows, 0.0), axis=0, keepdims=True) for k in (0, 1)
    ]
    return jnp.concatenate(picked, axis=1)


def attend_back_kernel(
    per, queries, keys_a, values_a, keys_b, values_b, grads, logs_deltas, cos, sin,
    out_queries, out_keys, out_values,
):
    rows, count = queries.shape[0], keys_a.shape[0]
    for pair, lanes in pairs_of(per):
        queries_two = two_heads(queries[:, lanes])
        grads_two = two_heads(grads[:, lanes])
        logs = row_pair(logs_deltas[...], 2 * pair)
        deltas = row_pair(logs_deltas[...], HEADS + 2 * pair)
        total = jnp.zeros((2 * rows, LANES), F32)
        for base, keys, values in ((0, keys_a, values_a), (count, keys_b, values_b)):
            for at in chunks_of(count):
                to = slice(base + at.start, base + at.stop)
                key_rows = keys[at, lanes]
                probs = jnp.exp(dot_nt(key_rows, queries_two) - logs)
                grad_probs = dot_nt(values[at, lanes], grads_two)
                grad_scores = (probs * (grad_probs - deltas)).astype(BF16)
                out_values[to, lanes] = dot_nn(probs.astype(BF16), grads_two).astype(BF16)
                grad_keys = dot_nn(grad_scores, queries_two)
                out_keys[to, lanes] = unrotated(grad_keys, cos[to, :], sin[to, :]).astype(BF16)
                total = total + dot_tn(grad_scores, key_rows)
        grad = one_pair(total) * 0.125
        out_queries[:, lanes] = unrotated(grad, cos[:rows, :], sin[:rows, :]).astype(BF16)


def attend_back(own_queries, halves, grads, logs_deltas, cos, sin):
    count = halves[0].shape[0]
    rows, width = own_queries.shape
    pairs = width // LANES
    per = pairs_per_step(count, pairs)
    steps, wide_lanes = pairs // per, per * LANES
    queries = pl.BlockSpec((rows, wide_lanes), lambda j: (0, j))
    shared = pl.BlockSpec((LANES, rows), lambda j: (0, 0))
    keys = pl.BlockSpec((count, wide_lanes), lambda j: (0, j))
    values = pl.BlockSpec((count, wide_lanes), lambda j: (0, steps + j))
    table = pl.BlockSpec((2 * count, LANES), lambda j: (0, 0))
    made = pl.BlockSpec((2 * count, wide_lanes), lambda j: (0, j))
    return pl.pallas_call(
        partial(attend_back_kernel, per),
        grid=(steps,),
        in_specs=[queries, keys, values, keys, values, queries, shared, table, table],
        out_specs=[queries, made, made],
        out_shape=[
            jax.ShapeDtypeStruct((rows, width), BF16),
            jax.ShapeDtypeStruct((2 * count, width), BF16),
            jax.ShapeDtypeStruct((2 * count, width), BF16),
        ],
        compiler_params=params(16 if count <= 1024 else 48),
        cost_estimate=cost(40 * rows * count * width, 20 * count * width),
        name="attend_back",
    )(
        own_queries, halves[0], halves[0], halves[1], halves[1],
        grads, logs_deltas, cos, sin,
    )


def late_rows_kernel(
    core, low_a, low_b, grad_q, grad_k, grad_v, out_own, out_other, total
):
    step, steps = pl.program_id(0), pl.num_programs(0)
    own_rows, width = grad_q.shape
    half = width // 2
    low = jnp.where(2 * step < steps, low_a[...], low_b[...])
    turned = low.T
    made_k, made_v = dot_nn(turned, grad_k[...]), dot_nn(turned, grad_v[...])

    @pl.when(step == 0)
    def _():
        total[:, :width] = dot_nn(turned[:, :own_rows], grad_q[...])
        total[:, width : 2 * width] = made_k
        total[:, 2 * width :] = made_v

    @pl.when(step > 0)
    def _():
        total[:, width : 2 * width] += made_k
        total[:, 2 * width :] += made_v

    @pl.when(step == steps - 1)
    def _():
        for out, side in ((out_own, core[0]), (out_other, 1 - core[0])):
            start = pl.multiple_of(side * half, half)
            for k in range(3):
                columns = slice(k * width, (k + 1) * width)
                out[k * half : (k + 1) * half, :] = total[pl.ds(start, half), columns].astype(BF16)
            if out.shape[0] > 3 * half:
                out[3 * half :, :] = jnp.zeros((out.shape[0] - 3 * half, width), BF16)


def late_rows_whole_kernel(
    core, low_a, low_b, grad_q, grad_k, grad_v, out_own, out_other, turned
):
    count, width = low_a.shape
    half, own_rows = width // 2, grad_q.shape[0]
    turned[:, :count] = low_a[...].T
    turned[:, count:] = low_b[...].T
    for out, side in ((out_own, core[0]), (out_other, 1 - core[0])):
        left = turned[pl.ds(pl.multiple_of(side * half, half), half), :]
        out[:half, :] = dot_nn(left[:, :own_rows], grad_q[...]).astype(BF16)
        out[half : 2 * half, :] = dot_nn(left, grad_k[...]).astype(BF16)
        out[2 * half : 3 * half, :] = dot_nn(left, grad_v[...]).astype(BF16)
        if out.shape[0] > 3 * half:
            out[3 * half :, :] = jnp.zeros((out.shape[0] - 3 * half, width), BF16)


def late_rows(core, pieces, lows, grad_q, grad_k, grad_v):
    count, width = lows[0].shape
    own_rows = grad_q.shape[0]
    step = min(count, 512)
    each = count // step
    total = padded(3 * width // 2, pieces)
    if each == 1:
        return pl.pallas_call(
            late_rows_whole_kernel,
            in_specs=[SMEM_SPEC] + [WHOLE] * 5,
            out_shape=[jax.ShapeDtypeStruct((total, width), BF16)] * 2,
            scratch_shapes=[pltpu.VMEM((width, 2 * count), BF16)],
            compiler_params=params(16),
            cost_estimate=cost(4 * count * width * width, 8 * count * width),
            name="late_rows",
        )(core, *lows, grad_q, grad_k, grad_v)
    grads = pl.BlockSpec((step, width), lambda i: (i, 0))
    fixed = pl.BlockSpec((own_rows, width), lambda i: (0, 0))
    made = pl.BlockSpec((total, width), lambda i: (0, 0))
    return pl.pallas_call(
        late_rows_kernel,
        grid=(2 * each,),
        in_specs=[
            SMEM_SPEC,
            pl.BlockSpec((step, width), lambda i: (jnp.minimum(i, each - 1), 0)),
            pl.BlockSpec((step, width), lambda i: (jnp.maximum(i - each, 0), 0)),
            fixed, grads, grads,
        ],
        out_specs=[made, made],
        out_shape=[jax.ShapeDtypeStruct((total, width), BF16)] * 2,
        scratch_shapes=[pltpu.VMEM((width, 3 * width), F32)],
        compiler_params=params(24),
        cost_estimate=cost(4 * count * width * width, 8 * count * width),
        name="late_rows",
    )(core, *lows, grad_q, grad_k, grad_v)


def first_rows_kernel(grad_q, grad_k, grad_v, weights, out):
    width = grad_q.shape[1]
    own_rows = grad_q.shape[0]
    made = dot_nt(grad_k[...], weights[:, width : 2 * width])
    made = made + dot_nt(grad_v[...], weights[:, 2 * width :])

    @pl.when(pl.program_id(0) == 0)
    def _():
        own = made[:own_rows] + dot_nt(grad_q[...], weights[:, :width])
        out[:own_rows, :] = own.astype(BF16)
        out[own_rows:, :] = made[own_rows:].astype(BF16)

    @pl.when(pl.program_id(0) > 0)
    def _():
        out[...] = made.astype(BF16)


def first_rows(grad_q, grad_k, grad_v, weights):
    rows, width = grad_k.shape
    own_rows = grad_q.shape[0]
    step = min(rows, 2 * own_rows)
    block = pl.BlockSpec((step, width), lambda i: (i, 0))
    return pl.pallas_call(
        first_rows_kernel,
        grid=(rows // step,),
        in_specs=[
            pl.BlockSpec((own_rows, width), lambda i: (0, 0)),
            block,
            block,
            pl.BlockSpec((width, 3 * width), lambda i: (0, 0)),
        ],
        out_specs=block,
        out_shape=jax.ShapeDtypeStruct((rows, width), BF16),
        compiler_params=params(16),
        cost_estimate=cost(4 * rows * width * width, 8 * rows * width),
        name="first_rows",
    )(grad_q, grad_k, grad_v, weights)


def last_kernel(tokens, grad_middle, part_a, part_b, gain, out):
    normed, rstd = normalize(tokens[...].astype(F32))
    grad_first = part_a[...].astype(F32) + part_b[...].astype(F32)
    back = norm_back(grad_first, normed, rstd, gain[...].astype(F32))
    out[...] = (grad_middle[...] + back).astype(BF16)


def last_part(tokens, grad_middle, parts, gain):
    return pl.pallas_call(
        last_kernel,
        out_shape=jax.ShapeDtypeStruct(tokens.shape, BF16),
        compiler_params=params(24),
        cost_estimate=cost(20 * tokens.size, 12 * tokens.size),
        name="last",
    )(tokens, grad_middle, *parts, gain)


def rotary_tables(positions, head_dim):
    half = head_dim // 2
    inverse = jnp.power(F32(THETA), -(jnp.arange(half, dtype=F32) * (2.0 / head_dim)))
    angles = positions[:, None] * inverse[None, :]
    cos, sin = jnp.cos(angles), jnp.sin(angles)
    return (
        jnp.concatenate([cos, cos, cos, cos], axis=1),
        jnp.concatenate([-sin, sin, -sin, sin], axis=1),
    )


def local(tokens, w_qkv, w_out, w_in, w_mlp, gain_attn, gain_mlp, cotangent):
    seqs_here, rows, width = tokens.shape
    half, half_ff = width // 2, FF // 2
    core = lax.axis_index("wsh")
    own = tokens.reshape(rows, width)
    upstream = cotangent.reshape(rows, width)
    pieces = lax.axis_size("seq") * lax.axis_size("ctx")

    gathered = gather_context(own)
    qkv_other = swap_cores(w_qkv)
    gains = jnp.stack([gain_attn, gain_mlp])
    gains_other = swap_cores(gains)
    gains_all = jnp.concatenate(
        [jnp.where(core == 0, gains, gains_other), jnp.where(core == 0, gains_other, gains)], axis=1
    )
    attn_gain, mlp_gain = gains_all[:1], gains_all[1:]
    full_out = both_halves(w_out)
    full_in = both_halves(w_in)
    full_mlp = both_halves(w_mlp)
    upstream_other = swap_cores(upstream)

    blocks = gathered_blocks()
    positions = (blocks[:, None] * rows + jnp.arange(rows, dtype=jnp.int32)[None, :]).reshape(-1)
    cos, sin = rotary_tables(positions.astype(F32), 64)
    count = gathered[0].shape[0]
    core_at = core.reshape(1)
    first_half, first_low, queries, full_qkv = project(
        core_at, gathered[0], w_qkv, qkv_other, attn_gain, cos[:count], sin[:count], rows
    )
    last_half, last_low = project(
        core_at, gathered[1], full_qkv, attn_gain, attn_gain, cos[count:], sin[count:], 0
    )
    halves = first_half, last_half
    attended, log_total = attend(queries, halves)
    (
        layer_out, own_halves, other_halves, whole, grad_middle, grads, logs_deltas,
    ) = middle_part(
        core_at, own, attended, log_total, upstream, full_out, full_in, full_mlp, mlp_gain
    )

    grad_q, grad_k, grad_v = attend_back(queries, halves, grads, logs_deltas, cos, sin)
    other_halves, whole_other = swap_cores(other_halves), swap_cores(whole)
    own_halves, grad_q = lax.optimization_barrier((own_halves, grad_q))
    mlp_rows, in_rows = grad_rows(
        pieces, width, own_halves, other_halves, upstream, upstream_other,
        whole, whole_other,
    )
    (grad_q,) = after([grad_q], mlp_rows, in_rows)
    late_own, late_other = late_rows(
        core_at, pieces, (first_low, last_low), grad_q, grad_k, grad_v
    )
    chains = [
        RowsSum([mlp_rows], MLP_ORDERS),
        RowsSum([in_rows], IN_ORDERS),
        RowsSum([late_own, swap_cores(late_other)], LATE_ORDERS),
    ]
    aways = lax.optimization_barrier(tuple(chain.first_away() for chain in chains))
    for chain, away in zip(chains, aways):
        chain.step(away)
    (grad_q,) = after([grad_q], *aways)
    chains.append(ContextSum(first_rows(grad_q, grad_k, grad_v, full_qkv)))
    while any(chain.left for chain in chains):
        for chain in chains:
            if chain.left:
                chain.step()
    mlp_grad, out_grad = unpack(chains[0], [(half_ff, width), (half, width)])
    in_grad, gain_mlp_grad = unpack(
        chains[1], [(half, 2 * FF)], (w_in, gain_mlp.reshape(1, half))
    )
    qkv_grad, gain_attn_grad = unpack(
        chains[2], [(half, 3 * width)], (w_qkv, gain_attn.reshape(1, half))
    )
    tokens_grad = last_part(own, grad_middle, chains[3].parts, attn_gain)
    return (
        layer_out.reshape(seqs_here, rows, width),
        tokens_grad.reshape(seqs_here, rows, width),
        qkv_grad,
        out_grad,
        in_grad,
        mlp_grad,
        gain_attn_grad,
        gain_mlp_grad,
    )


def solution(mesh):
    placed = (
        P(("seq", "wsh"), "ctx", None),
        P("wsh", None),
        P("wsh", None),
        P("wsh", None),
        P("wsh", None),
        P("wsh"),
        P("wsh"),
        P(("seq", "wsh"), "ctx", None),
    )
    return jax.shard_map(
        local,
        mesh=mesh,
        in_specs=placed,
        out_specs=(
            P(("seq", "wsh"), "ctx", None),
            P(("seq", "wsh"), "ctx", None),
            P("wsh", None),
            P("wsh", None),
            P("wsh", None),
            P("wsh", None),
            P("wsh"),
            P("wsh"),
        ),
        check_vma=False,
    )
```

```python
from functools import partial
import math

import jax
import jax.numpy as jnp
from jax import lax
from jax.experimental import pallas as pl
from jax.experimental.pallas import tpu as pltpu
from jax.sharding import PartitionSpec as P

HEADS = 12
FF = 1152
EPSILON = 1e-05
THETA = 160000.0
LANES = 128
NORMED_AT = 640
ATTENDED_AT = 1024
HALVES_WIDTH = 1408
MLP_ORDERS = ("xyab", "yxba")
IN_ORDERS = ("yxab", "xyab")
LATE_ORDERS = ("ayxb", "bxya")
MIB = 1 << 20
BF16 = jnp.bfloat16
F32 = jnp.float32


def bits_of(axis):
    return [(axis, k) for k in range((lax.axis_size(axis) - 1).bit_length())]


def my_bit(axis, k):
    return (lax.axis_index(axis) >> k) & 1


def flip(block, first, second):
    n_seq, n_ctx = lax.axis_size("seq"), lax.axis_size("ctx")
    route = []
    for s in range(n_seq):
        for t in range(n_ctx):
            for core, (axis, k) in enumerate((first, second)):
                s2, t2 = (s ^ (1 << k), t) if axis == "seq" else (s, t ^ (1 << k))
                route.append(((s * n_ctx + t) * 2 + core, (s2 * n_ctx + t2) * 2 + core))
    return lax.ppermute(block, ("seq", "ctx", "wsh"), route)


def swap_cores(block):
    return lax.ppermute(block, "wsh", [(0, 1), (1, 0)])


def gather_orders():
    bits = bits_of("ctx")
    return bits[::-1], bits[:1] + bits[:0:-1]


def gather_context(block):
    stages = list(zip(*gather_orders()))
    for first, second in stages[:-1]:
        block = jnp.concatenate([block, flip(block, first, second)], axis=0)
    return block, flip(block, *stages[-1])


class ContextSum:
    def __init__(self, rows):
        self.parts = [rows]
        self.stages = list(zip(*gather_orders()))[::-1]

    def step(self):
        half = self.parts[0].shape[0] // 2
        away, kept = (
            sum(part[at : at + half].astype(F32) for part in self.parts).astype(BF16)
            for at in (half, 0)
        )
        self.parts = [kept, flip(away, *self.stages.pop(0))]

    @property
    def left(self):
        return len(self.stages)


def gathered_blocks():
    tables = []
    for order in gather_orders():
        slots = [0]
        for _, k in order:
            slots = slots + [slot | (1 << k) for slot in slots]
        tables.append(slots)
    mine = jnp.where(lax.axis_index("wsh") == 0, jnp.array(tables[0]), jnp.array(tables[1]))
    return mine ^ lax.axis_index("ctx")


def sum_orders(orders):
    ctx = bits_of("ctx")
    bits = {"x": bits_of("seq"), "y": ctx[:1], "a": ctx[1:2], "b": ctx[2:]}
    return list(zip(*[sum((bits[letter] for letter in order), []) for order in orders]))


def stage_bit(first, second):
    return jnp.where(lax.axis_index("wsh") == 0, my_bit(*first), my_bit(*second))


def after(arrays, *made):
    return lax.optimization_barrier((*arrays, *made))[: len(arrays)]


class RowsSum:
    def __init__(self, parts, orders):
        self.parts = parts
        self.starts = [0] * len(parts)
        self.size = parts[0].shape[0]
        self.stages = sum_orders(orders)
        self.at = 0

    def summed(self, start, size):
        cut = [
            lax.dynamic_slice_in_dim(part, first + start, size, 0).astype(F32)
            for part, first in zip(self.parts, self.starts)
        ]
        return sum(cut[1:], cut[0]).astype(BF16)

    def first_away(self):
        return self.summed((1 - stage_bit(*self.stages[0])) * (self.size // 2), self.size // 2)

    def step(self, away=None):
        count, at = len(self.stages), self.at
        self.at += 1
        if at < count:
            stage = self.stages[at]
            bit = stage_bit(*stage)
            self.size //= 2
            if away is None:
                away = self.summed((1 - bit) * self.size, self.size)
            if at == 0:
                kept, starts = self.parts, [start + bit * self.size for start in self.starts]
            else:
                kept, starts = [self.summed(bit * self.size, self.size)], [0]
            self.parts = [*kept, flip(away, *stage)]
            self.starts = [*starts, 0]
            return
        stage = self.stages[2 * count - 1 - at]
        if at == count:
            rows = self.summed(0, self.size)
        else:
            own, other = self.parts
            low = jnp.where(self.bit == 0, own, other)
            high = jnp.where(self.bit == 0, other, own)
            rows = jnp.concatenate([low, high], axis=0)
        self.bit = stage_bit(*stage)
        self.parts = [rows, flip(rows, *stage)]

    @property
    def left(self):
        return 2 * len(self.stages) - self.at


def both_halves(block):
    other = swap_cores(block)
    core = lax.axis_index("wsh")
    return jnp.concatenate(
        [jnp.where(core == 0, block, other), jnp.where(core == 0, other, block)], axis=0
    )


def dot_nn(a, b):
    return lax.dot_general(a, b, (((1,), (0,)), ((), ())), preferred_element_type=F32)


def dot_nt(a, b):
    return lax.dot_general(a, b, (((1,), (1,)), ((), ())), preferred_element_type=F32)


def dot_tn(a, b):
    return lax.dot_general(a, b, (((0,), (0,)), ((), ())), preferred_element_type=F32)


SMEM_SPEC = pl.BlockSpec(memory_space=pltpu.SMEM)
WHOLE = pl.BlockSpec()


def cost(flops, moved):
    return pl.CostEstimate(flops=int(flops), bytes_accessed=int(moved), transcendentals=0)


def params(mib):
    return pltpu.CompilerParams(vmem_limit_bytes=mib * MIB)


def normalize(inputs):
    average = jnp.mean(inputs, axis=-1, keepdims=True)
    centred = inputs - average
    variance = jnp.mean(centred * centred, axis=-1, keepdims=True)
    rstd = lax.rsqrt(variance + EPSILON)
    return centred * rstd, rstd


def norm_back(grad_rows, normed, rstd, gain):
    scaled = grad_rows * gain
    inner = jnp.mean(scaled * normed, axis=-1, keepdims=True)
    return rstd * (scaled - jnp.mean(scaled, axis=-1, keepdims=True) - normed * inner)


def lane_of(shape):
    return lax.broadcasted_iota(jnp.int32, shape, len(shape) - 1)


def halves_swapped(vectors):
    first = (lane_of(vectors.shape) & 63) < 32
    return jnp.where(first, pltpu.roll(vectors, LANES - 32, 1), pltpu.roll(vectors, 32, 1))


def project_kernel(core, tokens, weights, other, gain, cos, sin, out, out_low, *more):
    width = tokens.shape[1]
    half = width // 2
    if more:
        queries, joined = more

        @pl.when(pl.program_id(0) == 0)
        def _():
            joined[pl.ds(pl.multiple_of(core[0] * half, half), half), :] = weights[...]
            joined[pl.ds(pl.multiple_of((1 - core[0]) * half, half), half), :] = other[...]

        weights = joined
    normed, _ = normalize(tokens[...].astype(F32))
    low = (normed * gain[...].astype(F32)).astype(BF16)
    out_low[...] = low

    def put(ref, start, rows, columns, turned, scale):
        for j in range(width // LANES):
            piece = columns[:, j * LANES : (j + 1) * LANES]
            if turned:
                piece = piece * cos[:rows, :] + halves_swapped(piece) * sin[:rows, :]
            ref[:, start + j * LANES : start + (j + 1) * LANES] = (piece * scale).astype(BF16)

    rows = tokens.shape[0]
    put(out, 0, rows, dot_nn(low, weights[:, width : 2 * width]), True, 1.0)
    put(out, width, rows, dot_nn(low, weights[:, 2 * width :]), False, 1.0)
    if more:

        @pl.when(pl.program_id(0) == 0)
        def _():
            own = queries.shape[0]
            put(queries, 0, own, dot_nn(low[:own], weights[:, :width]), True, 0.125)


def project(core, tokens, weights, other, gain, cos, sin, own_rows):
    rows, width = tokens.shape
    step = min(rows, 512)

    def fixed(shape):
        return pl.BlockSpec(shape, lambda i: (0, 0))

    out_specs = [
        pl.BlockSpec((step, 2 * width), lambda i: (i, 0)),
        pl.BlockSpec((step, width), lambda i: (i, 0)),
    ]
    out_shape = [
        jax.ShapeDtypeStruct((rows, 2 * width), BF16),
        jax.ShapeDtypeStruct((rows, width), BF16),
    ]
    if own_rows:
        out_specs += [fixed((own_rows, width)), fixed((width, 3 * width))]
        out_shape.append(jax.ShapeDtypeStruct((own_rows, width), BF16))
        out_shape.append(jax.ShapeDtypeStruct((width, 3 * width), BF16))
    return pl.pallas_call(
        project_kernel,
        grid=(rows // step,),
        in_specs=[
            SMEM_SPEC,
            pl.BlockSpec((step, width), lambda i: (i, 0)),
            fixed(weights.shape),
            fixed(other.shape),
            fixed((1, width)),
            pl.BlockSpec((step, LANES), lambda i: (i, 0)),
            pl.BlockSpec((step, LANES), lambda i: (i, 0)),
        ],
        out_specs=out_specs,
        out_shape=out_shape,
        compiler_params=params(28),
        cost_estimate=cost(4 * rows * width * width, 8 * rows * width),
        name="project",
    )(core, tokens, weights, other, gain, cos, sin)


def two_heads(block):
    first = lane_of(block.shape) < 64
    zero = jnp.zeros_like(block)
    return jnp.concatenate([jnp.where(first, block, zero), jnp.where(first, zero, block)], axis=0)


def one_pair(stacked):
    rows = stacked.shape[0] // 2
    return jnp.where(lane_of((rows, LANES)) < 64, stacked[:rows], stacked[rows:])


def column_pair(columns, at):
    lanes = lane_of(columns.shape)
    picked = [
        jnp.sum(jnp.where(lanes == at + k, columns, 0.0), axis=1, keepdims=True) for k in (0, 1)
    ]
    return jnp.concatenate(picked, axis=0)


def put_pair(ref, pair, values):
    rows = ref.shape[0]

    lanes = lane_of((rows, LANES))
    kept = jnp.where(lanes == 2 * pair, values[:rows], ref[...])
    ref[...] = jnp.where(lanes == 2 * pair + 1, values[rows:], kept)


def chunks_of(count):
    step = min(count, 1024)
    return [slice(at, at + step) for at in range(0, count, step)]


def attend_over(stacked, keys, values, lanes, peak, total, mixed):
    for at in chunks_of(keys.shape[0]):
        logits = dot_nt(stacked, keys[at, lanes])
        top = jnp.max(logits, axis=1, keepdims=True)
        if peak is None:
            weights = jnp.exp(logits - top)
            total = jnp.sum(weights, axis=1, keepdims=True)
            mixed = dot_nn(weights.astype(BF16), values[at, lanes])
        else:
            top = jnp.maximum(peak, top)
            weights = jnp.exp(logits - top)
            factor = jnp.exp(peak - top)
            total = total * factor + jnp.sum(weights, axis=1, keepdims=True)
            mixed = mixed * factor + dot_nn(weights.astype(BF16), values[at, lanes])
        peak = top
    return peak, total, mixed


def pairs_of(per, *shared):
    @pl.when(pl.program_id(0) == 0)
    def _():
        for ref in shared:
            ref[...] = jnp.zeros_like(ref)

    return [
        (pl.program_id(0) * per + p, slice(p * LANES, (p + 1) * LANES)) for p in range(per)
    ]


def attend_first_kernel(per, queries, keys, values, out_mixed, out_peak, out_total):
    for pair, lanes in pairs_of(per, out_peak, out_total):
        stacked = two_heads(queries[:, lanes])
        peak, total, mixed = attend_over(stacked, keys, values, lanes, None, None, None)
        out_mixed[:, lanes] = one_pair(mixed)
        put_pair(out_peak, pair, peak)
        put_pair(out_total, pair, total)


def attend_last_kernel(
    per, queries, keys, values, in_mixed, in_peak, in_total, attended, log_total
):
    for pair, lanes in pairs_of(per, log_total):
        stacked = two_heads(queries[:, lanes])
        peak = column_pair(in_peak[...], 2 * pair)
        total = column_pair(in_total[...], 2 * pair)
        mixed = jnp.concatenate([in_mixed[:, lanes]] * 2, axis=0)
        peak, total, mixed = attend_over(stacked, keys, values, lanes, peak, total, mixed)
        attended[:, lanes] = one_pair(mixed / total)
        put_pair(log_total, pair, peak + jnp.log(total))


def pairs_per_step(count, pairs):
    return pairs if count <= 1024 else 1


def attend(own_queries, halves):
    count = halves[0].shape[0]
    rows, width = own_queries.shape
    pairs = width // LANES
    per = pairs_per_step(count, pairs)
    steps, wide_lanes = pairs // per, per * LANES
    queries = pl.BlockSpec((rows, wide_lanes), lambda j: (0, j))
    shared = pl.BlockSpec((rows, LANES), lambda j: (0, 0))
    keys = pl.BlockSpec((count, wide_lanes), lambda j: (0, j))
    values = pl.BlockSpec((count, wide_lanes), lambda j: (0, steps + j))
    wide = jax.ShapeDtypeStruct((rows, width), F32)
    thin = jax.ShapeDtypeStruct((rows, LANES), F32)
    work = cost(8 * rows * count * width, 6 * count * width)
    mixed, peak, total = pl.pallas_call(
        partial(attend_first_kernel, per),
        grid=(steps,),
        in_specs=[queries, keys, values],
        out_specs=[queries, shared, shared],
        out_shape=[wide, thin, thin],
        compiler_params=params(24),
        cost_estimate=work,
        name="attend_first",
    )(own_queries, halves[0], halves[0])
    return pl.pallas_call(
        partial(attend_last_kernel, per),
        grid=(steps,),
        in_specs=[queries, keys, values, queries, shared, shared],
        out_specs=[queries, shared],
        out_shape=[wide, thin],
        compiler_params=params(24),
        cost_estimate=work,
        name="attend_last",
    )(own_queries, halves[1], halves[1], mixed, peak, total)


def middle_kernel(
    core, tokens, attended, log_total, cotangent, w_out, w_in, w_mlp, gain,
    layer_out, own_halves, other_halves, whole, grad_middle, grads, logs_deltas,
):

    rows, width = tokens.shape
    first = core[0] == 0

    def put_halves(at, block):
        half = block.shape[1] // 2
        left, right = block[:, :half], block[:, half:]
        own_halves[:, at : at + half] = jnp.where(first, left, right)
        other_halves[:, at : at + half] = jnp.where(first, right, left)

    mixed = attended[...]
    mixed_low = mixed.astype(BF16)
    put_halves(ATTENDED_AT, mixed_low)
    middle = tokens[...].astype(F32) + dot_nn(mixed_low, w_out[...])
    normed, rstd = normalize(middle)
    gain_row = gain[...].astype(F32)
    second = (normed * gain_row).astype(BF16)
    put_halves(NORMED_AT, second)
    gate = dot_nn(second, w_in[:, :FF])
    up = dot_nn(second, w_in[:, FF:])
    cdf = 0.5 * (1.0 + lax.erf(gate * (0.5**0.5)))
    activated = gate * cdf
    hidden = (activated * up).astype(BF16)
    put_halves(0, hidden)
    layer_out[...] = (middle + dot_nn(hidden, w_mlp[...])).astype(BF16)
    upstream = cotangent[...]
    grad_hidden = dot_nt(upstream, w_mlp[...]).astype(BF16).astype(F32)
    density = jnp.exp(-0.5 * gate * gate) * 0.3989422804014327
    grad_gate = (grad_hidden * up * (cdf + gate * density)).astype(BF16)
    grad_up = (grad_hidden * activated).astype(BF16)
    whole[:, :FF] = grad_gate
    whole[:, FF : 2 * FF] = grad_up
    grad_second = dot_nt(grad_gate, w_in[:, :FF]) + dot_nt(grad_up, w_in[:, FF:])
    grad_mid = upstream.astype(F32) + norm_back(grad_second, normed, rstd, gain_row)
    grad_middle[...] = grad_mid
    branch = grad_mid.astype(BF16)
    whole[:, 2 * FF :] = branch
    grad_attended = dot_nt(branch, w_out[...]).astype(BF16)
    grads[...] = grad_attended
    products = grad_attended.astype(F32) * mixed
    head = lax.broadcasted_iota(jnp.int32, (width, LANES), 0) // 64
    to_lane = (lane_of((width, LANES)) == head + HEADS).astype(F32)
    both = log_total[...] + lax.dot_general(
        products,
        to_lane,
        (((1,), (0,)), ((), ())),
        precision=lax.Precision.HIGHEST,
        preferred_element_type=F32,
    )
    logs_deltas[...] = both.T


def middle_part(core, tokens, attended, log_total, cotangent, w_out, w_in, w_mlp, gain):
    rows, width = tokens.shape
    wide, halves = (rows, width), (rows, HALVES_WIDTH)
    shapes = [
        (wide, BF16), (halves, BF16), (halves, BF16), ((rows, 2 * FF + width), BF16),
        (wide, F32), (wide, BF16), ((LANES, rows), F32),
    ]
    return pl.pallas_call(
        middle_kernel,
        in_specs=[SMEM_SPEC] + [WHOLE] * 8,
        out_shape=[jax.ShapeDtypeStruct(*shape) for shape in shapes],
        compiler_params=params(32),
        cost_estimate=cost(4 * rows * width * (2 * width + 6 * FF), 24 * MIB),
        name="middle",
    )(core, tokens, attended, log_total, cotangent, w_out, w_in, w_mlp, gain)


def rows_kernel(own, other, upstream, upstream_other, whole, whole_other, out_mlp, out_in):
    width = out_mlp.shape[1]
    half, half_ff = width // 2, FF // 2
    both = jnp.concatenate([own[...], other[...]], axis=0)
    right = jnp.concatenate([upstream[...], upstream_other[...]], axis=0)
    out_mlp[:half_ff, :] = dot_tn(both[:, :half_ff], right).astype(BF16)
    branch = jnp.concatenate([whole[:, 2 * FF :], whole_other[:, 2 * FF :]], axis=0)
    left = both[:, ATTENDED_AT : ATTENDED_AT + half]
    out_mlp[half_ff : half_ff + half, :] = dot_tn(left, branch).astype(BF16)
    turned = both[:, NORMED_AT : NORMED_AT + half].T
    for k in range(2 * FF // width):
        lanes = slice(k * width, (k + 1) * width)
        right = jnp.concatenate([whole[:, lanes], whole_other[:, lanes]], axis=0)
        out_in[k * half : (k + 1) * half, :] = dot_nn(turned, right).astype(BF16)
    for out, used in ((out_mlp, half_ff + half), (out_in, 2 * FF // width * half)):
        if used < out.shape[0]:
            out[used:, :] = jnp.zeros((out.shape[0] - used, width), BF16)


def padded(rows, pieces):
    unit = 8 * pieces
    return (rows + unit - 1) // unit * unit


def grad_rows(pieces, width, *arrays):
    sizes = padded((FF + width) // 2, pieces), padded(FF, pieces)
    return pl.pallas_call(
        rows_kernel,
        out_shape=[jax.ShapeDtypeStruct((size, width), BF16) for size in sizes],
        compiler_params=params(16),
        cost_estimate=cost(512 * 1728 * width, 12 * MIB),
        name="grad_rows",
    )(*arrays)


def unpack_kernel(places, gained, bit, own, other, *refs):
    half = own.shape[0]
    if gained:
        weights, gain = refs[:2]
    outs = refs[2:] if gained else refs

    def put(low, high):
        at = 0
        for out, blocks in places:
            ref = outs[out]
            made = ref.shape[0]
            for k in range(blocks):
                columns = slice(k * low.shape[1], (k + 1) * low.shape[1])
                cut = min(max(half - at, 0), made)
                if cut > 0:
                    ref[:cut, columns] = low[at : at + cut, :].astype(F32)
                if cut < made:
                    start = at + cut - half
                    ref[cut:, columns] = high[start : start + made - cut, :].astype(F32)
                at += made

    @pl.when(bit[0] == 0)
    def _():
        put(own, other)

    @pl.when(bit[0] != 0)
    def _():
        put(other, own)

    if gained:
        products = outs[0][...] * weights[...].astype(F32)
        sums = jnp.sum(products, axis=1, keepdims=True)
        row = jnp.broadcast_to(sums, (sums.shape[0], LANES)).T[:1]
        outs[-1][...] = (row / gain[...].astype(F32)).reshape(outs[-1].shape)


def unpack(chain, shapes, gained=()):
    own, other = chain.parts
    width = own.shape[1]
    places = [(k, shape[1] // width) for k, shape in enumerate(shapes)]
    if gained:
        shapes = shapes + [gained[1].shape[1:]]
    return pl.pallas_call(
        partial(unpack_kernel, places, bool(gained)),
        in_specs=[SMEM_SPEC] + [WHOLE] * (2 + len(gained)),
        out_shape=[jax.ShapeDtypeStruct(shape, F32) for shape in shapes],
        compiler_params=params(24),
        cost_estimate=cost(0, 12 * own.size),
        name="unpack",
    )(chain.bit.reshape(1), own, other, *gained)


def unrotated(block, cos, sin):
    return block * cos - halves_swapped(block) * sin


def row_pair(rows, at):
    index = lax.broadcasted_iota(jnp.int32, rows.shape, 0)
    picked = [
        jnp.sum(jnp.where(index == at + k, rows, 0.0), axis=0, keepdims=True) for k in (0, 1)
    ]
    return jnp.concatenate(picked, axis=1)


def attend_back_kernel(
    per, queries, keys_a, values_a, keys_b, values_b, grads, logs_deltas, cos, sin,
    out_queries, out_keys, out_values,
):
    rows, count = queries.shape[0], keys_a.shape[0]
    for pair, lanes in pairs_of(per):
        queries_two = two_heads(queries[:, lanes])
        grads_two = two_heads(grads[:, lanes])
        logs = row_pair(logs_deltas[...], 2 * pair)
        deltas = row_pair(logs_deltas[...], HEADS + 2 * pair)
        total = jnp.zeros((2 * rows, LANES), F32)
        for base, keys, values in ((0, keys_a, values_a), (count, keys_b, values_b)):
            for at in chunks_of(count):
                to = slice(base + at.start, base + at.stop)
                key_rows = keys[at, lanes]
                probs = jnp.exp(dot_nt(key_rows, queries_two) - logs)
                grad_probs = dot_nt(values[at, lanes], grads_two)
                grad_scores = (probs * (grad_probs - deltas)).astype(BF16)
                out_values[to, lanes] = dot_nn(probs.astype(BF16), grads_two).astype(BF16)
                grad_keys = dot_nn(grad_scores, queries_two)
                out_keys[to, lanes] = unrotated(grad_keys, cos[to, :], sin[to, :]).astype(BF16)
                total = total + dot_tn(grad_scores, key_rows)
        grad = one_pair(total) * 0.125
        out_queries[:, lanes] = unrotated(grad, cos[:rows, :], sin[:rows, :]).astype(BF16)


def attend_back(own_queries, halves, grads, logs_deltas, cos, sin):
    count = halves[0].shape[0]
    rows, width = own_queries.shape
    pairs = width // LANES
    per = pairs_per_step(count, pairs)
    steps, wide_lanes = pairs // per, per * LANES
    queries = pl.BlockSpec((rows, wide_lanes), lambda j: (0, j))
    shared = pl.BlockSpec((LANES, rows), lambda j: (0, 0))
    keys = pl.BlockSpec((count, wide_lanes), lambda j: (0, j))
    values = pl.BlockSpec((count, wide_lanes), lambda j: (0, steps + j))
    table = pl.BlockSpec((2 * count, LANES), lambda j: (0, 0))
    made = pl.BlockSpec((2 * count, wide_lanes), lambda j: (0, j))
    return pl.pallas_call(
        partial(attend_back_kernel, per),
        grid=(steps,),
        in_specs=[queries, keys, values, keys, values, queries, shared, table, table],
        out_specs=[queries, made, made],
        out_shape=[
            jax.ShapeDtypeStruct((rows, width), BF16),
            jax.ShapeDtypeStruct((2 * count, width), BF16),
            jax.ShapeDtypeStruct((2 * count, width), BF16),
        ],
        compiler_params=params(16 if count <= 1024 else 48),
        cost_estimate=cost(40 * rows * count * width, 20 * count * width),
        name="attend_back",
    )(
        own_queries, halves[0], halves[0], halves[1], halves[1],
        grads, logs_deltas, cos, sin,
    )


def late_rows_kernel(
    core, low_a, low_b, grad_q, grad_k, grad_v, out_own, out_other, total
):
    step, steps = pl.program_id(0), pl.num_programs(0)
    own_rows, width = grad_q.shape
    half = width // 2
    low = jnp.where(2 * step < steps, low_a[...], low_b[...])
    turned = low.T
    made_k, made_v = dot_nn(turned, grad_k[...]), dot_nn(turned, grad_v[...])

    @pl.when(step == 0)
    def _():
        total[:, :width] = dot_nn(turned[:, :own_rows], grad_q[...])
        total[:, width : 2 * width] = made_k
        total[:, 2 * width :] = made_v

    @pl.when(step > 0)
    def _():
        total[:, width : 2 * width] += made_k
        total[:, 2 * width :] += made_v

    @pl.when(step == steps - 1)
    def _():
        for out, side in ((out_own, core[0]), (out_other, 1 - core[0])):
            start = pl.multiple_of(side * half, half)
            for k in range(3):
                columns = slice(k * width, (k + 1) * width)
                out[k * half : (k + 1) * half, :] = total[pl.ds(start, half), columns].astype(BF16)
            if out.shape[0] > 3 * half:
                out[3 * half :, :] = jnp.zeros((out.shape[0] - 3 * half, width), BF16)


def late_rows_whole_kernel(
    core, low_a, low_b, grad_q, grad_k, grad_v, out_own, out_other, turned
):
    count, width = low_a.shape
    half, own_rows = width // 2, grad_q.shape[0]
    turned[:, :count] = low_a[...].T
    turned[:, count:] = low_b[...].T
    for out, side in ((out_own, core[0]), (out_other, 1 - core[0])):
        left = turned[pl.ds(pl.multiple_of(side * half, half), half), :]
        out[:half, :] = dot_nn(left[:, :own_rows], grad_q[...]).astype(BF16)
        out[half : 2 * half, :] = dot_nn(left, grad_k[...]).astype(BF16)
        out[2 * half : 3 * half, :] = dot_nn(left, grad_v[...]).astype(BF16)
        if out.shape[0] > 3 * half:
            out[3 * half :, :] = jnp.zeros((out.shape[0] - 3 * half, width), BF16)


def late_rows(core, pieces, lows, grad_q, grad_k, grad_v):
    count, width = lows[0].shape
    own_rows = grad_q.shape[0]
    step = min(count, 512)
    each = count // step
    total = padded(3 * width // 2, pieces)
    if each == 1:
        return pl.pallas_call(
            late_rows_whole_kernel,
            in_specs=[SMEM_SPEC] + [WHOLE] * 5,
            out_shape=[jax.ShapeDtypeStruct((total, width), BF16)] * 2,
            scratch_shapes=[pltpu.VMEM((width, 2 * count), BF16)],
            compiler_params=params(16),
            cost_estimate=cost(4 * count * width * width, 8 * count * width),
            name="late_rows",
        )(core, *lows, grad_q, grad_k, grad_v)
    grads = pl.BlockSpec((step, width), lambda i: (i, 0))
    fixed = pl.BlockSpec((own_rows, width), lambda i: (0, 0))
    made = pl.BlockSpec((total, width), lambda i: (0, 0))
    return pl.pallas_call(
        late_rows_kernel,
        grid=(2 * each,),
        in_specs=[
            SMEM_SPEC,
            pl.BlockSpec((step, width), lambda i: (jnp.minimum(i, each - 1), 0)),
            pl.BlockSpec((step, width), lambda i: (jnp.maximum(i - each, 0), 0)),
            fixed, grads, grads,
        ],
        out_specs=[made, made],
        out_shape=[jax.ShapeDtypeStruct((total, width), BF16)] * 2,
        scratch_shapes=[pltpu.VMEM((width, 3 * width), F32)],
        compiler_params=params(24),
        cost_estimate=cost(4 * count * width * width, 8 * count * width),
        name="late_rows",
    )(core, *lows, grad_q, grad_k, grad_v)


def first_rows_kernel(grad_q, grad_k, grad_v, weights, out):
    width = grad_q.shape[1]
    own_rows = grad_q.shape[0]
    made = dot_nt(grad_k[...], weights[:, width : 2 * width])
    made = made + dot_nt(grad_v[...], weights[:, 2 * width :])

    @pl.when(pl.program_id(0) == 0)
    def _():
        own = made[:own_rows] + dot_nt(grad_q[...], weights[:, :width])
        out[:own_rows, :] = own.astype(BF16)
        out[own_rows:, :] = made[own_rows:].astype(BF16)

    @pl.when(pl.program_id(0) > 0)
    def _():
        out[...] = made.astype(BF16)


def first_rows(grad_q, grad_k, grad_v, weights):
    rows, width = grad_k.shape
    own_rows = grad_q.shape[0]
    step = min(rows, 2 * own_rows)
    block = pl.BlockSpec((step, width), lambda i: (i, 0))
    return pl.pallas_call(
        first_rows_kernel,
        grid=(rows // step,),
        in_specs=[
            pl.BlockSpec((own_rows, width), lambda i: (0, 0)),
            block,
            block,
            pl.BlockSpec((width, 3 * width), lambda i: (0, 0)),
        ],
        out_specs=block,
        out_shape=jax.ShapeDtypeStruct((rows, width), BF16),
        compiler_params=params(16),
        cost_estimate=cost(4 * rows * width * width, 8 * rows * width),
        name="first_rows",
    )(grad_q, grad_k, grad_v, weights)


def last_kernel(tokens, grad_middle, part_a, part_b, gain, out):
    normed, rstd = normalize(tokens[...].astype(F32))
    grad_first = part_a[...].astype(F32) + part_b[...].astype(F32)
    back = norm_back(grad_first, normed, rstd, gain[...].astype(F32))
    out[...] = (grad_middle[...] + back).astype(BF16)


def last_part(tokens, grad_middle, parts, gain):
    return pl.pallas_call(
        last_kernel,
        out_shape=jax.ShapeDtypeStruct(tokens.shape, BF16),
        compiler_params=params(24),
        cost_estimate=cost(20 * tokens.size, 12 * tokens.size),
        name="last",
    )(tokens, grad_middle, *parts, gain)


def rotary_tables(positions, head_dim):
    half = head_dim // 2
    inverse = jnp.power(F32(THETA), -(jnp.arange(half, dtype=F32) * (2.0 / head_dim)))
    angles = positions[:, None] * inverse[None, :]
    cos, sin = jnp.cos(angles), jnp.sin(angles)
    return (
        jnp.concatenate([cos, cos, cos, cos], axis=1),
        jnp.concatenate([-sin, sin, -sin, sin], axis=1),
    )


def local(tokens, w_qkv, w_out, w_in, w_mlp, gain_attn, gain_mlp, cotangent):
    seqs_here, rows, width = tokens.shape
    half, half_ff = width // 2, FF // 2
    core = lax.axis_index("wsh")
    own = tokens.reshape(rows, width)
    upstream = cotangent.reshape(rows, width)
    pieces = lax.axis_size("seq") * lax.axis_size("ctx")

    gathered = gather_context(own)
    qkv_other = swap_cores(w_qkv)
    gains = jnp.stack([gain_attn, gain_mlp])
    gains_other = swap_cores(gains)
    gains_all = jnp.concatenate(
        [jnp.where(core == 0, gains, gains_other), jnp.where(core == 0, gains_other, gains)], axis=1
    )
    attn_gain, mlp_gain = gains_all[:1], gains_all[1:]
    full_out = both_halves(w_out)
    full_in = both_halves(w_in)
    full_mlp = both_halves(w_mlp)
    upstream_other = swap_cores(upstream)

    blocks = gathered_blocks()
    positions = (blocks[:, None] * rows + jnp.arange(rows, dtype=jnp.int32)[None, :]).reshape(-1)
    cos, sin = rotary_tables(positions.astype(F32), 64)
    count = gathered[0].shape[0]
    core_at = core.reshape(1)
    first_half, first_low, queries, full_qkv = project(
        core_at, gathered[0], w_qkv, qkv_other, attn_gain, cos[:count], sin[:count], rows
    )
    last_half, last_low = project(
        core_at, gathered[1], full_qkv, attn_gain, attn_gain, cos[count:], sin[count:], 0
    )
    halves = first_half, last_half
    attended, log_total = attend(queries, halves)
    (
        layer_out, own_halves, other_halves, whole, grad_middle, grads, logs_deltas,
    ) = middle_part(
        core_at, own, attended, log_total, upstream, full_out, full_in, full_mlp, mlp_gain
    )

    grad_q, grad_k, grad_v = attend_back(queries, halves, grads, logs_deltas, cos, sin)
    other_halves, whole_other = swap_cores(other_halves), swap_cores(whole)
    own_halves, grad_q = lax.optimization_barrier((own_halves, grad_q))
    mlp_rows, in_rows = grad_rows(
        pieces, width, own_halves, other_halves, upstream, upstream_other,
        whole, whole_other,
    )
    (grad_q,) = after([grad_q], mlp_rows, in_rows)
    late_own, late_other = late_rows(
        core_at, pieces, (first_low, last_low), grad_q, grad_k, grad_v
    )
    chains = [
        RowsSum([mlp_rows], MLP_ORDERS),
        RowsSum([in_rows], IN_ORDERS),
        RowsSum([late_own, swap_cores(late_other)], LATE_ORDERS),
    ]
    aways = lax.optimization_barrier(tuple(chain.first_away() for chain in chains))
    for chain, away in zip(chains, aways):
        chain.step(away)
    (grad_q,) = after([grad_q], *aways)
    chains.append(ContextSum(first_rows(grad_q, grad_k, grad_v, full_qkv)))
    while any(chain.left for chain in chains):
        for chain in chains:
            if chain.left:
                chain.step()
    mlp_grad, out_grad = unpack(chains[0], [(half_ff, width), (half, width)])
    in_grad, gain_mlp_grad = unpack(
        chains[1], [(half, 2 * FF)], (w_in, gain_mlp.reshape(1, half))
    )
    qkv_grad, gain_attn_grad = unpack(
        chains[2], [(half, 3 * width)], (w_qkv, gain_attn.reshape(1, half))
    )
    tokens_grad = last_part(own, grad_middle, chains[3].parts, attn_gain)
    return (
        layer_out.reshape(seqs_here, rows, width),
        tokens_grad.reshape(seqs_here, rows, width),
        qkv_grad,
        out_grad,
        in_grad,
        mlp_grad,
        gain_attn_grad,
        gain_mlp_grad,
    )


def solution(mesh):
    placed = (
        P(("seq", "wsh"), "ctx", None),
        P("wsh", None),
        P("wsh", None),
        P("wsh", None),
        P("wsh", None),
        P("wsh"),
        P("wsh"),
        P(("seq", "wsh"), "ctx", None),
    )
    return jax.shard_map(
        local,
        mesh=mesh,
        in_specs=placed,
        out_specs=(
            P(("seq", "wsh"), "ctx", None),
            P(("seq", "wsh"), "ctx", None),
            P("wsh", None),
            P("wsh", None),
            P("wsh", None),
            P("wsh", None),
            P("wsh"),
            P("wsh"),
        ),
        check_vma=False,
    )
```
